256 devices in a mesh: gx: 16 (over y, x), gy: 16 (over z, core).
Axes of the slice: x: 4, y: 4, z: 8, core: 2. Of those that a mesh axis runs over, the one named last changes fastest.
Arguments:
- right_side: float32 [128, 256, 192], P('gx', 'gy'), may hold values from -13 to 13
- phase: int32 [128, 256, 192], P('gx', 'gy'), may hold values 0 or 1
Outputs:
- pressure: float32 [128, 256, 192], P('gx', 'gy')
- residual: float32 [128, 256, 192], P('gx', 'gy')
The draws below stay inside these ranges and needn't reach their ends.
All inputs are finite; a program needn't handle non-finite values. No bound on the sum of `phase` on one device may be relied on, other than what follows from the above.
Results may differ from the reference program's by a relative error of at most 0.0003.
Values sent between devices are 32-bit elements; how exact they have to be, the bound alone decides.
A program may use at most 128 MiB of HBM per device.

```python
import jax
import jax.numpy as jnp
from jax import lax

NZ = 192
PRE = 2
BOTTOM = 8
NX = 128
NY = 256


def draw_right_side(key, part):
    key = jax.random.fold_in(key, 11)
    first_key, second_key = jax.random.split(key)
    factor = jnp.exp(jax.random.uniform(second_key, (NX, NY, 1), jnp.float32, -0.7, 0.7))
    rough = jax.random.truncated_normal(first_key, -6.0, 6.0, (NX, NY, NZ), jnp.float32)
    return rough * factor


def place_ends(values, own_key, least, high):
    dims = values.shape
    place = [jax.random.randint(jax.random.fold_in(own_key, axis), (), 0, dims[axis]) for axis in range(len(dims))]
    values = values.at[tuple(place)].set(least)
    longest = dims.index(max(dims))
    place[longest] = (place[longest] + 1) % dims[longest]
    return values.at[tuple(place)].set(high)


def setup_inputs(seed: int = 0) -> dict:
    key_of = jax.random.split(jax.random.key(seed), 3)
    right_side = draw_right_side(jax.random.fold_in(key_of[2], 71), 0)
    phase = place_ends((jax.random.randint(key_of[1], (NX, NY, NZ), 0, 5) < 2).astype(jnp.int32), jax.random.fold_in(key_of[1], 1), 0, 1)
    return {"right_side": right_side, "phase": phase}


def parity(shape):
    total = lax.broadcasted_iota(jnp.int32, shape, 0) + lax.broadcasted_iota(jnp.int32, shape, 1)
    return (total + lax.broadcasted_iota(jnp.int32, shape, 2)) % 2


def harmonic(first, second):
    return 2.0 * first * second / (first + second)


def weights_of(beta_grown):
    center = beta_grown[1:-1, 1:-1, 1:-1]
    return jnp.stack([
        harmonic(center, beta_grown[:-2, 1:-1, 1:-1]),
        harmonic(center, beta_grown[2:, 1:-1, 1:-1]),
        harmonic(center, beta_grown[1:-1, :-2, 1:-1]),
        harmonic(center, beta_grown[1:-1, 2:, 1:-1]),
        harmonic(center, beta_grown[1:-1, 1:-1, :-2]),
        harmonic(center, beta_grown[1:-1, 1:-1, 2:])], 0)


def diagonal_of(weights):
    return ((((weights[0] + weights[1]) + weights[2]) + weights[3]) + weights[4]) + weights[5]


def neighbor_sum(full, weights):
    total = weights[0] * full[:-2, 1:-1, 1:-1]
    total = total + weights[1] * full[2:, 1:-1, 1:-1]
    total = total + weights[2] * full[1:-1, :-2, 1:-1]
    total = total + weights[3] * full[1:-1, 2:, 1:-1]
    total = total + weights[4] * full[1:-1, 1:-1, :-2]
    return total + weights[5] * full[1:-1, 1:-1, 2:]


def blocks_of(field):
    sx, sy, sz = field.shape
    return field.reshape(sx // 2, 2, sy // 2, 2, sz // 2, 2)


def face_average(block, axis, side):
    parts = []
    for first in (0, 1):
        for second in (0, 1):
            for third in (0, 1):
                pick = (first, second, third)
                if pick[axis] == side:
                    parts.append(block[:, first, :, second, :, third])
    return ((parts[0] + parts[1]) + (parts[2] + parts[3])) * 0.25


def coarsen(weights):
    return jnp.stack([face_average(blocks_of(weights[c]), c // 2, c % 2) for c in range(6)], 0)


def restrict(field):
    block = blocks_of(field)
    parts = [block[:, a, :, b, :, c] for a in (0, 1) for b in (0, 1) for c in (0, 1)]
    return (((parts[0] + parts[1]) + (parts[2] + parts[3])) + ((parts[4] + parts[5]) + (parts[6] + parts[7]))) * 0.125


def prolong(field):
    return jnp.repeat(jnp.repeat(jnp.repeat(field, 2, 0), 2, 1), 2, 2)


def update(grown, source, weights, diagonal, scale, color):
    full = jnp.pad(grown, ((0, 0), (0, 0), (1, 1)))
    center = full[1:-1, 1:-1, 1:-1]
    fresh = (scale * source + neighbor_sum(full, weights)) / diagonal
    return jnp.where(parity(center.shape) == color, fresh, center)


def grow(field):
    return jnp.pad(field, ((1, 1), (1, 1), (0, 0)))


def relax(field, source, weights, diagonal, scale, count):
    for sweep in range(count):
        for color in (0, 1):
            field = update(grow(field), source, weights, diagonal, scale, color)
    return field


def residual_of(field, source, weights, diagonal, inverse):
    full = jnp.pad(grow(field), ((0, 0), (0, 0), (1, 1)))
    center = full[1:-1, 1:-1, 1:-1]
    return source - (diagonal * center - neighbor_sum(full, weights)) * inverse


def reference(right_side, phase):
    beta = jnp.where(jnp.pad(phase, 1) == 1, 0.1, 1.0).astype(jnp.float32)
    fine_w = weights_of(beta)
    mid_w = coarsen(fine_w)
    low_w = coarsen(mid_w)
    fine_d, mid_d, low_d = diagonal_of(fine_w), diagonal_of(mid_w), diagonal_of(low_w)
    fine_p = relax(jnp.zeros_like(right_side), right_side, fine_w, fine_d, 1.0, PRE)
    mid_b = restrict(residual_of(fine_p, right_side, fine_w, fine_d, 1.0))
    mid_p = relax(jnp.zeros_like(mid_b), mid_b, mid_w, mid_d, 4.0, PRE)
    low_b = restrict(residual_of(mid_p, mid_b, mid_w, mid_d, 0.25))
    low_p = relax(jnp.zeros_like(low_b), low_b, low_w, low_d, 16.0, BOTTOM)
    mid_p = relax(mid_p + prolong(low_p), mid_b, mid_w, mid_d, 4.0, PRE)
    pressure = relax(fine_p + prolong(mid_p), right_side, fine_w, fine_d, 1.0, PRE)
    residual = residual_of(pressure, right_side, fine_w, fine_d, 1.0)
    return pressure, residual
```

```python
import functools

import numpy as np

import jax
import jax.numpy as jnp
from jax import lax
from jax.experimental import pallas as pl
from jax.experimental.pallas import tpu as pltpu
from jax.sharding import PartitionSpec as P

F32 = jnp.float32
MESH = pl.DeviceIdType.MESH
LANES = 128
BOTTOM = 8

_L, _D = np.float32(1.0), np.float32(0.1)
W_LL = float(np.float32(2) * _L * _L / (_L + _L))
W_MX = float(np.float32(2) * _L * _D / (_L + _D))
W_DD = float(np.float32(2) * _D * _D / (_D + _D))

REACH = 5
NEAR = [(dx, dy) for dx in (-1, 0, 1) for dy in (-1, 0, 1) if (dx, dy) != (0, 0)]
FAR = [(dx, dy) for dx in (-2, 2) for dy in (-1, 0, 1)]
WIDE = NEAR + FAR
ALONG = [d * s for d in range(1, REACH + 1) for s in (1, -1)]


def rot(v, shift):
    return pltpu.roll(v, shift, 1)


def span(step, own, size, take):
    if step == 0:
        return own, size
    if isinstance(take, tuple):
        take = take[0] if step < 0 else take[1]
    if step > 0:
        return own + size - take, take
    return own, take


def kernel(
    nx, ny,
    rs_hbm, ph_hbm, p_hbm, r_hbm,
    rs_in, ph_in, out_p, out_r,
    ph, rs, wf, sf, df, rdf, pf, pb0, rf, tf, f1o,
    f1, b1, wm, sm, dm, rdm, pm, mb0, rm, em,
    lw, lb, gw, gb, ul, wl, sl, rdl, plow, e1, xo_s,
    in_sem, out_sem,
    s_ph, r_ph, s_rs, r_rs, s_f1, r_f1, s_b1, r_b1, s_pb, r_pb, s_mb, r_mb,
    s_lw, r_lw, s_lb, r_lb, s_gw, r_gw, s_gb, r_gb,
):
    a = lax.axis_index("gx")
    b = lax.axis_index("gy")

    def exists(dx, dy):
        ok = None
        for pos, d, n in ((a, dx, nx), (b, dy, ny)):
            if d:
                one = (pos + d >= 0) if d < 0 else (pos + d < n)
                ok = one if ok is None else jnp.logical_and(ok, one)
        return ok

    started = []

    def copy(src, dst, ssem, rsem, i, dev):
        return pltpu.make_async_remote_copy(
            src_ref=src, dst_ref=dst, send_sem=ssem.at[i], recv_sem=rsem.at[i], device_id=dev, device_id_type=MESH
        )

    def send(steps, refs, ssem, rsem, base=0):
        for i, (dx, dy) in enumerate(steps):
            src, dst = refs(dx, dy)
            cp = functools.partial(copy, src, dst, ssem, rsem, base + i, (a + dx, b + dy))
            ok = exists(dx, dy)

            @pl.when(ok)
            def _():
                cp().start()

            started.append((ok, cp))

    def arrive(steps, refs, ssem, rsem, base=0):
        for i, (dx, dy) in enumerate(steps):
            src, dst = refs(dx, dy)

            @pl.when(exists(-dx, -dy))
            def _():
                copy(src, dst, ssem, rsem, base + i, (a - dx, b - dy)).wait_recv()

    def ring_send(src, dst, ssem, rsem):
        for d in range(1, nx):
            cp = functools.partial(copy, src, dst((4 - d) % nx), ssem, rsem, d - 1, (lax.rem(a + d, nx), b))
            cp().start()
            started.append((None, cp))

    def ring_arrive(src, dst, ssem, rsem):
        for d in range(1, nx):
            copy(src, dst((4 - d) % nx), ssem, rsem, d - 1, (lax.rem(a + nx - d, nx), b)).wait_recv()

    def fine_refs(arr, lead, pairs, rows):
        def refs(dx, dy):
            x0, xn = span(dx, 3, 4, pairs)
            y0, yn = span(dy, 8, 16, rows)
            pre = (slice(None),) * lead
            return (
                arr.at[pre + (pl.ds(x0, xn), slice(None), pl.ds(y0, yn))],
                arr.at[pre + (pl.ds(x0 - 4 * dx, xn), slice(None), pl.ds(y0 - 16 * dy, yn))],
            )

        return refs

    def mid_refs(arr, lead, own, size, far, rows):
        def refs(dx, dy):
            x0, xn = span(dx, own, size, size if abs(dx) < 2 else far)
            y0, yn = span(dy, 16, 8, rows)
            pre = (slice(None),) * lead
            return (
                arr.at[pre + (pl.ds(x0, xn), pl.ds(y0, yn))],
                arr.at[pre + (pl.ds(x0 - size * dx, xn), pl.ds(y0 - 8 * dy, yn))],
            )

        return refs

    def low_refs(arr, lead):
        def refs(dx, dy):
            pre = (slice(None),) * lead
            return arr.at[pre + (pl.ds(20, 4),)], arr.at[pre + (pl.ds(20 - 4 * dy, 4),)]

        return refs

    ph_refs = fine_refs(ph, 1, 3, 5)
    rs_refs = fine_refs(rs, 1, 2, 4)
    pb_refs = fine_refs(pb0, 0, 3, 5)
    f1_refs = mid_refs(f1, 1, 8, 4, (3, 2), (7, 6))
    b1_refs = mid_refs(b1, 0, 8, 4, 2, 6)
    mb_refs = mid_refs(mb0, 0, 4, 2, 2, 7)
    lw_refs = low_refs(lw, 1)
    lb_refs = low_refs(lb, 0)
    gy_steps = [(0, d) for d in ALONG]

    in_rs = pltpu.make_async_copy(rs_hbm, rs_in, in_sem.at[0])
    in_ph = pltpu.make_async_copy(ph_hbm, ph_in, in_sem.at[1])
    in_ph.start()
    in_rs.start()

    bar = pltpu.get_barrier_semaphore()
    greet = list(WIDE) + [(0, d) for d in ALONG if abs(d) > 1]
    count = jnp.int32(0)
    for dx, dy in greet:
        ok = exists(dx, dy)

        @pl.when(ok)
        def _():
            pl.semaphore_signal(bar, inc=1, device_id=(a + dx, b + dy), device_id_type=MESH)

        count = count + ok.astype(jnp.int32)
    for d in range(1, nx):
        t = lax.rem(a + d, nx)
        far = jnp.logical_or(t > a + 2, t < a - 2)

        @pl.when(far)
        def _():
            pl.semaphore_signal(bar, inc=1, device_id=(t, b), device_id_type=MESH)

        count = count + far.astype(jnp.int32)

    def iota(rows, dim):
        return lax.broadcasted_iota(jnp.int32, (rows, LANES), dim)

    def h1_of(rows):
        return iota(rows, 1) >= 64

    def lane_ok(rows):
        return lax.rem(iota(rows, 1), 64) < 48

    def odd_fine(rows, start, t):
        return lax.rem(iota(rows, 0) + (start + t), 2) == 1

    def odd_mid(rows, start):
        return lax.rem(iota(rows, 0) + start + lax.div(iota(rows, 1), 64), 2) == 1

    def odd_low(rows, start):
        return lax.rem(iota(rows, 0) + start + iota(rows, 1), 2) == 1

    def zero(ref):
        ref[...] = jnp.zeros(ref.shape, F32)

    @pl.when(a == 0)
    def _():
        zero(ph.at[:, 0:3]); zero(rs.at[:, 0:3]); zero(pb0.at[0:3]); zero(f1.at[:, 0:8]); zero(b1.at[0:8]); zero(mb0.at[0:4])

    @pl.when(a == 1)
    def _():
        zero(f1.at[:, 0:4]); zero(b1.at[0:4]); zero(mb0.at[0:2])

    @pl.when(a == nx - 1)
    def _():
        zero(ph.at[:, 7:10]); zero(rs.at[:, 7:10]); zero(pb0.at[7:10])
        zero(f1.at[:, 12:21]); zero(b1.at[12:20]); zero(mb0.at[6:10])

    @pl.when(a == nx - 2)
    def _():
        zero(f1.at[:, 16:21]); zero(b1.at[16:20]); zero(mb0.at[8:10])

    @pl.when(b == 0)
    def _():
        zero(ph.at[:, :, :, 0:8]); zero(rs.at[:, :, :, 0:8]); zero(pb0.at[:, :, 0:8])
        zero(f1.at[:, :, 0:16]); zero(b1.at[:, 0:16]); zero(mb0.at[:, 0:16])

    @pl.when(b == ny - 1)
    def _():
        zero(ph.at[:, :, :, 24:32]); zero(rs.at[:, :, :, 24:32]); zero(pb0.at[:, :, 24:32])
        zero(f1.at[:, :, 24:40]); zero(b1.at[:, 24:40]); zero(mb0.at[:, 24:40])

    for d in ALONG:
        @pl.when(jnp.logical_not(exists(0, d)))
        def _():
            zero(lw.at[:, pl.ds(20 + 4 * d, 4)])
            zero(lb.at[pl.ds(20 + 4 * d, 4)])

    nz = rs_in.shape[2]
    kk = lax.broadcasted_iota(jnp.int32, (nz, 2 * LANES), 0)
    cc = lax.broadcasted_iota(jnp.int32, (nz, 2 * LANES), 1)
    q, hh, tt = lax.rem(cc, 64), lax.rem(lax.div(cc, 64), 2), lax.div(cc, 128)
    perm = jnp.where(jnp.logical_and(kk == 4 * q + 2 * hh + tt, q < 48), 1.0, 0.0).astype(F32)

    def split_into(values, dst):
        for t in (0, 1):
            odd = odd_fine(16, 0, t)
            for m in range(4):
                lo = values[32 * m:32 * m + 16, t * LANES:(t + 1) * LANES]
                hi = values[32 * m + 16:32 * m + 32, t * LANES:(t + 1) * LANES]
                dst[0, 3 + m, t, 8:24, :] = jnp.where(odd, hi, lo)
                dst[1, 3 + m, t, 8:24, :] = jnp.where(odd, lo, hi)

    in_ph.wait()
    labels = jnp.where(ph_in[...] == 1, 1.0, 0.0).astype(F32).reshape(128, nz)
    split_into(jnp.dot(labels, perm, preferred_element_type=F32), ph)
    in_rs.wait()
    block = rs_in[...].reshape(128, nz)
    split_into(jnp.dot(block, perm, precision=lax.Precision.HIGHEST, preferred_element_type=F32), rs)

    pl.semaphore_wait(bar, count)
    send(NEAR, ph_refs, s_ph, r_ph)
    send(NEAR, rs_refs, s_rs, r_rs)

    def pair_ok(first, m, total):
        g = first + m
        return jnp.logical_and(g >= 0, g < total)

    def inside(rows, start, total, ok):
        g = iota(rows, 0) + (start + jnp.where(ok, 0, -4096))
        return jnp.logical_and(jnp.logical_and(g >= 0, g < total), lane_ok(rows))

    def fine_sides(arr, c, m, t, r0, n, odd, h1):
        o = 1 - c
        xs = arr[o, m, t, pl.ds(r0, n), :]
        lo = arr[o, m - 1, t, pl.ds(r0, n), :]
        hi = arr[o, m + 1, t, pl.ds(r0, n), :]
        xo = jnp.where(odd, hi, lo) if c == 0 else jnp.where(odd, lo, hi)
        ym = arr[o, m, t, pl.ds(r0 - 1, n), :]
        yp = arr[o, m, t, pl.ds(r0 + 1, n), :]
        zs = arr[o, m, 1 - t, pl.ds(r0, n), :]
        if t == 0:
            zo = jnp.where(h1, rot(zs, 64), rot(zs, 65))
        else:
            zo = jnp.where(h1, rot(zs, 63), rot(zs, 64))
        return xs, xo, ym, yp, zs, zo

    R0, RN = 4, 24
    odd24 = [odd_fine(RN, R0, 0), odd_fine(RN, R0, 1)]
    h24 = h1_of(RN)

    arrive(NEAR, ph_refs, s_ph, r_ph)

    def fine_weights(m, carry):
        valid = inside(RN, 16 * b - 8 + R0, 16 * ny, pair_ok(4 * a - 3, m, 4 * nx))
        fx = fy = fz = None
        for t in (0, 1):
            both = []
            for c in (0, 1):
                dense = ph[c, m, t, pl.ds(R0, RN), :] > 0.5
                on = jnp.where(dense, W_DD, W_MX)
                off = jnp.where(dense, W_MX, W_LL)
                w = [jnp.where(s > 0.5, on, off) for s in fine_sides(ph, c, m, t, R0, RN, odd24[t], h24)]
                dg = ((((w[0] + w[1]) + w[2]) + w[3]) + w[4]) + w[5]
                rd = jnp.where(valid, 1.0 / dg, 0.0)
                for f in range(6):
                    wf[6 * c + f, m, t, pl.ds(R0, RN), :] = w[f] * rd
                df[c, m, t, pl.ds(R0, RN), :] = dg
                rdf[c, m, t, pl.ds(R0, RN), :] = rd
                both.append(w)
            x = jnp.where(odd24[t], both[1][1], both[0][1])
            y = both[0][2] + both[1][2]
            fx = x if fx is None else fx + x
            fy = y if fy is None else fy + y
            if t == 0:
                fz = both[0][5] + both[1][5]
        tf[0, m, 0:RN, :] = fx
        tf[1, m, 0:RN, :] = fy
        tf[2, m, 0:RN, :] = fz
        return carry

    lax.fori_loop(1, 9, fine_weights, 0)

    even, oddr = pl.ds(0, 16, stride=2), pl.ds(1, 16, stride=2)

    def mid_faces(i, carry):
        f1o[0, i, 0:16, :] = 0.25 * (tf[0, i + 3, even, :] + tf[0, i + 3, oddr, :])
        f1o[1, i, 0:16, :] = 0.25 * tf[1, i + 3, even, :]
        f1o[2, i, 0:16, :] = 0.25 * (tf[2, i + 3, even, :] + tf[2, i + 3, oddr, :])
        return carry

    lax.fori_loop(0, 5, mid_faces, 0)
    h8 = h1_of(8)
    for i in range(4):
        fx, fxn = f1o[0, i, 2:10, :], f1o[0, i + 1, 2:10, :]
        fy, fyn = f1o[1, i, 2:10, :], f1o[1, i, 3:11, :]
        fz = f1o[2, i, 2:10, :]
        fzn = jnp.where(h8, rot(fz, 63), rot(fz, 64))
        f1[0, 8 + i, 16:24, :] = fx
        f1[1, 8 + i, 16:24, :] = fy
        f1[2, 8 + i, 16:24, :] = fz
        f1[3, 8 + i, 16:24, :] = ((((fx + fxn) + fy) + fyn) + fz) + fzn
    send(NEAR, f1_refs, s_f1, r_f1)

    def zsum(v):
        return v + rot(v, 64)

    fx2 = [0.25 * zsum(f1o[0, 2 * i, pl.ds(2, 8, stride=2), :] + f1o[0, 2 * i, pl.ds(3, 8, stride=2), :]) for i in range(3)]
    fy2, fy2n, fz2, fz2n = [], [], [], []
    for i in range(2):
        fy2.append(0.25 * zsum(f1o[1, 2 * i, pl.ds(2, 8, stride=2), :] + f1o[1, 2 * i + 1, pl.ds(2, 8, stride=2), :]))
        fy2n.append(0.25 * zsum(f1o[1, 2 * i, pl.ds(4, 8, stride=2), :] + f1o[1, 2 * i + 1, pl.ds(4, 8, stride=2), :]))
        v = (f1o[2, 2 * i, pl.ds(2, 8, stride=2), :] + f1o[2, 2 * i, pl.ds(3, 8, stride=2), :]) + (
            f1o[2, 2 * i + 1, pl.ds(2, 8, stride=2), :] + f1o[2, 2 * i + 1, pl.ds(3, 8, stride=2), :]
        )
        v = 0.25 * jnp.where(h8, rot(v, 64), v)
        fz2.append(v)
        fz2n.append(rot(v, 127))
    odd8 = odd_low(8, 0)
    dg2 = [((((fx2[i] + fx2[i + 1]) + fy2[i]) + fy2n[i]) + fz2[i]) + fz2n[i] for i in range(2)]
    rd2 = [jnp.where(lane_ok(8), 1.0 / d, 0.0) for d in dg2]

    def red(v):
        return jnp.where(odd8, v[1], v[0])

    def black(v):
        return jnp.where(odd8, v[0], v[1])

    edge_low = jnp.where(a == 0, 0.0, 1.0)
    edge_high = jnp.where(a == nx - 1, 0.0, 1.0)
    xo2 = jnp.where(odd8, fx2[2] * edge_high, fx2[0] * edge_low)
    for f, (first, second) in enumerate(
        ((fx2[1], xo2), (red(fy2), red(fy2n)), (red(fz2), red(fz2n)), (red(rd2), black(rd2)))
    ):
        lw[f, 20:24, :] = jnp.where(h8, second, first)[0:4]
    send(gy_steps, lw_refs, s_lw, r_lw)

    def fine_nb(c, m, t, r0, n, odd, h1):
        v = fine_sides(pf, c, m, t, r0, n, odd, h1)
        total = wf[6 * c, m, t, pl.ds(r0, n), :] * v[0]
        for f in range(1, 6):
            total = total + wf[6 * c + f, m, t, pl.ds(r0, n), :] * v[f]
        return total

    def fine_half(c, m0, m1, r0, n):
        odd = [odd_fine(n, r0, 0), odd_fine(n, r0, 1)]
        h1 = h1_of(n)

        def body(m, carry):
            for t in (0, 1):
                nb = fine_nb(c, m, t, r0, n, odd[t], h1)
                pf[c, m, t, pl.ds(r0, n), :] = sf[c, m, t, pl.ds(r0, n), :] + nb
            return carry

        lax.fori_loop(m0, m1, body, 0)

    def fine_last(r0, n):
        odd = [odd_fine(n, r0, 0), odd_fine(n, r0, 1)]
        h1 = h1_of(n)

        def body(m, carry):
            for t in (0, 1):
                win = pl.ds(r0, n)
                nb = fine_nb(1, m, t, r0, n, odd[t], h1)
                fresh = sf[1, m, t, win, :] + nb
                pf[1, m, t, win, :] = fresh
                rf[1, m, t, win, :] = rs[1, m, t, win, :] - df[1, m, t, win, :] * (fresh - nb)
            return carry

        lax.fori_loop(2, 8, body, 0)

    def fine_red_residual():
        odd = [odd_fine(16, 8, 0), odd_fine(16, 8, 1)]
        h1 = h1_of(16)

        def body(m, carry):
            for t in (0, 1):
                win = pl.ds(8, 16)
                nb = fine_nb(0, m, t, 8, 16, odd[t], h1)
                rf[0, m, t, win, :] = rs[0, m, t, win, :] - df[0, m, t, win, :] * (pf[0, m, t, win, :] - nb)
            return carry

        lax.fori_loop(3, 7, body, 0)

    arrive(NEAR, rs_refs, s_rs, r_rs)

    def fine_source(m, carry):
        win = pl.ds(R0, RN)
        for t in (0, 1):
            first = rs[0, m, t, win, :] * rdf[0, m, t, win, :]
            sf[0, m, t, win, :] = first
            pf[0, m, t, win, :] = first
            sf[1, m, t, win, :] = rs[1, m, t, win, :] * rdf[1, m, t, win, :]
        return carry

    lax.fori_loop(1, 9, fine_source, 0)
    fine_half(1, 1, 9, 4, 24)
    fine_half(0, 2, 8, 6, 24)
    fine_last(7, 24)
    fine_red_residual()

    def restrict_fine(m, carry):
        v = (rf[0, m, 0, 8:24, :] + rf[1, m, 0, 8:24, :]) + (rf[0, m, 1, 8:24, :] + rf[1, m, 1, 8:24, :])
        rm[m, 0:16, :] = v
        b1[m + 5, 16:24, :] = 0.125 * (rm[m, pl.ds(0, 8, stride=2), :] + rm[m, pl.ds(1, 8, stride=2), :])
        return carry

    lax.fori_loop(3, 7, restrict_fine, 0)
    send(WIDE, b1_refs, s_b1, r_b1)

    def keep_black(m, carry):
        for t in (0, 1):
            pb0[m, t, 8:24, :] = pf[1, m, t, 8:24, :]
        return carry

    lax.fori_loop(3, 7, keep_black, 0)
    send(NEAR, pb_refs, s_pb, r_pb)
    send(FAR, f1_refs, s_f1, r_f1, len(NEAR))

    def mid_weights(m0, m1, r0, n, top):
        odd, h1 = odd_mid(n, r0), h1_of(n)
        win, nxt = pl.ds(r0, n), pl.ds(r0 + 1, n)

        def body(m, carry):
            valid = inside(n, 8 * b - 16 + r0, 8 * ny, pair_ok(2 * a - 4, m, 2 * nx))
            e0, e1_ = 2 * m, 2 * m + 1
            fx0, fx1, fx2_ = f1[0, e0, win, :], f1[0, e1_, win, :], f1[0, jnp.minimum(e1_ + 1, top), win, :]
            ym = [f1[1, e, win, :] for e in (e0, e1_)]
            yp = [f1[1, e, nxt, :] for e in (e0, e1_)]
            fz = [f1[2, e, win, :] for e in (e0, e1_)]
            zs = [jnp.where(h1, v, rot(v, 64)) for v in fz]
            zo = [jnp.where(h1, rot(v, 63), v) for v in fz]
            dg = [f1[3, e, win, :] for e in (e0, e1_)]
            for c in (0, 1):
                def pick(v):
                    return jnp.where(odd, v[1 - c], v[c])

                xo = jnp.where(odd, fx2_, fx0) if c == 0 else jnp.where(odd, fx0, fx2_)
                d = pick(dg)
                rd = jnp.where(valid, 1.0 / d, 0.0)
                for f, w in enumerate((fx1, xo, pick(ym), pick(yp), pick(zs), pick(zo))):
                    wm[6 * c + f, m, win, :] = w * rd
                dm[c, m, win, :] = d
                rdm[c, m, win, :] = rd
            return carry

        lax.fori_loop(m0, m1, body, 0)

    def mid_source(m0, m1, r0, n, start):
        odd = odd_mid(n, r0)
        win = pl.ds(r0, n)

        def body(m, carry):
            lo, hi = b1[2 * m, win, :], b1[2 * m + 1, win, :]
            first = 4.0 * jnp.where(odd, hi, lo) * rdm[0, m, win, :]
            sm[0, m, win, :] = first
            if start:
                pm[0, m, win, :] = first
            sm[1, m, win, :] = 4.0 * jnp.where(odd, lo, hi) * rdm[1, m, win, :]
            return carry

        lax.fori_loop(m0, m1, body, 0)

    def mid_nb(c, m, r0, n, odd, h1):
        o = 1 - c
        win = pl.ds(r0, n)
        xs, lo, hi = pm[o, m, win, :], pm[o, m - 1, win, :], pm[o, m + 1, win, :]
        xo = jnp.where(odd, hi, lo) if c == 0 else jnp.where(odd, lo, hi)
        zo = jnp.where(h1, rot(xs, 63), rot(xs, 65))
        total = wm[6 * c, m, win, :] * xs
        total = total + wm[6 * c + 1, m, win, :] * xo
        total = total + wm[6 * c + 2, m, win, :] * pm[o, m, pl.ds(r0 - 1, n), :]
        total = total + wm[6 * c + 3, m, win, :] * pm[o, m, pl.ds(r0 + 1, n), :]
        total = total + wm[6 * c + 4, m, win, :] * rot(xs, 64)
        return total + wm[6 * c + 5, m, win, :] * zo

    def mid_half(c, m0, m1, r0, n):
        odd, h1 = odd_mid(n, r0), h1_of(n)

        def body(m, carry):
            win = pl.ds(r0, n)
            pm[c, m, win, :] = sm[c, m, win, :] + mid_nb(c, m, r0, n, odd, h1)
            return carry

        lax.fori_loop(m0, m1, body, 0)

    arrive(NEAR, f1_refs, s_f1, r_f1)
    mid_weights(2, 8, 12, 16, 15)
    arrive(gy_steps, lw_refs, s_lw, r_lw)
    ring_send(lw.at[:, 0:44], lambda i: gw.at[i, :, 0:44], s_gw, r_gw)
    arrive(NEAR, b1_refs, s_b1, r_b1)
    mid_source(2, 8, 12, 16, True)
    mid_half(1, 2, 8, 13, 16)
    mid_half(0, 3, 7, 14, 16)
    mid_half(1, 3, 7, 15, 16)

    odd_own, h_own = odd_mid(8, 16), h1_of(8)
    own = pl.ds(16, 8)
    planes = []
    for m in (4, 5):
        lo, hi = b1[2 * m, own, :], b1[2 * m + 1, own, :]
        total = None
        for c in (0, 1):
            src = jnp.where(odd_own, hi, lo) if c == 0 else jnp.where(odd_own, lo, hi)
            nb = mid_nb(c, m, 16, 8, odd_own, h_own)
            res = src - dm[c, m, own, :] * (pm[c, m, own, :] - nb) * 0.25
            total = res if total is None else total + res
        rm[m, 0:8, :] = total
        rm[m, 8:16, :] = total
        planes.append(0.125 * zsum(rm[m, pl.ds(0, 8, stride=2), :] + rm[m, pl.ds(1, 8, stride=2), :]))
    lb[20:24, :] = jnp.where(h8, black(planes), red(planes))[0:4]
    send(gy_steps, lb_refs, s_lb, r_lb)
    for m in (4, 5):
        mb0[m, own, :] = pm[1, m, own, :]
    send(WIDE, mb_refs, s_mb, r_mb)

    arrive(FAR, f1_refs, s_f1, r_f1, len(NEAR))
    mid_weights(1, 9, 8, 24, 18)
    arrive(FAR, b1_refs, s_b1, r_b1, len(NEAR))
    mid_source(1, 9, 8, 24, False)

    arrive(gy_steps, lb_refs, s_lb, r_lb)
    ring_send(lb.at[0:44], lambda i: gb.at[i, 0:44], s_gb, r_gb)
    gw[4, :, 0:44] = lw[:, 0:44]
    gb[4, 0:44] = lb[0:44]

    LR = 48
    h48 = h1_of(LR)
    odd48 = odd_low(LR, 0)
    lwin = pl.ds(8, LR)

    def fold(lo, hi, half):
        if half == 0:
            return jnp.where(h48, rot(hi, 64), lo)
        return jnp.where(h48, hi, rot(lo, 64))

    ring_arrive(lw.at[:, 0:44], lambda i: gw.at[i, :, 0:44], s_gw, r_gw)

    def low_weights(s, carry):
        rdl[0, s, lwin, :] = fold(gw[s, 3], gw[s + 8, 3], 0)
        rdl[1, s, lwin, :] = fold(gw[s, 3], gw[s + 8, 3], 1)
        rd = rdl[0, s, lwin, :]
        for f in range(6):
            u = fold(gw[s, f // 2], gw[s + 8, f // 2], f % 2)
            ul[f, s + 1, lwin, :] = u
            wl[f, s, lwin, :] = u * rd
        return carry

    lax.fori_loop(0, 8, low_weights, 0)
    ul[1, 0, lwin, :] = rot(ul[1, 8, lwin, :], 64)
    ul[1, 9, lwin, :] = rot(ul[1, 1, lwin, :], 64)

    def low_black(s, carry):
        rd = rdl[1, s, lwin, :]
        wl[6, s, lwin, :] = ul[0, s + 1, lwin, :] * rd
        wl[7, s, lwin, :] = jnp.where(odd48, ul[1, s, lwin, :], ul[1, s + 2, lwin, :]) * rd
        wl[8, s, lwin, :] = ul[3, s + 1, pl.ds(7, LR), :] * rd
        wl[9, s, lwin, :] = ul[2, s + 1, pl.ds(9, LR), :] * rd
        wl[10, s, lwin, :] = rot(ul[5, s + 1, lwin, :], 1) * rd
        wl[11, s, lwin, :] = rot(ul[4, s + 1, lwin, :], 127) * rd
        return carry

    lax.fori_loop(0, 8, low_black, 0)

    ring_arrive(lb.at[0:44], lambda i: gb.at[i, 0:44], s_gb, r_gb)

    def low_source(s, carry):
        lo, hi = gb[s], gb[s + 8]
        first = 16.0 * fold(lo, hi, 0) * rdl[0, s, lwin, :]
        sl[0, s, lwin, :] = first
        plow[0, s + 1, lwin, :] = first
        sl[1, s, lwin, :] = 16.0 * fold(lo, hi, 1) * rdl[1, s, lwin, :]
        return carry

    lax.fori_loop(0, 8, low_source, 0)

    def low_ghosts(c, r0, n):
        win = pl.ds(r0, n)
        plow[c, 0, win, :] = rot(plow[c, 8, win, :], 64)
        plow[c, 9, win, :] = rot(plow[c, 1, win, :], 64)

    low_ghosts(0, 8, LR)
    for half in range(2, 2 * BOTTOM + 1):
        c = (half - 1) % 2
        reach = 4 + 2 * BOTTOM - half
        r0, n = 8 + 20 - reach, 8 * ((4 + 2 * reach + 7) // 8)
        odd = odd_low(n, r0)

        def low_body(s, carry, c=c, r0=r0, n=n, odd=odd):
            o = 1 - c
            win = pl.ds(r0, n)
            xs, lo, hi = plow[o, s + 1, win, :], plow[o, s, win, :], plow[o, s + 2, win, :]
            xo = jnp.where(odd, hi, lo) if c == 0 else jnp.where(odd, lo, hi)
            total = sl[c, s, win, :] + wl[6 * c, s, win, :] * xs
            total = total + wl[6 * c + 1, s, win, :] * xo
            total = total + wl[6 * c + 2, s, win, :] * plow[o, s + 1, pl.ds(r0 - 1, n), :]
            total = total + wl[6 * c + 3, s, win, :] * plow[o, s + 1, pl.ds(r0 + 1, n), :]
            total = total + wl[6 * c + 4, s, win, :] * rot(xs, 1)
            plow[c, s + 1, win, :] = total + wl[6 * c + 5, s, win, :] * rot(xs, 127)
            return carry

        lax.fori_loop(0, 8, low_body, 0)
        low_ghosts(c, r0, n)

    arrive(WIDE, mb_refs, s_mb, r_mb)
    odd16, h16 = odd_low(16, 0), h1_of(16)
    rows24 = pl.ds(8, 24)

    def mid_correct(s, carry):
        red_, black_ = plow[0, s + 3, pl.ds(24, 16), :], plow[1, s + 3, pl.ds(24, 16), :]
        for e in (0, 1):
            v = jnp.where(odd16, black_, red_) if e == 0 else jnp.where(odd16, red_, black_)
            v = jnp.where(h16, rot(v, 64), v)
            em[2 * s + e, pl.ds(0, 16, stride=2), :] = v
            em[2 * s + e, pl.ds(1, 16, stride=2), :] = v
            m = 2 * s + e
            add = em[m, 0:24, :] * jnp.where(pair_ok(2 * a - 4, m, 2 * nx), 1.0, 0.0)
            pm[1, m, rows24, :] = mb0[m, rows24, :] + add
        return carry

    lax.fori_loop(0, 5, mid_correct, 0)
    mid_half(0, 1, 9, 10, 24)
    mid_half(1, 1, 9, 11, 24)
    mid_half(0, 2, 8, 12, 16)
    mid_half(1, 2, 8, 13, 16)

    arrive(NEAR, pb_refs, s_pb, r_pb)
    odd_c = odd_mid(16, 13)

    for m in range(10):
        n, e = (m + 5) // 2, (m + 5) % 2
        red_, black_ = pm[0, n, pl.ds(13, 16), :], pm[1, n, pl.ds(13, 16), :]
        v = jnp.where(odd_c, black_, red_) if e == 0 else jnp.where(odd_c, red_, black_)
        e1[m, pl.ds(2, 16, stride=2), :] = v
        e1[m, pl.ds(3, 16, stride=2), :] = v
        for t in (0, 1):
            pf[1, m, t, pl.ds(3, 32), :] = pb0[m, t, pl.ds(3, 32), :] + e1[m, pl.ds(3, 32), :]

    fine_half(0, 1, 9, 4, 24)
    fine_half(1, 1, 9, 5, 24)
    fine_half(0, 2, 8, 6, 24)
    fine_last(7, 24)
    fine_red_residual()

    kk2 = lax.broadcasted_iota(jnp.int32, (2 * LANES, nz), 1)
    cc2 = lax.broadcasted_iota(jnp.int32, (2 * LANES, nz), 0)
    q2, hh2, tt2 = lax.rem(cc2, 64), lax.rem(lax.div(cc2, 64), 2), lax.div(cc2, 128)
    back = jnp.where(jnp.logical_and(kk2 == 4 * q2 + 2 * hh2 + tt2, q2 < 48), 1.0, 0.0).astype(F32)

    def join_from(src, out):
        for t in (0, 1):
            odd = odd_fine(16, 8, t)
            for m in range(4):
                r, k = src[0, 3 + m, t, 8:24, :], src[1, 3 + m, t, 8:24, :]
                xo_s[32 * m:32 * m + 16, t * LANES:(t + 1) * LANES] = jnp.where(odd, k, r)
                xo_s[32 * m + 16:32 * m + 32, t * LANES:(t + 1) * LANES] = jnp.where(odd, r, k)
        v = jnp.dot(xo_s[...], back, precision=lax.Precision.HIGHEST, preferred_element_type=F32)
        out[...] = v.reshape(out.shape)

    join_from(pf, out_p)
    put_p = pltpu.make_async_copy(out_p, p_hbm, out_sem.at[0])
    put_p.start()
    join_from(rf, out_r)
    put_r = pltpu.make_async_copy(out_r, r_hbm, out_sem.at[1])
    put_r.start()
    for ok, cp in started:
        if ok is None:
            cp().wait_send()
        else:
            @pl.when(ok)
            def _():
                cp().wait_send()
    put_p.wait()
    put_r.wait()


def solution(mesh):
    nx, ny = mesh.shape["gx"], mesh.shape["gy"]

    def local(right_side, phase):
        shape = right_side.shape
        v = lambda *dims: pltpu.VMEM(dims, F32)
        sems = []
        for n in (len(NEAR), len(NEAR), len(WIDE), len(WIDE), len(NEAR), len(WIDE), len(ALONG), len(ALONG), nx - 1, nx - 1):
            sems += [pltpu.SemaphoreType.DMA((n,)), pltpu.SemaphoreType.DMA((n,))]
        fine = (10, 2, 40, LANES)
        return pl.pallas_call(
            functools.partial(kernel, nx, ny),
            out_shape=[jax.ShapeDtypeStruct(shape, F32)] * 2,
            in_specs=[pl.BlockSpec(memory_space=pl.ANY)] * 2,
            out_specs=[pl.BlockSpec(memory_space=pl.ANY)] * 2,
            scratch_shapes=[
                v(*shape), pltpu.VMEM(shape, jnp.int32), v(*shape), v(*shape),
                v(2, *fine), v(2, *fine), v(12, *fine), v(2, *fine), v(2, *fine), v(2, *fine), v(2, *fine), v(*fine),
                v(2, *fine), v(3, 10, 32, LANES), v(3, 5, 24, LANES),
                v(4, 21, 40, LANES), v(20, 40, LANES), v(12, 10, 40, LANES), v(2, 10, 40, LANES), v(2, 10, 40, LANES),
                v(2, 10, 40, LANES), v(2, 10, 40, LANES), v(10, 40, LANES), v(10, 16, LANES), v(10, 32, LANES),
                v(4, 48, LANES), v(48, LANES), v(16, 4, 48, LANES), v(16, 48, LANES), v(6, 10, 64, LANES),
                v(12, 8, 64, LANES), v(2, 8, 64, LANES), v(2, 8, 64, LANES), v(2, 10, 64, LANES), v(10, 40, LANES),
                v(128, 2 * LANES),
                pltpu.SemaphoreType.DMA((2,)), pltpu.SemaphoreType.DMA((2,)),
            ] + sems,
            compiler_params=pltpu.CompilerParams(
                collective_id=0, has_side_effects=True, vmem_limit_bytes=48 * 2**20
            ),
        )(right_side, phase)

    spec = P("gx", "gy", None)
    return jax.shard_map(local, mesh=mesh, in_specs=(spec, spec), out_specs=(spec, spec), check_vma=False)
```

```python
import functools

import numpy as np

import jax
import jax.numpy as jnp
from jax import lax
from jax.experimental import pallas as pl
from jax.experimental.pallas import tpu as pltpu
from jax.sharding import PartitionSpec as P

F32 = jnp.float32
MESH = pl.DeviceIdType.MESH
LANES = 128
BOTTOM = 8

_L, _D = np.float32(1.0), np.float32(0.1)
W_LL = float(np.float32(2) * _L * _L / (_L + _L))
W_MX = float(np.float32(2) * _L * _D / (_L + _D))
W_DD = float(np.float32(2) * _D * _D / (_D + _D))

REACH = 5
NEAR = [(dx, dy) for dx in (-1, 0, 1) for dy in (-1, 0, 1) if (dx, dy) != (0, 0)]
FAR = [(dx, dy) for dx in (-2, 2) for dy in (-1, 0, 1)]
WIDE = NEAR + FAR
ALONG = [d * s for d in range(1, REACH + 1) for s in (1, -1)]


def rot(v, shift):
    return pltpu.roll(v, shift, 1)


def span(step, own, size, take):
    if step == 0:
        return own, size
    if isinstance(take, tuple):
        take = take[0] if step < 0 else take[1]
    if step > 0:
        return own + size - take, take
    return own, take


def kernel(
    nx, ny,
    rs_hbm, ph_hbm, p_hbm, r_hbm,
    rs_in, ph_in, out_p, out_r,
    ph, rs, wf, sf, df, rdf, pf, pb0, rf, tf, f1o,
    f1, b1, wm, sm, dm, rdm, pm, mb0, rm, em,
    lw, lb, gw, gb, ul, wl, sl, rdl, plow, e1, xo_s,
    in_sem, out_sem,
    s_ph, r_ph, s_rs, r_rs, s_f1, r_f1, s_b1, r_b1, s_pb, r_pb, s_mb, r_mb,
    s_lw, r_lw, s_lb, r_lb, s_gw, r_gw, s_gb, r_gb, s_re, r_re,
):
    a = lax.axis_index("gx")
    b = lax.axis_index("gy")

    def exists(dx, dy):
        ok = None
        for pos, d, n in ((a, dx, nx), (b, dy, ny)):
            if d:
                one = (pos + d >= 0) if d < 0 else (pos + d < n)
                ok = one if ok is None else jnp.logical_and(ok, one)
        return ok

    started = []

    def copy(src, dst, ssem, rsem, i, dev):
        return pltpu.make_async_remote_copy(
            src_ref=src, dst_ref=dst, send_sem=ssem.at[i], recv_sem=rsem.at[i], device_id=dev, device_id_type=MESH
        )

    def send(steps, refs, ssem, rsem, base=0):
        for i, (dx, dy) in enumerate(steps):
            src, dst = refs(dx, dy)
            cp = functools.partial(copy, src, dst, ssem, rsem, base + i, (a + dx, b + dy))
            ok = exists(dx, dy)

            @pl.when(ok)
            def _():
                cp().start()

            started.append((ok, cp))

    def arrive(steps, refs, ssem, rsem, base=0):
        for i, (dx, dy) in enumerate(steps):
            src, dst = refs(dx, dy)

            @pl.when(exists(-dx, -dy))
            def _():
                copy(src, dst, ssem, rsem, base + i, (a - dx, b - dy)).wait_recv()

    def ring_send(src, dst, ssem, rsem):
        for d in range(1, nx):
            cp = functools.partial(copy, src, dst((4 - d) % nx), ssem, rsem, d - 1, (lax.rem(a + d, nx), b))
            cp().start()
            started.append((None, cp))

    def relay_refs(i):
        core = lax.rem(b, 2)
        return gw.at[i, :, pl.ds(4 + 16 * core, 20)], gw.at[i, :, pl.ds(24 * core, 20)], (a, b + 1 - 2 * core)

    def relay(i):
        src, dst, dev = relay_refs(i)
        cp = functools.partial(copy, src, dst, s_re, r_re, i, dev)
        cp().start()
        started.append((None, cp))

    def relay_arrive(i):
        src, dst, dev = relay_refs(i)
        core = lax.rem(b, 2)
        copy(src, gw.at[i, :, pl.ds(24 - 24 * core, 20)], s_re, r_re, i, dev).wait_recv()

    def ring_arrive(src, dst, ssem, rsem):
        for d in range(1, nx):
            copy(src, dst((4 - d) % nx), ssem, rsem, d - 1, (lax.rem(a + nx - d, nx), b)).wait_recv()

    def fine_refs(arr, lead, pairs, rows):
        def refs(dx, dy):
            x0, xn = span(dx, 3, 4, pairs)
            y0, yn = span(dy, 8, 16, rows)
            pre = (slice(None),) * lead
            return (
                arr.at[pre + (pl.ds(x0, xn), slice(None), pl.ds(y0, yn))],
                arr.at[pre + (pl.ds(x0 - 4 * dx, xn), slice(None), pl.ds(y0 - 16 * dy, yn))],
            )

        return refs

    def mid_refs(arr, lead, own, size, far, rows):
        def refs(dx, dy):
            x0, xn = span(dx, own, size, size if abs(dx) < 2 else far)
            y0, yn = span(dy, 16, 8, rows)
            pre = (slice(None),) * lead
            return (
                arr.at[pre + (pl.ds(x0, xn), pl.ds(y0, yn))],
                arr.at[pre + (pl.ds(x0 - size * dx, xn), pl.ds(y0 - 8 * dy, yn))],
            )

        return refs

    def low_refs(arr, lead):
        def refs(dx, dy):
            pre = (slice(None),) * lead
            return arr.at[pre + (pl.ds(20, 4),)], arr.at[pre + (pl.ds(20 - 4 * dy, 4),)]

        return refs

    ph_refs = fine_refs(ph, 1, 3, 5)
    rs_refs = fine_refs(rs, 1, 2, 4)
    pb_refs = fine_refs(pb0, 0, 3, 5)
    f1_refs = mid_refs(f1, 1, 8, 4, (3, 2), (7, 6))
    b1_refs = mid_refs(b1, 0, 8, 4, 2, 6)
    mb_refs = mid_refs(mb0, 0, 4, 2, 2, 7)
    lw_refs = low_refs(lw, 1)
    lb_refs = low_refs(lb, 0)
    gy_steps = [(0, d) for d in ALONG]

    in_rs = pltpu.make_async_copy(rs_hbm, rs_in, in_sem.at[0])
    in_ph = pltpu.make_async_copy(ph_hbm, ph_in, in_sem.at[1])
    in_ph.start()
    in_rs.start()

    bar = pltpu.get_barrier_semaphore()
    greet = list(WIDE) + [(0, d) for d in ALONG if abs(d) > 1]
    count = jnp.int32(0)
    for dx, dy in greet:
        ok = exists(dx, dy)

        @pl.when(ok)
        def _():
            pl.semaphore_signal(bar, inc=1, device_id=(a + dx, b + dy), device_id_type=MESH)

        count = count + ok.astype(jnp.int32)
    for d in range(1, nx):
        t = lax.rem(a + d, nx)
        far = jnp.logical_or(t > a + 2, t < a - 2)

        @pl.when(far)
        def _():
            pl.semaphore_signal(bar, inc=1, device_id=(t, b), device_id_type=MESH)

        count = count + far.astype(jnp.int32)

    def iota(rows, dim):
        return lax.broadcasted_iota(jnp.int32, (rows, LANES), dim)

    def h1_of(rows):
        return iota(rows, 1) >= 64

    def lane_ok(rows):
        return lax.rem(iota(rows, 1), 64) < 48

    def odd_fine(rows, start, t):
        return lax.rem(iota(rows, 0) + (start + t), 2) == 1

    def odd_mid(rows, start):
        return lax.rem(iota(rows, 0) + start + lax.div(iota(rows, 1), 64), 2) == 1

    def odd_low(rows, start):
        return lax.rem(iota(rows, 0) + start + iota(rows, 1), 2) == 1

    def zero(ref):
        ref[...] = jnp.zeros(ref.shape, F32)

    @pl.when(a == 0)
    def _():
        zero(ph.at[:, 0:3]); zero(rs.at[:, 0:3]); zero(pb0.at[0:3]); zero(f1.at[:, 0:8]); zero(b1.at[0:8]); zero(mb0.at[0:4])

    @pl.when(a == 1)
    def _():
        zero(f1.at[:, 0:4]); zero(b1.at[0:4]); zero(mb0.at[0:2])

    @pl.when(a == nx - 1)
    def _():
        zero(ph.at[:, 7:10]); zero(rs.at[:, 7:10]); zero(pb0.at[7:10])
        zero(f1.at[:, 12:21]); zero(b1.at[12:20]); zero(mb0.at[6:10])

    @pl.when(a == nx - 2)
    def _():
        zero(f1.at[:, 16:21]); zero(b1.at[16:20]); zero(mb0.at[8:10])

    @pl.when(b == 0)
    def _():
        zero(ph.at[:, :, :, 0:8]); zero(rs.at[:, :, :, 0:8]); zero(pb0.at[:, :, 0:8])
        zero(f1.at[:, :, 0:16]); zero(b1.at[:, 0:16]); zero(mb0.at[:, 0:16])

    @pl.when(b == ny - 1)
    def _():
        zero(ph.at[:, :, :, 24:32]); zero(rs.at[:, :, :, 24:32]); zero(pb0.at[:, :, 24:32])
        zero(f1.at[:, :, 24:40]); zero(b1.at[:, 24:40]); zero(mb0.at[:, 24:40])

    for d in ALONG:
        @pl.when(jnp.logical_not(exists(0, d)))
        def _():
            zero(lw.at[:, pl.ds(20 + 4 * d, 4)])
            zero(lb.at[pl.ds(20 + 4 * d, 4)])

    nz = rs_in.shape[2]
    kk = lax.broadcasted_iota(jnp.int32, (nz, 2 * LANES), 0)
    cc = lax.broadcasted_iota(jnp.int32, (nz, 2 * LANES), 1)
    q, hh, tt = lax.rem(cc, 64), lax.rem(lax.div(cc, 64), 2), lax.div(cc, 128)
    perm = jnp.where(jnp.logical_and(kk == 4 * q + 2 * hh + tt, q < 48), 1.0, 0.0).astype(F32)

    def split_into(values, dst):
        for t in (0, 1):
            odd = odd_fine(16, 0, t)
            for m in range(4):
                lo = values[32 * m:32 * m + 16, t * LANES:(t + 1) * LANES]
                hi = values[32 * m + 16:32 * m + 32, t * LANES:(t + 1) * LANES]
                dst[0, 3 + m, t, 8:24, :] = jnp.where(odd, hi, lo)
                dst[1, 3 + m, t, 8:24, :] = jnp.where(odd, lo, hi)

    in_ph.wait()
    labels = jnp.where(ph_in[...] == 1, 1.0, 0.0).astype(F32).reshape(128, nz)
    split_into(jnp.dot(labels, perm, preferred_element_type=F32), ph)
    in_rs.wait()
    block = rs_in[...].reshape(128, nz)
    split_into(jnp.dot(block, perm, precision=lax.Precision.HIGHEST, preferred_element_type=F32), rs)

    pl.semaphore_wait(bar, count)
    send(NEAR, ph_refs, s_ph, r_ph)
    send(NEAR, rs_refs, s_rs, r_rs)

    def pair_ok(first, m, total):
        g = first + m
        return jnp.logical_and(g >= 0, g < total)

    def inside(rows, start, total, ok):
        g = iota(rows, 0) + (start + jnp.where(ok, 0, -4096))
        return jnp.logical_and(jnp.logical_and(g >= 0, g < total), lane_ok(rows))

    def fine_sides(arr, c, m, t, r0, n, odd, h1):
        o = 1 - c
        xs = arr[o, m, t, pl.ds(r0, n), :]
        lo = arr[o, m - 1, t, pl.ds(r0, n), :]
        hi = arr[o, m + 1, t, pl.ds(r0, n), :]
        xo = jnp.where(odd, hi, lo) if c == 0 else jnp.where(odd, lo, hi)
        ym = arr[o, m, t, pl.ds(r0 - 1, n), :]
        yp = arr[o, m, t, pl.ds(r0 + 1, n), :]
        zs = arr[o, m, 1 - t, pl.ds(r0, n), :]
        if t == 0:
            zo = jnp.where(h1, rot(zs, 64), rot(zs, 65))
        else:
            zo = jnp.where(h1, rot(zs, 63), rot(zs, 64))
        return xs, xo, ym, yp, zs, zo

    R0, RN = 4, 24
    odd24 = [odd_fine(RN, R0, 0), odd_fine(RN, R0, 1)]
    h24 = h1_of(RN)

    arrive(NEAR, ph_refs, s_ph, r_ph)

    def fine_weights(m, carry):
        valid = inside(RN, 16 * b - 8 + R0, 16 * ny, pair_ok(4 * a - 3, m, 4 * nx))
        fx = fy = fz = None
        for t in (0, 1):
            both = []
            for c in (0, 1):
                dense = ph[c, m, t, pl.ds(R0, RN), :] > 0.5
                on = jnp.where(dense, W_DD, W_MX)
                off = jnp.where(dense, W_MX, W_LL)
                w = [jnp.where(s > 0.5, on, off) for s in fine_sides(ph, c, m, t, R0, RN, odd24[t], h24)]
                dg = ((((w[0] + w[1]) + w[2]) + w[3]) + w[4]) + w[5]
                rd = jnp.where(valid, 1.0 / dg, 0.0)
                for f in range(6):
                    wf[6 * c + f, m, t, pl.ds(R0, RN), :] = w[f] * rd
                df[c, m, t, pl.ds(R0, RN), :] = dg
                rdf[c, m, t, pl.ds(R0, RN), :] = rd
                both.append(w)
            x = jnp.where(odd24[t], both[1][1], both[0][1])
            y = both[0][2] + both[1][2]
            fx = x if fx is None else fx + x
            fy = y if fy is None else fy + y
            if t == 0:
                fz = both[0][5] + both[1][5]
        tf[0, m, 0:RN, :] = fx
        tf[1, m, 0:RN, :] = fy
        tf[2, m, 0:RN, :] = fz
        return carry

    lax.fori_loop(1, 9, fine_weights, 0)

    even, oddr = pl.ds(0, 16, stride=2), pl.ds(1, 16, stride=2)

    def mid_faces(i, carry):
        f1o[0, i, 0:16, :] = 0.25 * (tf[0, i + 3, even, :] + tf[0, i + 3, oddr, :])
        f1o[1, i, 0:16, :] = 0.25 * tf[1, i + 3, even, :]
        f1o[2, i, 0:16, :] = 0.25 * (tf[2, i + 3, even, :] + tf[2, i + 3, oddr, :])
        return carry

    lax.fori_loop(0, 5, mid_faces, 0, unroll=True)
    h8 = h1_of(8)
    for i in range(4):
        fx, fxn = f1o[0, i, 2:10, :], f1o[0, i + 1, 2:10, :]
        fy, fyn = f1o[1, i, 2:10, :], f1o[1, i, 3:11, :]
        fz = f1o[2, i, 2:10, :]
        fzn = jnp.where(h8, rot(fz, 63), rot(fz, 64))
        f1[0, 8 + i, 16:24, :] = fx
        f1[1, 8 + i, 16:24, :] = fy
        f1[2, 8 + i, 16:24, :] = fz
        f1[3, 8 + i, 16:24, :] = ((((fx + fxn) + fy) + fyn) + fz) + fzn
    send(NEAR, f1_refs, s_f1, r_f1)

    def zsum(v):
        return v + rot(v, 64)

    fx2 = [0.25 * zsum(f1o[0, 2 * i, pl.ds(2, 8, stride=2), :] + f1o[0, 2 * i, pl.ds(3, 8, stride=2), :]) for i in range(3)]
    fy2, fy2n, fz2, fz2n = [], [], [], []
    for i in range(2):
        fy2.append(0.25 * zsum(f1o[1, 2 * i, pl.ds(2, 8, stride=2), :] + f1o[1, 2 * i + 1, pl.ds(2, 8, stride=2), :]))
        fy2n.append(0.25 * zsum(f1o[1, 2 * i, pl.ds(4, 8, stride=2), :] + f1o[1, 2 * i + 1, pl.ds(4, 8, stride=2), :]))
        v = (f1o[2, 2 * i, pl.ds(2, 8, stride=2), :] + f1o[2, 2 * i, pl.ds(3, 8, stride=2), :]) + (
            f1o[2, 2 * i + 1, pl.ds(2, 8, stride=2), :] + f1o[2, 2 * i + 1, pl.ds(3, 8, stride=2), :]
        )
        v = 0.25 * jnp.where(h8, rot(v, 64), v)
        fz2.append(v)
        fz2n.append(rot(v, 127))
    odd8 = odd_low(8, 0)
    dg2 = [((((fx2[i] + fx2[i + 1]) + fy2[i]) + fy2n[i]) + fz2[i]) + fz2n[i] for i in range(2)]
    rd2 = [jnp.where(lane_ok(8), 1.0 / d, 0.0) for d in dg2]

    def red(v):
        return jnp.where(odd8, v[1], v[0])

    def black(v):
        return jnp.where(odd8, v[0], v[1])

    edge_low = jnp.where(a == 0, 0.0, 1.0)
    edge_high = jnp.where(a == nx - 1, 0.0, 1.0)
    xo2 = jnp.where(odd8, fx2[2] * edge_high, fx2[0] * edge_low)
    inv = jnp.where(h8, black(rd2), red(rd2))
    for f, (first, second) in enumerate(((fx2[1], xo2), (red(fy2), red(fy2n)), (red(fz2), red(fz2n)))):
        v = jnp.where(lane_ok(8), jnp.where(h8, second, first), rot(inv, 48 - 16 * f))
        lw[f, 20:24, :] = v[0:4]
    send(gy_steps, lw_refs, s_lw, r_lw)

    def fine_nb(c, m, t, r0, n, odd, h1):
        v = fine_sides(pf, c, m, t, r0, n, odd, h1)
        total = wf[6 * c, m, t, pl.ds(r0, n), :] * v[0]
        for f in range(1, 6):
            total = total + wf[6 * c + f, m, t, pl.ds(r0, n), :] * v[f]
        return total

    def fine_half(c, m0, m1, r0, n):
        odd = [odd_fine(n, r0, 0), odd_fine(n, r0, 1)]
        h1 = h1_of(n)

        def body(m, carry):
            for t in (0, 1):
                nb = fine_nb(c, m, t, r0, n, odd[t], h1)
                pf[c, m, t, pl.ds(r0, n), :] = sf[c, m, t, pl.ds(r0, n), :] + nb
            return carry

        lax.fori_loop(m0, m1, body, 0, unroll=True)

    def fine_last(r0, n):
        odd = [odd_fine(n, r0, 0), odd_fine(n, r0, 1)]
        h1 = h1_of(n)

        def body(m, carry):
            for t in (0, 1):
                win = pl.ds(r0, n)
                nb = fine_nb(1, m, t, r0, n, odd[t], h1)
                fresh = sf[1, m, t, win, :] + nb
                pf[1, m, t, win, :] = fresh
                rf[1, m, t, win, :] = rs[1, m, t, win, :] - df[1, m, t, win, :] * (fresh - nb)
            return carry

        lax.fori_loop(2, 8, body, 0, unroll=True)

    def fine_red_residual():
        odd = [odd_fine(16, 8, 0), odd_fine(16, 8, 1)]
        h1 = h1_of(16)

        def body(m, carry):
            for t in (0, 1):
                win = pl.ds(8, 16)
                nb = fine_nb(0, m, t, 8, 16, odd[t], h1)
                rf[0, m, t, win, :] = rs[0, m, t, win, :] - df[0, m, t, win, :] * (pf[0, m, t, win, :] - nb)
            return carry

        lax.fori_loop(3, 7, body, 0, unroll=True)

    arrive(NEAR, rs_refs, s_rs, r_rs)

    def fine_source(m, carry):
        win = pl.ds(R0, RN)
        for t in (0, 1):
            first = rs[0, m, t, win, :] * rdf[0, m, t, win, :]
            sf[0, m, t, win, :] = first
            pf[0, m, t, win, :] = first
            sf[1, m, t, win, :] = rs[1, m, t, win, :] * rdf[1, m, t, win, :]
        return carry

    lax.fori_loop(1, 9, fine_source, 0, unroll=True)
    fine_half(1, 1, 9, 4, 24)
    fine_half(0, 2, 8, 6, 24)
    fine_last(7, 24)
    fine_red_residual()

    def restrict_fine(m, carry):
        v = (rf[0, m, 0, 8:24, :] + rf[1, m, 0, 8:24, :]) + (rf[0, m, 1, 8:24, :] + rf[1, m, 1, 8:24, :])
        rm[m, 0:16, :] = v
        b1[m + 5, 16:24, :] = 0.125 * (rm[m, pl.ds(0, 8, stride=2), :] + rm[m, pl.ds(1, 8, stride=2), :])
        return carry

    lax.fori_loop(3, 7, restrict_fine, 0, unroll=True)
    send(WIDE, b1_refs, s_b1, r_b1)

    def keep_black(m, carry):
        for t in (0, 1):
            pb0[m, t, 8:24, :] = pf[1, m, t, 8:24, :]
        return carry

    lax.fori_loop(3, 7, keep_black, 0, unroll=True)
    send(NEAR, pb_refs, s_pb, r_pb)
    send(FAR, f1_refs, s_f1, r_f1, len(NEAR))

    def mid_weights(m0, m1, r0, n, top):
        odd, h1 = odd_mid(n, r0), h1_of(n)
        win, nxt = pl.ds(r0, n), pl.ds(r0 + 1, n)

        def body(m, carry):
            valid = inside(n, 8 * b - 16 + r0, 8 * ny, pair_ok(2 * a - 4, m, 2 * nx))
            e0, e1_ = 2 * m, 2 * m + 1
            fx0, fx1, fx2_ = f1[0, e0, win, :], f1[0, e1_, win, :], f1[0, jnp.minimum(e1_ + 1, top), win, :]
            ym = [f1[1, e, win, :] for e in (e0, e1_)]
            yp = [f1[1, e, nxt, :] for e in (e0, e1_)]
            fz = [f1[2, e, win, :] for e in (e0, e1_)]
            zs = [jnp.where(h1, v, rot(v, 64)) for v in fz]
            zo = [jnp.where(h1, rot(v, 63), v) for v in fz]
            dg = [f1[3, e, win, :] for e in (e0, e1_)]
            for c in (0, 1):
                def pick(v):
                    return jnp.where(odd, v[1 - c], v[c])

                xo = jnp.where(odd, fx2_, fx0) if c == 0 else jnp.where(odd, fx0, fx2_)
                d = pick(dg)
                rd = jnp.where(valid, 1.0 / d, 0.0)
                for f, w in enumerate((fx1, xo, pick(ym), pick(yp), pick(zs), pick(zo))):
                    wm[6 * c + f, m, win, :] = w * rd
                dm[c, m, win, :] = d
                rdm[c, m, win, :] = rd
            return carry

        lax.fori_loop(m0, m1, body, 0, unroll=True)

    def mid_source(m0, m1, r0, n, start):
        odd = odd_mid(n, r0)
        win = pl.ds(r0, n)

        def body(m, carry):
            lo, hi = b1[2 * m, win, :], b1[2 * m + 1, win, :]
            first = 4.0 * jnp.where(odd, hi, lo) * rdm[0, m, win, :]
            sm[0, m, win, :] = first
            if start:
                pm[0, m, win, :] = first
            sm[1, m, win, :] = 4.0 * jnp.where(odd, lo, hi) * rdm[1, m, win, :]
            return carry

        lax.fori_loop(m0, m1, body, 0, unroll=True)

    def mid_nb(c, m, r0, n, odd, h1):
        o = 1 - c
        win = pl.ds(r0, n)
        xs, lo, hi = pm[o, m, win, :], pm[o, m - 1, win, :], pm[o, m + 1, win, :]
        xo = jnp.where(odd, hi, lo) if c == 0 else jnp.where(odd, lo, hi)
        zo = jnp.where(h1, rot(xs, 63), rot(xs, 65))
        total = wm[6 * c, m, win, :] * xs
        total = total + wm[6 * c + 1, m, win, :] * xo
        total = total + wm[6 * c + 2, m, win, :] * pm[o, m, pl.ds(r0 - 1, n), :]
        total = total + wm[6 * c + 3, m, win, :] * pm[o, m, pl.ds(r0 + 1, n), :]
        total = total + wm[6 * c + 4, m, win, :] * rot(xs, 64)
        return total + wm[6 * c + 5, m, win, :] * zo

    def mid_half(c, m0, m1, r0, n):
        odd, h1 = odd_mid(n, r0), h1_of(n)

        def body(m, carry):
            win = pl.ds(r0, n)
            pm[c, m, win, :] = sm[c, m, win, :] + mid_nb(c, m, r0, n, odd, h1)
            return carry

        lax.fori_loop(m0, m1, body, 0, unroll=True)

    arrive(NEAR, f1_refs, s_f1, r_f1)
    mid_weights(2, 8, 12, 16, 15)
    arrive(gy_steps, lw_refs, s_lw, r_lw)
    half_rows = pl.ds(20 * lax.rem(b, 2), 24)
    ring_send(lw.at[:, half_rows], lambda i: gw.at[i, :, half_rows], s_gw, r_gw)
    arrive(NEAR, b1_refs, s_b1, r_b1)
    mid_source(2, 8, 12, 16, True)
    mid_half(1, 2, 8, 13, 16)
    mid_half(0, 3, 7, 14, 16)
    mid_half(1, 3, 7, 15, 16)

    odd_own, h_own = odd_mid(8, 16), h1_of(8)
    own = pl.ds(16, 8)
    planes = []
    for m in (4, 5):
        lo, hi = b1[2 * m, own, :], b1[2 * m + 1, own, :]
        total = None
        for c in (0, 1):
            src = jnp.where(odd_own, hi, lo) if c == 0 else jnp.where(odd_own, lo, hi)
            nb = mid_nb(c, m, 16, 8, odd_own, h_own)
            res = src - dm[c, m, own, :] * (pm[c, m, own, :] - nb) * 0.25
            total = res if total is None else total + res
        rm[m, 0:8, :] = total
        rm[m, 8:16, :] = total
        planes.append(0.125 * zsum(rm[m, pl.ds(0, 8, stride=2), :] + rm[m, pl.ds(1, 8, stride=2), :]))
    lb[20:24, :] = jnp.where(h8, black(planes), red(planes))[0:4]
    send(gy_steps, lb_refs, s_lb, r_lb)
    for m in (4, 5):
        mb0[m, own, :] = pm[1, m, own, :]
    send(WIDE, mb_refs, s_mb, r_mb)

    arrive(FAR, f1_refs, s_f1, r_f1, len(NEAR))
    mid_weights(1, 9, 8, 24, 18)
    arrive(FAR, b1_refs, s_b1, r_b1, len(NEAR))
    mid_source(1, 9, 8, 24, False)

    arrive(gy_steps, lb_refs, s_lb, r_lb)
    ring_send(lb.at[0:44], lambda i: gb.at[i, 0:44], s_gb, r_gb)
    gw[4, :, 0:44] = lw[:, 0:44]
    gb[4, 0:44] = lb[0:44]

    LR = 48
    h48 = h1_of(LR)
    odd48 = odd_low(LR, 0)
    q48 = lax.rem(iota(LR, 1), 64)
    lwin = pl.ds(8, LR)

    def fold(lo, hi, half):
        if half == 0:
            return jnp.where(h48, rot(hi, 64), lo)
        return jnp.where(h48, hi, rot(lo, 64))

    ring_arrive(lw.at[:, half_rows], lambda i: gw.at[i, :, half_rows], s_gw, r_gw)
    for i in range(nx):
        if i != 4:
            relay(i)
    for i in range(nx):
        if i != 4:
            relay_arrive(i)

    def low_weights(s, carry):
        u = [fold(gw[s, f // 2], gw[s + 8, f // 2], f % 2) for f in range(6)]
        for c in (0, 1):
            third = jnp.where(q48 < 16, rot(u[c], 80), jnp.where(q48 < 32, rot(u[2 + c], 96), rot(u[4 + c], 112)))
            rdl[c, s, lwin, :] = jnp.where(q48 < 48, third, 0.0)
        rd = rdl[0, s, lwin, :]
        for f in range(6):
            ul[f, s + 1, lwin, :] = u[f]
            wl[f, s, lwin, :] = u[f] * rd
        return carry

    lax.fori_loop(0, 8, low_weights, 0, unroll=True)
    ul[1, 0, lwin, :] = rot(ul[1, 8, lwin, :], 64)
    ul[1, 9, lwin, :] = rot(ul[1, 1, lwin, :], 64)

    def low_black(s, carry):
        rd = rdl[1, s, lwin, :]
        wl[6, s, lwin, :] = ul[0, s + 1, lwin, :] * rd
        wl[7, s, lwin, :] = jnp.where(odd48, ul[1, s, lwin, :], ul[1, s + 2, lwin, :]) * rd
        wl[8, s, lwin, :] = ul[3, s + 1, pl.ds(7, LR), :] * rd
        wl[9, s, lwin, :] = ul[2, s + 1, pl.ds(9, LR), :] * rd
        wl[10, s, lwin, :] = rot(ul[5, s + 1, lwin, :], 1) * rd
        wl[11, s, lwin, :] = rot(ul[4, s + 1, lwin, :], 127) * rd
        return carry

    lax.fori_loop(0, 8, low_black, 0, unroll=True)

    ring_arrive(lb.at[0:44], lambda i: gb.at[i, 0:44], s_gb, r_gb)

    def low_source(s, carry):
        lo, hi = gb[s], gb[s + 8]
        first = 16.0 * fold(lo, hi, 0) * rdl[0, s, lwin, :]
        sl[0, s, lwin, :] = first
        plow[0, s + 1, lwin, :] = first
        sl[1, s, lwin, :] = 16.0 * fold(lo, hi, 1) * rdl[1, s, lwin, :]
        return carry

    lax.fori_loop(0, 8, low_source, 0, unroll=True)

    def low_ghosts(c, r0, n):
        win = pl.ds(r0, n)
        plow[c, 0, win, :] = rot(plow[c, 8, win, :], 64)
        plow[c, 9, win, :] = rot(plow[c, 1, win, :], 64)

    low_ghosts(0, 8, LR)
    for half in range(2, 2 * BOTTOM + 1):
        c = (half - 1) % 2
        reach = 4 + 2 * BOTTOM - half
        r0, n = 8 + 20 - reach, 8 * ((4 + 2 * reach + 7) // 8)
        odd = odd_low(n, r0)

        def low_body(s, carry, c=c, r0=r0, n=n, odd=odd):
            o = 1 - c
            win = pl.ds(r0, n)
            xs, lo, hi = plow[o, s + 1, win, :], plow[o, s, win, :], plow[o, s + 2, win, :]
            xo = jnp.where(odd, hi, lo) if c == 0 else jnp.where(odd, lo, hi)
            total = sl[c, s, win, :] + wl[6 * c, s, win, :] * xs
            total = total + wl[6 * c + 1, s, win, :] * xo
            total = total + wl[6 * c + 2, s, win, :] * plow[o, s + 1, pl.ds(r0 - 1, n), :]
            total = total + wl[6 * c + 3, s, win, :] * plow[o, s + 1, pl.ds(r0 + 1, n), :]
            total = total + wl[6 * c + 4, s, win, :] * rot(xs, 1)
            plow[c, s + 1, win, :] = total + wl[6 * c + 5, s, win, :] * rot(xs, 127)
            return carry

        lax.fori_loop(0, 8, low_body, 0, unroll=True)
        low_ghosts(c, r0, n)

    arrive(WIDE, mb_refs, s_mb, r_mb)
    odd16, h16 = odd_low(16, 0), h1_of(16)
    rows24 = pl.ds(8, 24)

    def mid_correct(s, carry):
        red_, black_ = plow[0, s + 3, pl.ds(24, 16), :], plow[1, s + 3, pl.ds(24, 16), :]
        for e in (0, 1):
            v = jnp.where(odd16, black_, red_) if e == 0 else jnp.where(odd16, red_, black_)
            v = jnp.where(h16, rot(v, 64), v)
            em[2 * s + e, pl.ds(0, 16, stride=2), :] = v
            em[2 * s + e, pl.ds(1, 16, stride=2), :] = v
            m = 2 * s + e
            add = em[m, 0:24, :] * jnp.where(pair_ok(2 * a - 4, m, 2 * nx), 1.0, 0.0)
            pm[1, m, rows24, :] = mb0[m, rows24, :] + add
        return carry

    lax.fori_loop(0, 5, mid_correct, 0, unroll=True)
    mid_half(0, 1, 9, 10, 24)
    mid_half(1, 1, 9, 11, 24)
    mid_half(0, 2, 8, 12, 16)
    mid_half(1, 2, 8, 13, 16)

    arrive(NEAR, pb_refs, s_pb, r_pb)
    odd_c = odd_mid(16, 13)

    for m in range(10):
        n, e = (m + 5) // 2, (m + 5) % 2
        red_, black_ = pm[0, n, pl.ds(13, 16), :], pm[1, n, pl.ds(13, 16), :]
        v = jnp.where(odd_c, black_, red_) if e == 0 else jnp.where(odd_c, red_, black_)
        e1[m, pl.ds(2, 16, stride=2), :] = v
        e1[m, pl.ds(3, 16, stride=2), :] = v
        for t in (0, 1):
            pf[1, m, t, pl.ds(3, 32), :] = pb0[m, t, pl.ds(3, 32), :] + e1[m, pl.ds(3, 32), :]

    fine_half(0, 1, 9, 4, 24)
    fine_half(1, 1, 9, 5, 24)
    fine_half(0, 2, 8, 6, 24)
    fine_last(7, 24)
    fine_red_residual()

    kk2 = lax.broadcasted_iota(jnp.int32, (2 * LANES, nz), 1)
    cc2 = lax.broadcasted_iota(jnp.int32, (2 * LANES, nz), 0)
    q2, hh2, tt2 = lax.rem(cc2, 64), lax.rem(lax.div(cc2, 64), 2), lax.div(cc2, 128)
    back = jnp.where(jnp.logical_and(kk2 == 4 * q2 + 2 * hh2 + tt2, q2 < 48), 1.0, 0.0).astype(F32)

    def join_from(src, out):
        for t in (0, 1):
            odd = odd_fine(16, 8, t)
            for m in range(4):
                r, k = src[0, 3 + m, t, 8:24, :], src[1, 3 + m, t, 8:24, :]
                xo_s[32 * m:32 * m + 16, t * LANES:(t + 1) * LANES] = jnp.where(odd, k, r)
                xo_s[32 * m + 16:32 * m + 32, t * LANES:(t + 1) * LANES] = jnp.where(odd, r, k)
        v = jnp.dot(xo_s[...], back, precision=lax.Precision.HIGHEST, preferred_element_type=F32)
        out[...] = v.reshape(out.shape)

    join_from(pf, out_p)
    put_p = pltpu.make_async_copy(out_p, p_hbm, out_sem.at[0])
    put_p.start()
    join_from(rf, out_r)
    put_r = pltpu.make_async_copy(out_r, r_hbm, out_sem.at[1])
    put_r.start()
    for ok, cp in started:
        if ok is None:
            cp().wait_send()
        else:
            @pl.when(ok)
            def _():
                cp().wait_send()
    put_p.wait()
    put_r.wait()


def solution(mesh):
    nx, ny = mesh.shape["gx"], mesh.shape["gy"]

    def local(right_side, phase):
        shape = right_side.shape
        v = lambda *dims: pltpu.VMEM(dims, F32)
        sems = []
        for n in (len(NEAR), len(NEAR), len(WIDE), len(WIDE), len(NEAR), len(WIDE), len(ALONG), len(ALONG), nx - 1, nx - 1, nx):
            sems += [pltpu.SemaphoreType.DMA((n,)), pltpu.SemaphoreType.DMA((n,))]
        fine = (10, 2, 40, LANES)
        return pl.pallas_call(
            functools.partial(kernel, nx, ny),
            out_shape=[jax.ShapeDtypeStruct(shape, F32)] * 2,
            in_specs=[pl.BlockSpec(memory_space=pl.ANY)] * 2,
            out_specs=[pl.BlockSpec(memory_space=pl.ANY)] * 2,
            scratch_shapes=[
                v(*shape), pltpu.VMEM(shape, jnp.int32), v(*shape), v(*shape),
                v(2, *fine), v(2, *fine), v(12, *fine), v(2, *fine), v(2, *fine), v(2, *fine), v(2, *fine), v(*fine),
                v(2, *fine), v(3, 10, 32, LANES), v(3, 5, 24, LANES),
                v(4, 21, 40, LANES), v(20, 40, LANES), v(12, 10, 40, LANES), v(2, 10, 40, LANES), v(2, 10, 40, LANES),
                v(2, 10, 40, LANES), v(2, 10, 40, LANES), v(10, 40, LANES), v(10, 16, LANES), v(10, 32, LANES),
                v(3, 48, LANES), v(48, LANES), v(16, 3, 48, LANES), v(16, 48, LANES), v(6, 10, 64, LANES),
                v(12, 8, 64, LANES), v(2, 8, 64, LANES), v(2, 8, 64, LANES), v(2, 10, 64, LANES), v(10, 40, LANES),
                v(128, 2 * LANES),
                pltpu.SemaphoreType.DMA((2,)), pltpu.SemaphoreType.DMA((2,)),
            ] + sems,
            compiler_params=pltpu.CompilerParams(
                collective_id=0, has_side_effects=True, vmem_limit_bytes=48 * 2**20
            ),
        )(right_side, phase)

    spec = P("gx", "gy", None)
    return jax.shard_map(local, mesh=mesh, in_specs=(spec, spec), out_specs=(spec, spec), check_vma=False)
```

```python
import functools

import numpy as np

import jax
import jax.numpy as jnp
from jax import lax
from jax.experimental import pallas as pl
from jax.experimental.pallas import tpu as pltpu
from jax.sharding import PartitionSpec as P

F32 = jnp.float32
MESH = pl.DeviceIdType.MESH
LANES = 128
BOTTOM = 8

_L, _D = np.float32(1.0), np.float32(0.1)
W_LL = float(np.float32(2) * _L * _L / (_L + _L))
W_MX = float(np.float32(2) * _L * _D / (_L + _D))
W_DD = float(np.float32(2) * _D * _D / (_D + _D))

REACH = 5
NEAR = [(dx, dy) for dx in (-1, 0, 1) for dy in (-1, 0, 1) if (dx, dy) != (0, 0)]
FAR = [(dx, dy) for dx in (-2, 2) for dy in (-1, 0, 1)]
WIDE = NEAR + FAR
ALONG = [d * s for d in range(1, REACH + 1) for s in (1, -1)]


def rot(v, shift):
    return pltpu.roll(v, shift, 1)


def span(step, own, size, take):
    if step == 0:
        return own, size
    if isinstance(take, tuple):
        take = take[0] if step < 0 else take[1]
    if step > 0:
        return own + size - take, take
    return own, take


def kernel(
    nx, ny,
    rs_hbm, ph_hbm, out_p, out_r,
    rs_in, ph_in,
    ph, rs, wf, sf, df, rdf, pf, pb0, rf, tf, f1o,
    f1, b1, wm, sm, dm, rdm, pm, mb0, rm, em,
    lw, lb, gw, gb, ul, wl, sl, rdl, plow, e1, xo_s,
    in_sem,
    s_ph, r_ph, s_rs, r_rs, s_f1, r_f1, s_b1, r_b1, s_pb, r_pb, s_mb, r_mb,
    s_lw, r_lw, s_lb, r_lb, s_gw, r_gw, s_gb, r_gb, s_re, r_re,
):
    a = lax.axis_index("gx")
    b = lax.axis_index("gy")

    def exists(dx, dy):
        ok = None
        for pos, d, n in ((a, dx, nx), (b, dy, ny)):
            if d:
                one = (pos + d >= 0) if d < 0 else (pos + d < n)
                ok = one if ok is None else jnp.logical_and(ok, one)
        return ok

    started = []

    def copy(src, dst, ssem, rsem, i, dev):
        return pltpu.make_async_remote_copy(
            src_ref=src, dst_ref=dst, send_sem=ssem.at[i], recv_sem=rsem.at[i], device_id=dev, device_id_type=MESH
        )

    def send(steps, refs, ssem, rsem, base=0):
        for i, (dx, dy) in enumerate(steps):
            src, dst = refs(dx, dy)
            cp = functools.partial(copy, src, dst, ssem, rsem, base + i, (a + dx, b + dy))
            ok = exists(dx, dy)

            @pl.when(ok)
            def _():
                cp().start()

            started.append((ok, cp))

    def arrive(steps, refs, ssem, rsem, base=0):
        for i, (dx, dy) in enumerate(steps):
            src, dst = refs(dx, dy)

            @pl.when(exists(-dx, -dy))
            def _():
                copy(src, dst, ssem, rsem, base + i, (a - dx, b - dy)).wait_recv()

    def ring_send(src, dst, ssem, rsem):
        for d in range(1, nx):
            cp = functools.partial(copy, src, dst((4 - d) % nx), ssem, rsem, d - 1, (lax.rem(a + d, nx), b))
            cp().start()
            started.append((None, cp))

    def relay_refs(i):
        core = lax.rem(b, 2)
        return gw.at[i, :, pl.ds(4 + 16 * core, 20)], gw.at[i, :, pl.ds(24 * core, 20)], (a, b + 1 - 2 * core)

    def relay(i):
        src, dst, dev = relay_refs(i)
        cp = functools.partial(copy, src, dst, s_re, r_re, i, dev)
        cp().start()
        started.append((None, cp))

    def relay_arrive(i):
        src, dst, dev = relay_refs(i)
        core = lax.rem(b, 2)
        copy(src, gw.at[i, :, pl.ds(24 - 24 * core, 20)], s_re, r_re, i, dev).wait_recv()

    def ring_arrive(src, dst, ssem, rsem):
        for d in range(1, nx):
            copy(src, dst((4 - d) % nx), ssem, rsem, d - 1, (lax.rem(a + nx - d, nx), b)).wait_recv()

    def fine_refs(arr, lead, pairs, rows):
        def refs(dx, dy):
            x0, xn = span(dx, 3, 4, 2 if dy else pairs)
            y0, yn = span(dy, 8, 16, rows - 1 if dx else rows)
            pre = (slice(None),) * lead
            return (
                arr.at[pre + (pl.ds(x0, xn), slice(None), pl.ds(y0, yn))],
                arr.at[pre + (pl.ds(x0 - 4 * dx, xn), slice(None), pl.ds(y0 - 16 * dy, yn))],
            )

        return refs

    def mid_refs(arr, lead, own, size, far, rows, far_corner):
        def refs(dx, dy):
            x0, xn = span(dx, own, size, size if abs(dx) < 2 else far_corner[0] if dy else far)
            y0, yn = span(dy, 16, 8, rows[0] if dx == 0 else rows[1] if abs(dx) < 2 else far_corner[1])
            pre = (slice(None),) * lead
            return (
                arr.at[pre + (pl.ds(x0, xn), pl.ds(y0, yn))],
                arr.at[pre + (pl.ds(x0 - size * dx, xn), pl.ds(y0 - 8 * dy, yn))],
            )

        return refs

    def low_refs(arr, lead):
        def refs(dx, dy):
            pre = (slice(None),) * lead
            return arr.at[pre + (pl.ds(20, 4),)], arr.at[pre + (pl.ds(20 - 4 * dy, 4),)]

        return refs

    ph_refs = fine_refs(ph, 1, 3, 5)
    rs_refs = fine_refs(rs, 1, 2, 4)
    pb_refs = fine_refs(pb0, 0, 3, 5)
    f1_refs = mid_refs(f1, 1, 8, 4, (3, 2), ((7, 6), (6, 5)), (2, 2))
    b1_refs = mid_refs(b1, 0, 8, 4, 2, (6, 5), (1, 1))
    mb_refs = mid_refs(mb0, 0, 4, 2, 2, (7, 6), (1, 2))
    lw_refs = low_refs(lw, 1)
    lb_refs = low_refs(lb, 0)
    gy_steps = [(0, d) for d in ALONG]

    in_rs = pltpu.make_async_copy(rs_hbm, rs_in, in_sem.at[0])
    in_ph = pltpu.make_async_copy(ph_hbm, ph_in, in_sem.at[1])
    in_ph.start()
    in_rs.start()

    bar = pltpu.get_barrier_semaphore()
    greet = list(WIDE) + [(0, d) for d in ALONG if abs(d) > 1]
    count = jnp.int32(0)
    for dx, dy in greet:
        ok = exists(dx, dy)

        @pl.when(ok)
        def _():
            pl.semaphore_signal(bar, inc=1, device_id=(a + dx, b + dy), device_id_type=MESH)

        count = count + ok.astype(jnp.int32)
    for d in range(1, nx):
        t = lax.rem(a + d, nx)
        far = jnp.logical_or(t > a + 2, t < a - 2)

        @pl.when(far)
        def _():
            pl.semaphore_signal(bar, inc=1, device_id=(t, b), device_id_type=MESH)

        count = count + far.astype(jnp.int32)

    def iota(rows, dim):
        return lax.broadcasted_iota(jnp.int32, (rows, LANES), dim)

    def h1_of(rows):
        return iota(rows, 1) >= 64

    def lane_ok(rows):
        return lax.rem(iota(rows, 1), 64) < 48

    def odd_fine(rows, start, t):
        return lax.rem(iota(rows, 0) + (start + t), 2) == 1

    def odd_mid(rows, start):
        return lax.rem(iota(rows, 0) + start + lax.div(iota(rows, 1), 64), 2) == 1

    def odd_low(rows, start):
        return lax.rem(iota(rows, 0) + start + iota(rows, 1), 2) == 1

    def zero(ref):
        ref[...] = jnp.zeros(ref.shape, F32)

    @pl.when(a == 0)
    def _():
        zero(ph.at[:, 0:3]); zero(rs.at[:, 0:3]); zero(pb0.at[0:3]); zero(f1.at[:, 0:8]); zero(b1.at[0:8]); zero(mb0.at[0:4])

    @pl.when(a == 1)
    def _():
        zero(f1.at[:, 0:4]); zero(b1.at[0:4]); zero(mb0.at[0:2])

    @pl.when(a == nx - 1)
    def _():
        zero(ph.at[:, 7:10]); zero(rs.at[:, 7:10]); zero(pb0.at[7:10])
        zero(f1.at[:, 12:21]); zero(b1.at[12:20]); zero(mb0.at[6:10])

    @pl.when(a == nx - 2)
    def _():
        zero(f1.at[:, 16:21]); zero(b1.at[16:20]); zero(mb0.at[8:10])

    @pl.when(b == 0)
    def _():
        zero(ph.at[:, :, :, 0:8]); zero(rs.at[:, :, :, 0:8]); zero(pb0.at[:, :, 0:8])
        zero(f1.at[:, :, 0:16]); zero(b1.at[:, 0:16]); zero(mb0.at[:, 0:16])

    @pl.when(b == ny - 1)
    def _():
        zero(ph.at[:, :, :, 24:32]); zero(rs.at[:, :, :, 24:32]); zero(pb0.at[:, :, 24:32])
        zero(f1.at[:, :, 24:40]); zero(b1.at[:, 24:40]); zero(mb0.at[:, 24:40])

    for d in ALONG:
        @pl.when(jnp.logical_not(exists(0, d)))
        def _():
            zero(lw.at[:, pl.ds(20 + 4 * d, 4)])
            zero(lb.at[pl.ds(20 + 4 * d, 4)])

    nz = rs_in.shape[2]
    kk = lax.broadcasted_iota(jnp.int32, (nz, 2 * LANES), 0)
    cc = lax.broadcasted_iota(jnp.int32, (nz, 2 * LANES), 1)
    q, hh, tt = lax.rem(cc, 64), lax.rem(lax.div(cc, 64), 2), lax.div(cc, 128)
    perm = jnp.where(jnp.logical_and(kk == 4 * q + 2 * hh + tt, q < 48), 1.0, 0.0).astype(F32)

    def split_into(values, dst):
        for t in (0, 1):
            odd = odd_fine(16, 0, t)
            for m in range(4):
                lo = values[32 * m:32 * m + 16, t * LANES:(t + 1) * LANES]
                hi = values[32 * m + 16:32 * m + 32, t * LANES:(t + 1) * LANES]
                dst[0, 3 + m, t, 8:24, :] = jnp.where(odd, hi, lo)
                dst[1, 3 + m, t, 8:24, :] = jnp.where(odd, lo, hi)

    in_ph.wait()
    labels = jnp.where(ph_in[...] == 1, 1.0, 0.0).astype(F32).reshape(128, nz)
    split_into(jnp.dot(labels, perm, preferred_element_type=F32), ph)
    in_rs.wait()
    block = rs_in[...].reshape(128, nz)
    split_into(jnp.dot(block, perm, precision=lax.Precision.HIGHEST, preferred_element_type=F32), rs)

    pl.semaphore_wait(bar, count)
    send(NEAR, ph_refs, s_ph, r_ph)
    send(NEAR, rs_refs, s_rs, r_rs)

    def pair_ok(first, m, total):
        g = first + m
        return jnp.logical_and(g >= 0, g < total)

    def inside(rows, start, total, ok):
        g = iota(rows, 0) + (start + jnp.where(ok, 0, -4096))
        return jnp.logical_and(jnp.logical_and(g >= 0, g < total), lane_ok(rows))

    def fine_sides(arr, c, m, t, r0, n, odd, h1):
        o = 1 - c
        xs = arr[o, m, t, pl.ds(r0, n), :]
        lo = arr[o, m - 1, t, pl.ds(r0, n), :]
        hi = arr[o, m + 1, t, pl.ds(r0, n), :]
        xo = jnp.where(odd, hi, lo) if c == 0 else jnp.where(odd, lo, hi)
        ym = arr[o, m, t, pl.ds(r0 - 1, n), :]
        yp = arr[o, m, t, pl.ds(r0 + 1, n), :]
        zs = arr[o, m, 1 - t, pl.ds(r0, n), :]
        if t == 0:
            zo = jnp.where(h1, rot(zs, 64), rot(zs, 65))
        else:
            zo = jnp.where(h1, rot(zs, 63), rot(zs, 64))
        return xs, xo, ym, yp, zs, zo

    R0, RN = 4, 24
    odd24 = [odd_fine(RN, R0, 0), odd_fine(RN, R0, 1)]
    h24 = h1_of(RN)

    arrive(NEAR, ph_refs, s_ph, r_ph)

    def fine_weights(m, carry):
        valid = inside(RN, 16 * b - 8 + R0, 16 * ny, pair_ok(4 * a - 3, m, 4 * nx))
        fx = fy = fz = None
        for t in (0, 1):
            both = []
            for c in (0, 1):
                dense = ph[c, m, t, pl.ds(R0, RN), :] > 0.5
                on = jnp.where(dense, W_DD, W_MX)
                off = jnp.where(dense, W_MX, W_LL)
                w = [jnp.where(s > 0.5, on, off) for s in fine_sides(ph, c, m, t, R0, RN, odd24[t], h24)]
                dg = ((((w[0] + w[1]) + w[2]) + w[3]) + w[4]) + w[5]
                rd = jnp.where(valid, 1.0 / dg, 0.0)
                for f in range(6):
                    wf[6 * c + f, m, t, pl.ds(R0, RN), :] = w[f] * rd
                df[c, m, t, pl.ds(R0, RN), :] = dg
                rdf[c, m, t, pl.ds(R0, RN), :] = rd
                both.append(w)
            x = jnp.where(odd24[t], both[1][1], both[0][1])
            y = both[0][2] + both[1][2]
            fx = x if fx is None else fx + x
            fy = y if fy is None else fy + y
            if t == 0:
                fz = both[0][5] + both[1][5]
        tf[0, m, 0:RN, :] = fx
        tf[1, m, 0:RN, :] = fy
        tf[2, m, 0:RN, :] = fz
        return carry

    lax.fori_loop(1, 9, fine_weights, 0)

    even, oddr = pl.ds(0, 16, stride=2), pl.ds(1, 16, stride=2)

    def mid_faces(i, carry):
        f1o[0, i, 0:16, :] = 0.25 * (tf[0, i + 3, even, :] + tf[0, i + 3, oddr, :])
        f1o[1, i, 0:16, :] = 0.25 * tf[1, i + 3, even, :]
        f1o[2, i, 0:16, :] = 0.25 * (tf[2, i + 3, even, :] + tf[2, i + 3, oddr, :])
        return carry

    lax.fori_loop(0, 5, mid_faces, 0, unroll=True)
    h8 = h1_of(8)
    for i in range(4):
        fx, fxn = f1o[0, i, 2:10, :], f1o[0, i + 1, 2:10, :]
        fy, fyn = f1o[1, i, 2:10, :], f1o[1, i, 3:11, :]
        fz = f1o[2, i, 2:10, :]
        fzn = jnp.where(h8, rot(fz, 63), rot(fz, 64))
        dg = ((((fx + fxn) + fy) + fyn) + fz) + fzn
        for f, w in enumerate((fx, fy, fz)):
            f1[f, 8 + i, 16:24, :] = jnp.where(lane_ok(8), w, rot(dg, 48 - 16 * f))
    send(NEAR, f1_refs, s_f1, r_f1)

    def zsum(v):
        return v + rot(v, 64)

    fx2 = [0.25 * zsum(f1o[0, 2 * i, pl.ds(2, 8, stride=2), :] + f1o[0, 2 * i, pl.ds(3, 8, stride=2), :]) for i in range(3)]
    fy2, fy2n, fz2, fz2n = [], [], [], []
    for i in range(2):
        fy2.append(0.25 * zsum(f1o[1, 2 * i, pl.ds(2, 8, stride=2), :] + f1o[1, 2 * i + 1, pl.ds(2, 8, stride=2), :]))
        fy2n.append(0.25 * zsum(f1o[1, 2 * i, pl.ds(4, 8, stride=2), :] + f1o[1, 2 * i + 1, pl.ds(4, 8, stride=2), :]))
        v = (f1o[2, 2 * i, pl.ds(2, 8, stride=2), :] + f1o[2, 2 * i, pl.ds(3, 8, stride=2), :]) + (
            f1o[2, 2 * i + 1, pl.ds(2, 8, stride=2), :] + f1o[2, 2 * i + 1, pl.ds(3, 8, stride=2), :]
        )
        v = 0.25 * jnp.where(h8, rot(v, 64), v)
        fz2.append(v)
        fz2n.append(rot(v, 127))
    odd8 = odd_low(8, 0)
    dg2 = [((((fx2[i] + fx2[i + 1]) + fy2[i]) + fy2n[i]) + fz2[i]) + fz2n[i] for i in range(2)]
    rd2 = [jnp.where(lane_ok(8), 1.0 / d, 0.0) for d in dg2]

    def red(v):
        return jnp.where(odd8, v[1], v[0])

    def black(v):
        return jnp.where(odd8, v[0], v[1])

    edge_low = jnp.where(a == 0, 0.0, 1.0)
    edge_high = jnp.where(a == nx - 1, 0.0, 1.0)
    xo2 = jnp.where(odd8, fx2[2] * edge_high, fx2[0] * edge_low)
    inv = jnp.where(h8, black(rd2), red(rd2))
    for f, (first, second) in enumerate(((fx2[1], xo2), (red(fy2), red(fy2n)), (red(fz2), red(fz2n)))):
        v = jnp.where(lane_ok(8), jnp.where(h8, second, first), rot(inv, 48 - 16 * f))
        lw[f, 20:24, :] = v[0:4]
    send(gy_steps, lw_refs, s_lw, r_lw)

    def fine_nb(c, m, t, r0, n, odd, h1):
        v = fine_sides(pf, c, m, t, r0, n, odd, h1)
        total = wf[6 * c, m, t, pl.ds(r0, n), :] * v[0]
        for f in range(1, 6):
            total = total + wf[6 * c + f, m, t, pl.ds(r0, n), :] * v[f]
        return total

    def fine_half(c, m0, m1, r0, n):
        odd = [odd_fine(n, r0, 0), odd_fine(n, r0, 1)]
        h1 = h1_of(n)

        def body(m, carry):
            for t in (0, 1):
                nb = fine_nb(c, m, t, r0, n, odd[t], h1)
                pf[c, m, t, pl.ds(r0, n), :] = sf[c, m, t, pl.ds(r0, n), :] + nb
            return carry

        lax.fori_loop(m0, m1, body, 0, unroll=True)

    def fine_last(r0, n):
        odd = [odd_fine(n, r0, 0), odd_fine(n, r0, 1)]
        h1 = h1_of(n)

        def body(m, carry):
            for t in (0, 1):
                win = pl.ds(r0, n)
                nb = fine_nb(1, m, t, r0, n, odd[t], h1)
                fresh = sf[1, m, t, win, :] + nb
                pf[1, m, t, win, :] = fresh
                rf[1, m, t, win, :] = rs[1, m, t, win, :] - df[1, m, t, win, :] * (fresh - nb)
            return carry

        lax.fori_loop(2, 8, body, 0, unroll=True)

    def fine_red_residual():
        odd = [odd_fine(16, 8, 0), odd_fine(16, 8, 1)]
        h1 = h1_of(16)

        def body(m, carry):
            for t in (0, 1):
                win = pl.ds(8, 16)
                nb = fine_nb(0, m, t, 8, 16, odd[t], h1)
                rf[0, m, t, win, :] = rs[0, m, t, win, :] - df[0, m, t, win, :] * (pf[0, m, t, win, :] - nb)
            return carry

        lax.fori_loop(3, 7, body, 0, unroll=True)

    arrive(NEAR, rs_refs, s_rs, r_rs)

    def fine_source(m, carry):
        win = pl.ds(R0, RN)
        for t in (0, 1):
            first = rs[0, m, t, win, :] * rdf[0, m, t, win, :]
            sf[0, m, t, win, :] = first
            pf[0, m, t, win, :] = first
            sf[1, m, t, win, :] = rs[1, m, t, win, :] * rdf[1, m, t, win, :]
        return carry

    lax.fori_loop(1, 9, fine_source, 0, unroll=True)
    fine_half(1, 1, 9, 4, 24)
    fine_half(0, 2, 8, 6, 24)
    fine_last(7, 24)
    fine_red_residual()

    def restrict_fine(m, carry):
        v = (rf[0, m, 0, 8:24, :] + rf[1, m, 0, 8:24, :]) + (rf[0, m, 1, 8:24, :] + rf[1, m, 1, 8:24, :])
        rm[m, 0:16, :] = v
        b1[m + 5, 16:24, :] = 0.125 * (rm[m, pl.ds(0, 8, stride=2), :] + rm[m, pl.ds(1, 8, stride=2), :])
        return carry

    lax.fori_loop(3, 7, restrict_fine, 0, unroll=True)
    send(WIDE, b1_refs, s_b1, r_b1)

    def keep_black(m, carry):
        for t in (0, 1):
            pb0[m, t, 8:24, :] = pf[1, m, t, 8:24, :]
        return carry

    lax.fori_loop(3, 7, keep_black, 0, unroll=True)
    send(NEAR, pb_refs, s_pb, r_pb)
    send(FAR, f1_refs, s_f1, r_f1, len(NEAR))

    def mid_weights(m0, m1, r0, n, top):
        odd, h1 = odd_mid(n, r0), h1_of(n)
        win, nxt = pl.ds(r0, n), pl.ds(r0 + 1, n)
        q = lax.rem(iota(n, 1), 64)
        q16, q32 = q < 16, q < 32

        def body(m, carry):
            valid = inside(n, 8 * b - 16 + r0, 8 * ny, pair_ok(2 * a - 4, m, 2 * nx))
            e0, e1_ = 2 * m, 2 * m + 1
            fx0, fx1, fx2_ = f1[0, e0, win, :], f1[0, e1_, win, :], f1[0, jnp.minimum(e1_ + 1, top), win, :]
            ym = [f1[1, e, win, :] for e in (e0, e1_)]
            yp = [f1[1, e, nxt, :] for e in (e0, e1_)]
            fz = [f1[2, e, win, :] for e in (e0, e1_)]
            zs = [jnp.where(h1, v, rot(v, 64)) for v in fz]
            zo = [jnp.where(h1, rot(v, 63), v) for v in fz]
            dg = [
                jnp.where(q16, rot(f1[0, e, win, :], 80), jnp.where(q32, rot(f1[1, e, win, :], 96), rot(f1[2, e, win, :], 112)))
                for e in (e0, e1_)
            ]
            for c in (0, 1):
                def pick(v):
                    return jnp.where(odd, v[1 - c], v[c])

                xo = jnp.where(odd, fx2_, fx0) if c == 0 else jnp.where(odd, fx0, fx2_)
                d = pick(dg)
                rd = jnp.where(valid, 1.0 / d, 0.0)
                for f, w in enumerate((fx1, xo, pick(ym), pick(yp), pick(zs), pick(zo))):
                    wm[6 * c + f, m, win, :] = w * rd
                dm[c, m, win, :] = d
                rdm[c, m, win, :] = rd
            return carry

        lax.fori_loop(m0, m1, body, 0, unroll=True)

    def mid_source(m0, m1, r0, n, start):
        odd = odd_mid(n, r0)
        win = pl.ds(r0, n)

        def body(m, carry):
            lo, hi = b1[2 * m, win, :], b1[2 * m + 1, win, :]
            first = 4.0 * jnp.where(odd, hi, lo) * rdm[0, m, win, :]
            sm[0, m, win, :] = first
            if start:
                pm[0, m, win, :] = first
            sm[1, m, win, :] = 4.0 * jnp.where(odd, lo, hi) * rdm[1, m, win, :]
            return carry

        lax.fori_loop(m0, m1, body, 0, unroll=True)

    def mid_nb(c, m, r0, n, odd, h1):
        o = 1 - c
        win = pl.ds(r0, n)
        xs, lo, hi = pm[o, m, win, :], pm[o, m - 1, win, :], pm[o, m + 1, win, :]
        xo = jnp.where(odd, hi, lo) if c == 0 else jnp.where(odd, lo, hi)
        zo = jnp.where(h1, rot(xs, 63), rot(xs, 65))
        total = wm[6 * c, m, win, :] * xs
        total = total + wm[6 * c + 1, m, win, :] * xo
        total = total + wm[6 * c + 2, m, win, :] * pm[o, m, pl.ds(r0 - 1, n), :]
        total = total + wm[6 * c + 3, m, win, :] * pm[o, m, pl.ds(r0 + 1, n), :]
        total = total + wm[6 * c + 4, m, win, :] * rot(xs, 64)
        return total + wm[6 * c + 5, m, win, :] * zo

    def mid_half(c, m0, m1, r0, n):
        odd, h1 = odd_mid(n, r0), h1_of(n)

        def body(m, carry):
            win = pl.ds(r0, n)
            pm[c, m, win, :] = sm[c, m, win, :] + mid_nb(c, m, r0, n, odd, h1)
            return carry

        lax.fori_loop(m0, m1, body, 0, unroll=True)

    arrive(NEAR, f1_refs, s_f1, r_f1)
    mid_weights(2, 8, 12, 16, 15)
    arrive(gy_steps, lw_refs, s_lw, r_lw)
    half_rows = pl.ds(20 * lax.rem(b, 2), 24)
    ring_send(lw.at[:, half_rows], lambda i: gw.at[i, :, half_rows], s_gw, r_gw)
    arrive(NEAR, b1_refs, s_b1, r_b1)
    mid_source(2, 8, 12, 16, True)
    mid_half(1, 2, 8, 13, 16)
    mid_half(0, 3, 7, 14, 16)
    mid_half(1, 3, 7, 15, 16)

    odd_own, h_own = odd_mid(8, 16), h1_of(8)
    own = pl.ds(16, 8)
    planes = []
    for m in (4, 5):
        lo, hi = b1[2 * m, own, :], b1[2 * m + 1, own, :]
        total = None
        for c in (0, 1):
            src = jnp.where(odd_own, hi, lo) if c == 0 else jnp.where(odd_own, lo, hi)
            nb = mid_nb(c, m, 16, 8, odd_own, h_own)
            res = src - dm[c, m, own, :] * (pm[c, m, own, :] - nb) * 0.25
            total = res if total is None else total + res
        rm[m, 0:8, :] = total
        rm[m, 8:16, :] = total
        planes.append(0.125 * zsum(rm[m, pl.ds(0, 8, stride=2), :] + rm[m, pl.ds(1, 8, stride=2), :]))
    lb[20:24, :] = jnp.where(h8, black(planes), red(planes))[0:4]
    send(gy_steps, lb_refs, s_lb, r_lb)
    for m in (4, 5):
        mb0[m, own, :] = pm[1, m, own, :]
    send(WIDE, mb_refs, s_mb, r_mb)

    arrive(FAR, f1_refs, s_f1, r_f1, len(NEAR))
    mid_weights(1, 9, 8, 24, 18)
    arrive(FAR, b1_refs, s_b1, r_b1, len(NEAR))
    mid_source(1, 9, 8, 24, False)

    arrive(gy_steps, lb_refs, s_lb, r_lb)
    ring_send(lb.at[0:44], lambda i: gb.at[i, 0:44], s_gb, r_gb)
    gw[4, :, 0:44] = lw[:, 0:44]
    gb[4, 0:44] = lb[0:44]

    LR = 48
    h48 = h1_of(LR)
    odd48 = odd_low(LR, 0)
    q48 = lax.rem(iota(LR, 1), 64)
    lwin = pl.ds(8, LR)

    def fold(lo, hi, half):
        if half == 0:
            return jnp.where(h48, rot(hi, 64), lo)
        return jnp.where(h48, hi, rot(lo, 64))

    ring_arrive(lw.at[:, half_rows], lambda i: gw.at[i, :, half_rows], s_gw, r_gw)
    for i in range(nx):
        if i != 4:
            relay(i)
    for i in range(nx):
        if i != 4:
            relay_arrive(i)

    def low_weights(s, carry):
        u = [fold(gw[s, f // 2], gw[s + 8, f // 2], f % 2) for f in range(6)]
        for c in (0, 1):
            third = jnp.where(q48 < 16, rot(u[c], 80), jnp.where(q48 < 32, rot(u[2 + c], 96), rot(u[4 + c], 112)))
            rdl[c, s, lwin, :] = jnp.where(q48 < 48, third, 0.0)
        rd = rdl[0, s, lwin, :]
        for f in range(6):
            ul[f, s + 1, lwin, :] = u[f]
            wl[f, s, lwin, :] = u[f] * rd
        return carry

    lax.fori_loop(0, 8, low_weights, 0, unroll=True)
    ul[1, 0, lwin, :] = rot(ul[1, 8, lwin, :], 64)
    ul[1, 9, lwin, :] = rot(ul[1, 1, lwin, :], 64)

    def low_black(s, carry):
        rd = rdl[1, s, lwin, :]
        wl[6, s, lwin, :] = ul[0, s + 1, lwin, :] * rd
        wl[7, s, lwin, :] = jnp.where(odd48, ul[1, s, lwin, :], ul[1, s + 2, lwin, :]) * rd
        wl[8, s, lwin, :] = ul[3, s + 1, pl.ds(7, LR), :] * rd
        wl[9, s, lwin, :] = ul[2, s + 1, pl.ds(9, LR), :] * rd
        wl[10, s, lwin, :] = rot(ul[5, s + 1, lwin, :], 1) * rd
        wl[11, s, lwin, :] = rot(ul[4, s + 1, lwin, :], 127) * rd
        return carry

    lax.fori_loop(0, 8, low_black, 0, unroll=True)

    ring_arrive(lb.at[0:44], lambda i: gb.at[i, 0:44], s_gb, r_gb)

    def low_source(s, carry):
        lo, hi = gb[s], gb[s + 8]
        first = 16.0 * fold(lo, hi, 0) * rdl[0, s, lwin, :]
        sl[0, s, lwin, :] = first
        plow[0, s + 1, lwin, :] = first
        sl[1, s, lwin, :] = 16.0 * fold(lo, hi, 1) * rdl[1, s, lwin, :]
        return carry

    lax.fori_loop(0, 8, low_source, 0, unroll=True)

    def low_ghosts(c, r0, n):
        win = pl.ds(r0, n)
        plow[c, 0, win, :] = rot(plow[c, 8, win, :], 64)
        plow[c, 9, win, :] = rot(plow[c, 1, win, :], 64)

    low_ghosts(0, 8, LR)
    for half in range(2, 2 * BOTTOM + 1):
        c = (half - 1) % 2
        reach = 4 + 2 * BOTTOM - half
        r0, n = 8 + 20 - reach, 8 * ((4 + 2 * reach + 7) // 8)
        odd = odd_low(n, r0)

        def low_body(s, carry, c=c, r0=r0, n=n, odd=odd):
            o = 1 - c
            win = pl.ds(r0, n)
            xs, lo, hi = plow[o, s + 1, win, :], plow[o, s, win, :], plow[o, s + 2, win, :]
            xo = jnp.where(odd, hi, lo) if c == 0 else jnp.where(odd, lo, hi)
            total = sl[c, s, win, :] + wl[6 * c, s, win, :] * xs
            total = total + wl[6 * c + 1, s, win, :] * xo
            total = total + wl[6 * c + 2, s, win, :] * plow[o, s + 1, pl.ds(r0 - 1, n), :]
            total = total + wl[6 * c + 3, s, win, :] * plow[o, s + 1, pl.ds(r0 + 1, n), :]
            total = total + wl[6 * c + 4, s, win, :] * rot(xs, 1)
            plow[c, s + 1, win, :] = total + wl[6 * c + 5, s, win, :] * rot(xs, 127)
            return carry

        lax.fori_loop(0, 8, low_body, 0, unroll=True)
        low_ghosts(c, r0, n)

    arrive(WIDE, mb_refs, s_mb, r_mb)
    odd16, h16 = odd_low(16, 0), h1_of(16)
    rows24 = pl.ds(8, 24)

    def mid_correct(s, carry):
        red_, black_ = plow[0, s + 3, pl.ds(24, 16), :], plow[1, s + 3, pl.ds(24, 16), :]
        for e in (0, 1):
            v = jnp.where(odd16, black_, red_) if e == 0 else jnp.where(odd16, red_, black_)
            v = jnp.where(h16, rot(v, 64), v)
            em[2 * s + e, pl.ds(0, 16, stride=2), :] = v
            em[2 * s + e, pl.ds(1, 16, stride=2), :] = v
            m = 2 * s + e
            add = em[m, 0:24, :] * jnp.where(pair_ok(2 * a - 4, m, 2 * nx), 1.0, 0.0)
            pm[1, m, rows24, :] = mb0[m, rows24, :] + add
        return carry

    lax.fori_loop(0, 5, mid_correct, 0, unroll=True)
    mid_half(0, 1, 9, 10, 24)
    mid_half(1, 1, 9, 11, 24)
    mid_half(0, 2, 8, 12, 16)
    mid_half(1, 2, 8, 13, 16)

    arrive(NEAR, pb_refs, s_pb, r_pb)
    odd_c = odd_mid(16, 13)

    for m in range(10):
        n, e = (m + 5) // 2, (m + 5) % 2
        red_, black_ = pm[0, n, pl.ds(13, 16), :], pm[1, n, pl.ds(13, 16), :]
        v = jnp.where(odd_c, black_, red_) if e == 0 else jnp.where(odd_c, red_, black_)
        e1[m, pl.ds(2, 16, stride=2), :] = v
        e1[m, pl.ds(3, 16, stride=2), :] = v
        for t in (0, 1):
            pf[1, m, t, pl.ds(3, 32), :] = pb0[m, t, pl.ds(3, 32), :] + e1[m, pl.ds(3, 32), :]

    fine_half(0, 1, 9, 4, 24)
    fine_half(1, 1, 9, 5, 24)
    fine_half(0, 2, 8, 6, 24)
    fine_last(7, 24)
    fine_red_residual()

    kk2 = lax.broadcasted_iota(jnp.int32, (2 * LANES, nz), 1)
    cc2 = lax.broadcasted_iota(jnp.int32, (2 * LANES, nz), 0)
    q2, hh2, tt2 = lax.rem(cc2, 64), lax.rem(lax.div(cc2, 64), 2), lax.div(cc2, 128)
    back = jnp.where(jnp.logical_and(kk2 == 4 * q2 + 2 * hh2 + tt2, q2 < 48), 1.0, 0.0).astype(F32)

    def join_from(src, out):
        for t in (0, 1):
            odd = odd_fine(16, 8, t)
            for m in range(4):
                r, k = src[0, 3 + m, t, 8:24, :], src[1, 3 + m, t, 8:24, :]
                xo_s[32 * m:32 * m + 16, t * LANES:(t + 1) * LANES] = jnp.where(odd, k, r)
                xo_s[32 * m + 16:32 * m + 32, t * LANES:(t + 1) * LANES] = jnp.where(odd, r, k)
        v = jnp.dot(xo_s[...], back, precision=lax.Precision.HIGHEST, preferred_element_type=F32)
        out[...] = v.reshape(out.shape)

    join_from(pf, out_p)
    join_from(rf, out_r)
    for ok, cp in started:
        if ok is None:
            cp().wait_send()
        else:
            @pl.when(ok)
            def _():
                cp().wait_send()


def solution(mesh):
    nx, ny = mesh.shape["gx"], mesh.shape["gy"]

    def local(right_side, phase):
        shape = right_side.shape
        v = lambda *dims: pltpu.VMEM(dims, F32)
        sems = []
        for n in (len(NEAR), len(NEAR), len(WIDE), len(WIDE), len(NEAR), len(WIDE), len(ALONG), len(ALONG), nx - 1, nx - 1, nx):
            sems += [pltpu.SemaphoreType.DMA((n,)), pltpu.SemaphoreType.DMA((n,))]
        fine = (10, 2, 40, LANES)
        return pl.pallas_call(
            functools.partial(kernel, nx, ny),
            out_shape=[jax.ShapeDtypeStruct(shape, F32)] * 2,
            in_specs=[pl.BlockSpec(memory_space=pltpu.HBM)] * 2,
            out_specs=[pl.BlockSpec(memory_space=pltpu.VMEM)] * 2,
            scratch_shapes=[
                v(*shape), pltpu.VMEM(shape, jnp.int32),
                v(2, *fine), v(2, *fine), v(12, *fine), v(2, *fine), v(2, *fine), v(2, *fine), v(2, *fine), v(*fine),
                v(2, *fine), v(3, 10, 32, LANES), v(3, 5, 24, LANES),
                v(3, 21, 40, LANES), v(20, 40, LANES), v(12, 10, 40, LANES), v(2, 10, 40, LANES), v(2, 10, 40, LANES),
                v(2, 10, 40, LANES), v(2, 10, 40, LANES), v(10, 40, LANES), v(10, 16, LANES), v(10, 32, LANES),
                v(3, 48, LANES), v(48, LANES), v(16, 3, 48, LANES), v(16, 48, LANES), v(6, 10, 64, LANES),
                v(12, 8, 64, LANES), v(2, 8, 64, LANES), v(2, 8, 64, LANES), v(2, 10, 64, LANES), v(10, 40, LANES),
                v(128, 2 * LANES),
                pltpu.SemaphoreType.DMA((2,)),
            ] + sems,
            compiler_params=pltpu.CompilerParams(
                collective_id=0, has_side_effects=True, vmem_limit_bytes=63 * 2**20
            ),
        )(right_side, phase)

    spec = P("gx", "gy", None)
    return jax.shard_map(local, mesh=mesh, in_specs=(spec, spec), out_specs=(spec, spec), check_vma=False)
```

```python
import functools

import numpy as np

import jax
import jax.numpy as jnp
from jax import lax
from jax.experimental import pallas as pl
from jax.experimental.pallas import tpu as pltpu
from jax.sharding import PartitionSpec as P

F32 = jnp.float32
MESH = pl.DeviceIdType.MESH
LANES = 128
BOTTOM = 8

_L, _D = np.float32(1.0), np.float32(0.1)
W_LL = float(np.float32(2) * _L * _L / (_L + _L))
W_MX = float(np.float32(2) * _L * _D / (_L + _D))
W_DD = float(np.float32(2) * _D * _D / (_D + _D))

REACH = 5
NEAR = [(-1, 0), (1, 0), (-1, -1), (1, -1), (-1, 1), (1, 1), (0, -1), (0, 1)]
FAR = [(dx, dy) for dx in (-2, 2) for dy in (-1, 0, 1)]
WIDE = NEAR + FAR
ALONG = [d * s for d in range(REACH, 0, -1) for s in (1, -1)]


def ring_order(n):
    side = 4
    return sorted(range(1, n), key=lambda d: -(min(d % side, side - d % side) + min(d // side, side - d // side)))


def rot(v, shift):
    return pltpu.roll(v, shift, 1)


def span(step, own, size, take):
    if step == 0:
        return own, size
    if isinstance(take, tuple):
        take = take[0] if step < 0 else take[1]
    if step > 0:
        return own + size - take, take
    return own, take


def kernel(
    nx, ny,
    rs_hbm, ph_hbm, out_p, out_r,
    rs_in, ph_in,
    ph, rs, wf, sf, df, rdf, pf, pb0, rf, tf, f1o,
    f1, b1, wm, sm, dm, rdm, pm, mb0, rm, em,
    lw, lb, gw, gb, ul, wl, sl, rdl, plow, e1, xo_s,
    in_sem,
    s_ph, r_ph, s_rs, r_rs, s_f1, r_f1, s_b1, r_b1, s_pb, r_pb, s_mb, r_mb,
    s_lw, r_lw, s_lb, r_lb, s_gw, r_gw, s_gb, r_gb, s_re, r_re,
):
    a = lax.axis_index("gx")
    b = lax.axis_index("gy")

    def exists(dx, dy):
        ok = None
        for pos, d, n in ((a, dx, nx), (b, dy, ny)):
            if d:
                one = (pos + d >= 0) if d < 0 else (pos + d < n)
                ok = one if ok is None else jnp.logical_and(ok, one)
        return ok

    started = []

    def copy(src, dst, ssem, rsem, i, dev):
        return pltpu.make_async_remote_copy(
            src_ref=src, dst_ref=dst, send_sem=ssem.at[i], recv_sem=rsem.at[i], device_id=dev, device_id_type=MESH
        )

    def send(steps, refs, ssem, rsem, base=0):
        for i, (dx, dy) in enumerate(steps):
            src, dst = refs(dx, dy)
            cp = functools.partial(copy, src, dst, ssem, rsem, base + i, (a + dx, b + dy))
            ok = exists(dx, dy)

            @pl.when(ok)
            def _():
                cp().start()

            started.append((ok, cp))

    def arrive(steps, refs, ssem, rsem, base=0):
        for i, (dx, dy) in enumerate(steps):
            src, dst = refs(dx, dy)

            @pl.when(exists(-dx, -dy))
            def _():
                copy(src, dst, ssem, rsem, base + i, (a - dx, b - dy)).wait_recv()

    def ring_send(src, dst, ssem, rsem):
        for d in ring_order(nx):
            cp = functools.partial(copy, src, dst((4 - d) % nx), ssem, rsem, d - 1, (lax.rem(a + d, nx), b))
            cp().start()
            started.append((None, cp))

    def relay_refs(i):
        core = lax.rem(b, 2)
        return gw.at[i, :, pl.ds(4 + 16 * core, 20)], gw.at[i, :, pl.ds(24 * core, 20)], (a, b + 1 - 2 * core)

    def relay(i):
        src, dst, dev = relay_refs(i)
        cp = functools.partial(copy, src, dst, s_re, r_re, i, dev)
        cp().start()
        started.append((None, cp))

    def relay_arrive(i):
        src, dst, dev = relay_refs(i)
        core = lax.rem(b, 2)
        copy(src, gw.at[i, :, pl.ds(24 - 24 * core, 20)], s_re, r_re, i, dev).wait_recv()

    def ring_arrive(src, dst, ssem, rsem):
        for d in ring_order(nx):
            copy(src, dst((4 - d) % nx), ssem, rsem, d - 1, (lax.rem(a + nx - d, nx), b)).wait_recv()

    def fine_refs(arr, lead, pairs, rows):
        def refs(dx, dy):
            x0, xn = span(dx, 3, 4, 2 if dy else pairs)
            y0, yn = span(dy, 8, 16, rows - 1 if dx else rows)
            pre = (slice(None),) * lead
            return (
                arr.at[pre + (pl.ds(x0, xn), slice(None), pl.ds(y0, yn))],
                arr.at[pre + (pl.ds(x0 - 4 * dx, xn), slice(None), pl.ds(y0 - 16 * dy, yn))],
            )

        return refs

    def mid_refs(arr, lead, own, size, far, rows, far_corner):
        def refs(dx, dy):
            x0, xn = span(dx, own, size, size if abs(dx) < 2 else far_corner[0] if dy else far)
            y0, yn = span(dy, 16, 8, rows[0] if dx == 0 else rows[1] if abs(dx) < 2 else far_corner[1])
            pre = (slice(None),) * lead
            return (
                arr.at[pre + (pl.ds(x0, xn), pl.ds(y0, yn))],
                arr.at[pre + (pl.ds(x0 - size * dx, xn), pl.ds(y0 - 8 * dy, yn))],
            )

        return refs

    def low_refs(arr, lead):
        def refs(dx, dy):
            pre = (slice(None),) * lead
            return arr.at[pre + (pl.ds(20, 4),)], arr.at[pre + (pl.ds(20 - 4 * dy, 4),)]

        return refs

    ph_refs = fine_refs(ph, 1, 3, 5)
    rs_refs = fine_refs(rs, 1, 2, 4)
    pb_refs = fine_refs(pb0, 0, 3, 5)
    f1_refs = mid_refs(f1, 1, 8, 4, (3, 2), ((7, 6), (6, 5)), (2, 2))
    b1_refs = mid_refs(b1, 0, 8, 4, 2, (6, 5), (1, 1))
    mb_refs = mid_refs(mb0, 0, 4, 2, 2, (7, 6), (1, 2))
    lw_refs = low_refs(lw, 1)
    lb_refs = low_refs(lb, 0)
    gy_steps = [(0, d) for d in ALONG]

    bar = pltpu.get_barrier_semaphore()
    count = jnp.int32(nx - 1)
    for dx, dy in [(dx, dy) for dx, dy in WIDE if dy] + [(0, d) for d in ALONG if abs(d) > 1]:
        ok = exists(dx, dy)

        @pl.when(ok)
        def _():
            pl.semaphore_signal(bar, inc=1, device_id=(a + dx, b + dy), device_id_type=MESH)

        count = count + ok.astype(jnp.int32)

    for d in ring_order(nx):
        pl.semaphore_signal(bar, inc=1, device_id=(lax.rem(a + d, nx), b), device_id_type=MESH)
    in_rs = pltpu.make_async_copy(rs_hbm, rs_in, in_sem.at[0])
    in_ph = pltpu.make_async_copy(ph_hbm, ph_in, in_sem.at[1])
    in_ph.start()
    in_rs.start()

    def iota(rows, dim):
        return lax.broadcasted_iota(jnp.int32, (rows, LANES), dim)

    def h1_of(rows):
        return iota(rows, 1) >= 64

    def lane_ok(rows):
        return lax.rem(iota(rows, 1), 64) < 48

    def odd_fine(rows, start, t):
        return lax.rem(iota(rows, 0) + (start + t), 2) == 1

    def odd_mid(rows, start):
        return lax.rem(iota(rows, 0) + start + lax.div(iota(rows, 1), 64), 2) == 1

    def odd_low(rows, start):
        return lax.rem(iota(rows, 0) + start + iota(rows, 1), 2) == 1

    def inverse(v):
        r = pl.reciprocal(v, approx=True)
        r = r * (2.0 - v * r)
        return r * (2.0 - v * r)

    def zero(ref):
        ref[...] = jnp.zeros(ref.shape, F32)

    @pl.when(a == 0)
    def _():
        zero(ph.at[:, 0:3]); zero(rs.at[:, 0:3]); zero(pb0.at[0:3]); zero(f1.at[:, 0:8]); zero(b1.at[0:8]); zero(mb0.at[0:4])

    @pl.when(a == 1)
    def _():
        zero(f1.at[:, 0:4]); zero(b1.at[0:4]); zero(mb0.at[0:2])

    @pl.when(a == nx - 1)
    def _():
        zero(ph.at[:, 7:10]); zero(rs.at[:, 7:10]); zero(pb0.at[7:10])
        zero(f1.at[:, 12:21]); zero(b1.at[12:20]); zero(mb0.at[6:10])

    @pl.when(a == nx - 2)
    def _():
        zero(f1.at[:, 16:21]); zero(b1.at[16:20]); zero(mb0.at[8:10])

    @pl.when(b == 0)
    def _():
        zero(ph.at[:, :, :, 0:8]); zero(rs.at[:, :, :, 0:8]); zero(pb0.at[:, :, 0:8])
        zero(f1.at[:, :, 0:16]); zero(b1.at[:, 0:16]); zero(mb0.at[:, 0:16])

    @pl.when(b == ny - 1)
    def _():
        zero(ph.at[:, :, :, 24:32]); zero(rs.at[:, :, :, 24:32]); zero(pb0.at[:, :, 24:32])
        zero(f1.at[:, :, 24:40]); zero(b1.at[:, 24:40]); zero(mb0.at[:, 24:40])

    for d in ALONG:
        @pl.when(jnp.logical_not(exists(0, d)))
        def _():
            zero(lw.at[:, pl.ds(20 + 4 * d, 4)])
            zero(lb.at[pl.ds(20 + 4 * d, 4)])

    nz = rs_in.shape[2]
    kk = lax.broadcasted_iota(jnp.int32, (nz, 2 * LANES), 0)
    cc = lax.broadcasted_iota(jnp.int32, (nz, 2 * LANES), 1)
    q, hh, tt = lax.rem(cc, 64), lax.rem(lax.div(cc, 64), 2), lax.div(cc, 128)
    perm = jnp.where(jnp.logical_and(kk == 4 * q + 2 * hh + tt, q < 48), 1.0, 0.0).astype(F32)

    def reorder(v, matrix):
        m16 = matrix.astype(jnp.bfloat16)
        total = None
        for _ in range(3):
            part = v.astype(jnp.bfloat16)
            v = v - part.astype(F32)
            dot = jnp.dot(part, m16, preferred_element_type=F32)
            total = dot if total is None else total + dot
        return total

    def split_into(values, dst):
        for t in (0, 1):
            odd = odd_fine(16, 0, t)
            for m in range(4):
                lo = values[32 * m:32 * m + 16, t * LANES:(t + 1) * LANES]
                hi = values[32 * m + 16:32 * m + 32, t * LANES:(t + 1) * LANES]
                dst[0, 3 + m, t, 8:24, :] = jnp.where(odd, hi, lo)
                dst[1, 3 + m, t, 8:24, :] = jnp.where(odd, lo, hi)

    in_ph.wait()
    labels = jnp.where(ph_in[...] == 1, 1.0, 0.0).astype(F32).reshape(128, nz)
    split_into(jnp.dot(labels, perm, preferred_element_type=F32), ph)
    in_rs.wait()
    block = rs_in[...].reshape(128, nz)
    split_into(reorder(block, perm), rs)

    pl.semaphore_wait(bar, count)
    send(NEAR, ph_refs, s_ph, r_ph)
    send(NEAR, rs_refs, s_rs, r_rs)

    def pair_ok(first, m, total):
        g = first + m
        return jnp.logical_and(g >= 0, g < total)

    def inside(rows, start, total, ok):
        g = iota(rows, 0) + (start + jnp.where(ok, 0, -4096))
        return jnp.logical_and(jnp.logical_and(g >= 0, g < total), lane_ok(rows))

    def fine_sides(arr, c, m, t, r0, n, odd, h1):
        o = 1 - c
        xs = arr[o, m, t, pl.ds(r0, n), :]
        lo = arr[o, m - 1, t, pl.ds(r0, n), :]
        hi = arr[o, m + 1, t, pl.ds(r0, n), :]
        xo = jnp.where(odd, hi, lo) if c == 0 else jnp.where(odd, lo, hi)
        ym = arr[o, m, t, pl.ds(r0 - 1, n), :]
        yp = arr[o, m, t, pl.ds(r0 + 1, n), :]
        zs = arr[o, m, 1 - t, pl.ds(r0, n), :]
        if t == 0:
            zo = jnp.where(h1, rot(zs, 64), rot(zs, 65))
        else:
            zo = jnp.where(h1, rot(zs, 63), rot(zs, 64))
        return xs, xo, ym, yp, zs, zo

    R0, RN = 4, 24
    odd24 = [odd_fine(RN, R0, 0), odd_fine(RN, R0, 1)]
    h24 = h1_of(RN)

    arrive(NEAR, ph_refs, s_ph, r_ph)

    def levels(c, m, t):
        dense = ph[c, m, t, pl.ds(R0, RN), :] > 0.5
        return jnp.where(dense, W_DD, W_MX), jnp.where(dense, W_MX, W_LL)

    def own_faces(m, carry):
        fx = fy = fz = None
        for t in (0, 1):
            both = []
            for c in (0, 1):
                on, off = levels(c, m, t)
                side = fine_sides(ph, c, m, t, R0, RN, odd24[t], h24)
                both.append([jnp.where(side[f] > 0.5, on, off) for f in (1, 2, 5)])
            x = jnp.where(odd24[t], both[1][0], both[0][0])
            y = both[0][1] + both[1][1]
            fx = x if fx is None else fx + x
            fy = y if fy is None else fy + y
            if t == 0:
                fz = both[0][2] + both[1][2]
        tf[0, m, 0:RN, :] = fx
        tf[1, m, 0:RN, :] = fy
        tf[2, m, 0:RN, :] = fz
        return carry

    lax.fori_loop(3, 8, own_faces, 0, unroll=True)

    even, oddr = pl.ds(0, 16, stride=2), pl.ds(1, 16, stride=2)

    def mid_faces(i, carry):
        f1o[0, i, 0:16, :] = 0.25 * (tf[0, i + 3, even, :] + tf[0, i + 3, oddr, :])
        f1o[1, i, 0:16, :] = 0.25 * tf[1, i + 3, even, :]
        f1o[2, i, 0:16, :] = 0.25 * (tf[2, i + 3, even, :] + tf[2, i + 3, oddr, :])
        return carry

    lax.fori_loop(0, 5, mid_faces, 0, unroll=True)
    h8 = h1_of(8)
    for i in range(4):
        fx, fxn = f1o[0, i, 2:10, :], f1o[0, i + 1, 2:10, :]
        fy, fyn = f1o[1, i, 2:10, :], f1o[1, i, 3:11, :]
        fz = f1o[2, i, 2:10, :]
        fzn = jnp.where(h8, rot(fz, 63), rot(fz, 64))
        dg = ((((fx + fxn) + fy) + fyn) + fz) + fzn
        for f, w in enumerate((fx, fy, fz)):
            f1[f, 8 + i, 16:24, :] = jnp.where(lane_ok(8), w, rot(dg, 48 - 16 * f))
    send(NEAR, f1_refs, s_f1, r_f1)

    def zsum(v):
        return v + rot(v, 64)

    fx2 = [0.25 * zsum(f1o[0, 2 * i, pl.ds(2, 8, stride=2), :] + f1o[0, 2 * i, pl.ds(3, 8, stride=2), :]) for i in range(3)]
    fy2, fy2n, fz2, fz2n = [], [], [], []
    for i in range(2):
        fy2.append(0.25 * zsum(f1o[1, 2 * i, pl.ds(2, 8, stride=2), :] + f1o[1, 2 * i + 1, pl.ds(2, 8, stride=2), :]))
        fy2n.append(0.25 * zsum(f1o[1, 2 * i, pl.ds(4, 8, stride=2), :] + f1o[1, 2 * i + 1, pl.ds(4, 8, stride=2), :]))
        v = (f1o[2, 2 * i, pl.ds(2, 8, stride=2), :] + f1o[2, 2 * i, pl.ds(3, 8, stride=2), :]) + (
            f1o[2, 2 * i + 1, pl.ds(2, 8, stride=2), :] + f1o[2, 2 * i + 1, pl.ds(3, 8, stride=2), :]
        )
        v = 0.25 * jnp.where(h8, rot(v, 64), v)
        fz2.append(v)
        fz2n.append(rot(v, 127))
    odd8 = odd_low(8, 0)
    dg2 = [((((fx2[i] + fx2[i + 1]) + fy2[i]) + fy2n[i]) + fz2[i]) + fz2n[i] for i in range(2)]
    rd2 = [jnp.where(lane_ok(8), 1.0 / d, 0.0) for d in dg2]

    def red(v):
        return jnp.where(odd8, v[1], v[0])

    def black(v):
        return jnp.where(odd8, v[0], v[1])

    edge_low = jnp.where(a == 0, 0.0, 1.0)
    edge_high = jnp.where(a == nx - 1, 0.0, 1.0)
    xo2 = jnp.where(odd8, fx2[2] * edge_high, fx2[0] * edge_low)
    inv = jnp.where(h8, black(rd2), red(rd2))
    for f, (first, second) in enumerate(((fx2[1], xo2), (red(fy2), red(fy2n)), (red(fz2), red(fz2n)))):
        v = jnp.where(lane_ok(8), jnp.where(h8, second, first), rot(inv, 48 - 16 * f))
        lw[f, 20:24, :] = v[0:4]
    send(gy_steps, lw_refs, s_lw, r_lw)

    def fine_weights(m, carry):
        valid = inside(RN, 16 * b - 8 + R0, 16 * ny, pair_ok(4 * a - 3, m, 4 * nx))
        for t in (0, 1):
            for c in (0, 1):
                on, off = levels(c, m, t)
                side = fine_sides(ph, c, m, t, R0, RN, odd24[t], h24)
                many = ((((side[0] + side[1]) + side[2]) + side[3]) + side[4]) + side[5]
                dg = 6.0 * off + many * (on - off)
                rd = jnp.where(valid, inverse(dg), 0.0)
                won, woff = on * rd, off * rd
                for f in range(6):
                    wf[6 * c + f, m, t, pl.ds(R0, RN), :] = jnp.where(side[f] > 0.5, won, woff)
                df[c, m, t, pl.ds(R0, RN), :] = dg
                rdf[c, m, t, pl.ds(R0, RN), :] = rd
        return carry

    lax.fori_loop(1, 9, fine_weights, 0, unroll=True)

    def fine_nb(c, m, t, r0, n, odd, h1):
        v = fine_sides(pf, c, m, t, r0, n, odd, h1)
        total = wf[6 * c, m, t, pl.ds(r0, n), :] * v[0]
        for f in range(1, 6):
            total = total + wf[6 * c + f, m, t, pl.ds(r0, n), :] * v[f]
        return total

    def fine_half(c, m0, m1, r0, n):
        odd = [odd_fine(n, r0, 0), odd_fine(n, r0, 1)]
        h1 = h1_of(n)

        def body(m, carry):
            for t in (0, 1):
                nb = fine_nb(c, m, t, r0, n, odd[t], h1)
                pf[c, m, t, pl.ds(r0, n), :] = sf[c, m, t, pl.ds(r0, n), :] + nb
            return carry

        lax.fori_loop(m0, m1, body, 0, unroll=True)

    def fine_last(r0, n):
        odd = [odd_fine(n, r0, 0), odd_fine(n, r0, 1)]
        h1 = h1_of(n)

        def body(m, carry):
            for t in (0, 1):
                win = pl.ds(r0, n)
                nb = fine_nb(1, m, t, r0, n, odd[t], h1)
                fresh = sf[1, m, t, win, :] + nb
                pf[1, m, t, win, :] = fresh
                rf[1, m, t, win, :] = rs[1, m, t, win, :] - df[1, m, t, win, :] * (fresh - nb)
            return carry

        lax.fori_loop(2, 8, body, 0, unroll=True)

    def fine_red_residual():
        odd = [odd_fine(16, 8, 0), odd_fine(16, 8, 1)]
        h1 = h1_of(16)

        def body(m, carry):
            for t in (0, 1):
                win = pl.ds(8, 16)
                nb = fine_nb(0, m, t, 8, 16, odd[t], h1)
                rf[0, m, t, win, :] = rs[0, m, t, win, :] - df[0, m, t, win, :] * (pf[0, m, t, win, :] - nb)
            return carry

        lax.fori_loop(3, 7, body, 0, unroll=True)

    arrive(NEAR, rs_refs, s_rs, r_rs)

    def fine_source(m, carry):
        win = pl.ds(R0, RN)
        for t in (0, 1):
            first = rs[0, m, t, win, :] * rdf[0, m, t, win, :]
            sf[0, m, t, win, :] = first
            pf[0, m, t, win, :] = first
            sf[1, m, t, win, :] = rs[1, m, t, win, :] * rdf[1, m, t, win, :]
        return carry

    lax.fori_loop(1, 9, fine_source, 0, unroll=True)
    fine_half(1, 1, 9, 4, 24)
    fine_half(0, 2, 8, 6, 24)
    fine_last(7, 24)
    fine_red_residual()

    def restrict_fine(m, carry):
        v = (rf[0, m, 0, 8:24, :] + rf[1, m, 0, 8:24, :]) + (rf[0, m, 1, 8:24, :] + rf[1, m, 1, 8:24, :])
        rm[m, 0:16, :] = v
        b1[m + 5, 16:24, :] = 0.125 * (rm[m, pl.ds(0, 8, stride=2), :] + rm[m, pl.ds(1, 8, stride=2), :])
        return carry

    lax.fori_loop(3, 7, restrict_fine, 0, unroll=True)
    send(WIDE, b1_refs, s_b1, r_b1)

    def keep_black(m, carry):
        for t in (0, 1):
            pb0[m, t, 8:24, :] = pf[1, m, t, 8:24, :]
        return carry

    lax.fori_loop(3, 7, keep_black, 0, unroll=True)
    send(NEAR, pb_refs, s_pb, r_pb)
    send(FAR, f1_refs, s_f1, r_f1, len(NEAR))

    def mid_weights(m0, m1, r0, n, top):
        odd, h1 = odd_mid(n, r0), h1_of(n)
        win, nxt = pl.ds(r0, n), pl.ds(r0 + 1, n)
        q = lax.rem(iota(n, 1), 64)
        q16, q32 = q < 16, q < 32

        def body(m, carry):
            valid = inside(n, 8 * b - 16 + r0, 8 * ny, pair_ok(2 * a - 4, m, 2 * nx))
            e0, e1_ = 2 * m, 2 * m + 1
            fx0, fx1, fx2_ = f1[0, e0, win, :], f1[0, e1_, win, :], f1[0, jnp.minimum(e1_ + 1, top), win, :]
            ym = [f1[1, e, win, :] for e in (e0, e1_)]
            yp = [f1[1, e, nxt, :] for e in (e0, e1_)]
            fz = [f1[2, e, win, :] for e in (e0, e1_)]
            zs = [jnp.where(h1, v, rot(v, 64)) for v in fz]
            zo = [jnp.where(h1, rot(v, 63), v) for v in fz]
            dg = [
                jnp.where(q16, rot(f1[0, e, win, :], 80), jnp.where(q32, rot(f1[1, e, win, :], 96), rot(f1[2, e, win, :], 112)))
                for e in (e0, e1_)
            ]
            for c in (0, 1):
                def pick(v):
                    return jnp.where(odd, v[1 - c], v[c])

                xo = jnp.where(odd, fx2_, fx0) if c == 0 else jnp.where(odd, fx0, fx2_)
                d = pick(dg)
                rd = jnp.where(valid, 1.0 / d, 0.0)
                for f, w in enumerate((fx1, xo, pick(ym), pick(yp), pick(zs), pick(zo))):
                    wm[6 * c + f, m, win, :] = w * rd
                dm[c, m, win, :] = d
                rdm[c, m, win, :] = rd
            return carry

        lax.fori_loop(m0, m1, body, 0, unroll=True)

    def mid_source(m0, m1, r0, n, start):
        odd = odd_mid(n, r0)
        win = pl.ds(r0, n)

        def body(m, carry):
            lo, hi = b1[2 * m, win, :], b1[2 * m + 1, win, :]
            first = 4.0 * jnp.where(odd, hi, lo) * rdm[0, m, win, :]
            sm[0, m, win, :] = first
            if start:
                pm[0, m, win, :] = first
            sm[1, m, win, :] = 4.0 * jnp.where(odd, lo, hi) * rdm[1, m, win, :]
            return carry

        lax.fori_loop(m0, m1, body, 0, unroll=True)

    def mid_nb(c, m, r0, n, odd, h1):
        o = 1 - c
        win = pl.ds(r0, n)
        xs, lo, hi = pm[o, m, win, :], pm[o, m - 1, win, :], pm[o, m + 1, win, :]
        xo = jnp.where(odd, hi, lo) if c == 0 else jnp.where(odd, lo, hi)
        zo = jnp.where(h1, rot(xs, 63), rot(xs, 65))
        total = wm[6 * c, m, win, :] * xs
        total = total + wm[6 * c + 1, m, win, :] * xo
        total = total + wm[6 * c + 2, m, win, :] * pm[o, m, pl.ds(r0 - 1, n), :]
        total = total + wm[6 * c + 3, m, win, :] * pm[o, m, pl.ds(r0 + 1, n), :]
        total = total + wm[6 * c + 4, m, win, :] * rot(xs, 64)
        return total + wm[6 * c + 5, m, win, :] * zo

    def mid_half(c, m0, m1, r0, n):
        odd, h1 = odd_mid(n, r0), h1_of(n)

        def body(m, carry):
            win = pl.ds(r0, n)
            pm[c, m, win, :] = sm[c, m, win, :] + mid_nb(c, m, r0, n, odd, h1)
            return carry

        lax.fori_loop(m0, m1, body, 0, unroll=True)

    arrive(NEAR, f1_refs, s_f1, r_f1)
    mid_weights(2, 8, 12, 16, 15)
    arrive(gy_steps, lw_refs, s_lw, r_lw)
    half_rows = pl.ds(20 * lax.rem(b, 2), 24)
    ring_send(lw.at[:, half_rows], lambda i: gw.at[i, :, half_rows], s_gw, r_gw)
    arrive(NEAR, b1_refs, s_b1, r_b1)
    mid_source(2, 8, 12, 16, True)
    mid_half(1, 2, 8, 13, 16)
    mid_half(0, 3, 7, 14, 16)
    mid_half(1, 3, 7, 15, 16)

    odd_own, h_own = odd_mid(8, 16), h1_of(8)
    own = pl.ds(16, 8)
    planes = []
    for m in (4, 5):
        lo, hi = b1[2 * m, own, :], b1[2 * m + 1, own, :]
        total = None
        for c in (0, 1):
            src = jnp.where(odd_own, hi, lo) if c == 0 else jnp.where(odd_own, lo, hi)
            nb = mid_nb(c, m, 16, 8, odd_own, h_own)
            res = src - dm[c, m, own, :] * (pm[c, m, own, :] - nb) * 0.25
            total = res if total is None else total + res
        rm[m, 0:8, :] = total
        rm[m, 8:16, :] = total
        planes.append(0.125 * zsum(rm[m, pl.ds(0, 8, stride=2), :] + rm[m, pl.ds(1, 8, stride=2), :]))
    lb[20:24, :] = jnp.where(h8, black(planes), red(planes))[0:4]
    send(gy_steps, lb_refs, s_lb, r_lb)
    for m in (4, 5):
        mb0[m, own, :] = pm[1, m, own, :]
    send(WIDE, mb_refs, s_mb, r_mb)

    arrive(FAR, f1_refs, s_f1, r_f1, len(NEAR))
    mid_weights(1, 9, 8, 24, 18)
    arrive(FAR, b1_refs, s_b1, r_b1, len(NEAR))
    mid_source(1, 9, 8, 24, False)

    arrive(gy_steps, lb_refs, s_lb, r_lb)
    ring_send(lb.at[0:44], lambda i: gb.at[i, 0:44], s_gb, r_gb)
    gw[4, :, 0:44] = lw[:, 0:44]
    gb[4, 0:44] = lb[0:44]

    LR = 48
    h48 = h1_of(LR)
    odd48 = odd_low(LR, 0)
    q48 = lax.rem(iota(LR, 1), 64)
    lwin = pl.ds(8, LR)

    def fold(lo, hi, half):
        if half == 0:
            return jnp.where(h48, rot(hi, 64), lo)
        return jnp.where(h48, hi, rot(lo, 64))

    ring_arrive(lw.at[:, half_rows], lambda i: gw.at[i, :, half_rows], s_gw, r_gw)
    for i in range(nx):
        if i != 4:
            relay(i)
    for i in range(nx):
        if i != 4:
            relay_arrive(i)

    def low_weights(s, carry):
        u = [fold(gw[s, f // 2], gw[s + 8, f // 2], f % 2) for f in range(6)]
        for c in (0, 1):
            third = jnp.where(q48 < 16, rot(u[c], 80), jnp.where(q48 < 32, rot(u[2 + c], 96), rot(u[4 + c], 112)))
            rdl[c, s, lwin, :] = jnp.where(q48 < 48, third, 0.0)
        rd = rdl[0, s, lwin, :]
        for f in range(6):
            ul[f, s + 1, lwin, :] = u[f]
            wl[f, s, lwin, :] = u[f] * rd
        return carry

    lax.fori_loop(0, 8, low_weights, 0, unroll=True)
    ul[1, 0, lwin, :] = rot(ul[1, 8, lwin, :], 64)
    ul[1, 9, lwin, :] = rot(ul[1, 1, lwin, :], 64)

    def low_black(s, carry):
        rd = rdl[1, s, lwin, :]
        wl[6, s, lwin, :] = ul[0, s + 1, lwin, :] * rd
        wl[7, s, lwin, :] = jnp.where(odd48, ul[1, s, lwin, :], ul[1, s + 2, lwin, :]) * rd
        wl[8, s, lwin, :] = ul[3, s + 1, pl.ds(7, LR), :] * rd
        wl[9, s, lwin, :] = ul[2, s + 1, pl.ds(9, LR), :] * rd
        wl[10, s, lwin, :] = rot(ul[5, s + 1, lwin, :], 1) * rd
        wl[11, s, lwin, :] = rot(ul[4, s + 1, lwin, :], 127) * rd
        return carry

    lax.fori_loop(0, 8, low_black, 0, unroll=True)

    ring_arrive(lb.at[0:44], lambda i: gb.at[i, 0:44], s_gb, r_gb)

    def low_source(s, carry):
        lo, hi = gb[s], gb[s + 8]
        first = 16.0 * fold(lo, hi, 0) * rdl[0, s, lwin, :]
        sl[0, s, lwin, :] = first
        plow[0, s + 1, lwin, :] = first
        sl[1, s, lwin, :] = 16.0 * fold(lo, hi, 1) * rdl[1, s, lwin, :]
        return carry

    lax.fori_loop(0, 8, low_source, 0, unroll=True)

    def low_ghosts(c, r0, n):
        win = pl.ds(r0, n)
        plow[c, 0, win, :] = rot(plow[c, 8, win, :], 64)
        plow[c, 9, win, :] = rot(plow[c, 1, win, :], 64)

    low_ghosts(0, 8, LR)
    for half in range(2, 2 * BOTTOM + 1):
        c = (half - 1) % 2
        reach = 4 + 2 * BOTTOM - half
        r0, n = 8 + 20 - reach, 8 * ((4 + 2 * reach + 7) // 8)
        odd = odd_low(n, r0)

        def low_body(s, carry, c=c, r0=r0, n=n, odd=odd):
            o = 1 - c
            win = pl.ds(r0, n)
            xs, lo, hi = plow[o, s + 1, win, :], plow[o, s, win, :], plow[o, s + 2, win, :]
            xo = jnp.where(odd, hi, lo) if c == 0 else jnp.where(odd, lo, hi)
            total = sl[c, s, win, :] + wl[6 * c, s, win, :] * xs
            total = total + wl[6 * c + 1, s, win, :] * xo
            total = total + wl[6 * c + 2, s, win, :] * plow[o, s + 1, pl.ds(r0 - 1, n), :]
            total = total + wl[6 * c + 3, s, win, :] * plow[o, s + 1, pl.ds(r0 + 1, n), :]
            total = total + wl[6 * c + 4, s, win, :] * rot(xs, 1)
            plow[c, s + 1, win, :] = total + wl[6 * c + 5, s, win, :] * rot(xs, 127)
            return carry

        side = (reach + 1) // 2
        if side <= 3:
            lax.fori_loop(4 - side, 5 + side, low_body, 0, unroll=True)
        else:
            lax.fori_loop(0, 8, low_body, 0, unroll=True)
            low_ghosts(c, r0, n)

    arrive(WIDE, mb_refs, s_mb, r_mb)
    odd16, h16 = odd_low(16, 0), h1_of(16)
    rows24 = pl.ds(8, 24)

    def mid_correct(s, carry):
        red_, black_ = plow[0, s + 3, pl.ds(24, 16), :], plow[1, s + 3, pl.ds(24, 16), :]
        for e in (0, 1):
            v = jnp.where(odd16, black_, red_) if e == 0 else jnp.where(odd16, red_, black_)
            v = jnp.where(h16, rot(v, 64), v)
            em[2 * s + e, pl.ds(0, 16, stride=2), :] = v
            em[2 * s + e, pl.ds(1, 16, stride=2), :] = v
            m = 2 * s + e
            add = em[m, 0:24, :] * jnp.where(pair_ok(2 * a - 4, m, 2 * nx), 1.0, 0.0)
            pm[1, m, rows24, :] = mb0[m, rows24, :] + add
        return carry

    lax.fori_loop(0, 5, mid_correct, 0, unroll=True)
    mid_half(0, 1, 9, 10, 24)
    mid_half(1, 1, 9, 11, 24)
    mid_half(0, 2, 8, 12, 16)
    mid_half(1, 2, 8, 13, 16)

    arrive(NEAR, pb_refs, s_pb, r_pb)
    odd_c = odd_mid(16, 13)

    for m in range(10):
        n, e = (m + 5) // 2, (m + 5) % 2
        red_, black_ = pm[0, n, pl.ds(13, 16), :], pm[1, n, pl.ds(13, 16), :]
        v = jnp.where(odd_c, black_, red_) if e == 0 else jnp.where(odd_c, red_, black_)
        e1[m, pl.ds(2, 16, stride=2), :] = v
        e1[m, pl.ds(3, 16, stride=2), :] = v
        for t in (0, 1):
            pf[1, m, t, pl.ds(3, 32), :] = pb0[m, t, pl.ds(3, 32), :] + e1[m, pl.ds(3, 32), :]

    fine_half(0, 1, 9, 4, 24)
    fine_half(1, 1, 9, 5, 24)
    fine_half(0, 2, 8, 6, 24)
    fine_last(7, 24)
    fine_red_residual()

    kk2 = lax.broadcasted_iota(jnp.int32, (2 * LANES, nz), 1)
    cc2 = lax.broadcasted_iota(jnp.int32, (2 * LANES, nz), 0)
    q2, hh2, tt2 = lax.rem(cc2, 64), lax.rem(lax.div(cc2, 64), 2), lax.div(cc2, 128)
    back = jnp.where(jnp.logical_and(kk2 == 4 * q2 + 2 * hh2 + tt2, q2 < 48), 1.0, 0.0).astype(F32)

    def join_from(src, out):
        for t in (0, 1):
            odd = odd_fine(16, 8, t)
            for m in range(4):
                r, k = src[0, 3 + m, t, 8:24, :], src[1, 3 + m, t, 8:24, :]
                xo_s[32 * m:32 * m + 16, t * LANES:(t + 1) * LANES] = jnp.where(odd, k, r)
                xo_s[32 * m + 16:32 * m + 32, t * LANES:(t + 1) * LANES] = jnp.where(odd, r, k)
        out[...] = reorder(xo_s[...], back).reshape(out.shape)

    join_from(pf, out_p)
    join_from(rf, out_r)
    for ok, cp in started:
        if ok is None:
            cp().wait_send()
        else:
            @pl.when(ok)
            def _():
                cp().wait_send()


def solution(mesh):
    nx, ny = mesh.shape["gx"], mesh.shape["gy"]

    def local(right_side, phase):
        shape = right_side.shape
        v = lambda *dims: pltpu.VMEM(dims, F32)
        sems = []
        for n in (len(NEAR), len(NEAR), len(WIDE), len(WIDE), len(NEAR), len(WIDE), len(ALONG), len(ALONG), nx - 1, nx - 1, nx):
            sems += [pltpu.SemaphoreType.DMA((n,)), pltpu.SemaphoreType.DMA((n,))]
        fine = (10, 2, 40, LANES)
        return pl.pallas_call(
            functools.partial(kernel, nx, ny),
            out_shape=[jax.ShapeDtypeStruct(shape, F32)] * 2,
            in_specs=[pl.BlockSpec(memory_space=pltpu.HBM)] * 2,
            out_specs=[pl.BlockSpec(memory_space=pltpu.VMEM)] * 2,
            scratch_shapes=[
                v(*shape), pltpu.VMEM(shape, jnp.int32),
                v(2, *fine), v(2, *fine), v(12, *fine), v(2, *fine), v(2, *fine), v(2, *fine), v(2, *fine), v(*fine),
                v(2, *fine), v(3, 10, 32, LANES), v(3, 5, 24, LANES),
                v(3, 21, 40, LANES), v(20, 40, LANES), v(12, 10, 40, LANES), v(2, 10, 40, LANES), v(2, 10, 40, LANES),
                v(2, 10, 40, LANES), v(2, 10, 40, LANES), v(10, 40, LANES), v(10, 16, LANES), v(10, 32, LANES),
                v(3, 48, LANES), v(48, LANES), v(16, 3, 48, LANES), v(16, 48, LANES), v(6, 10, 64, LANES),
                v(12, 8, 64, LANES), v(2, 8, 64, LANES), v(2, 8, 64, LANES), v(2, 10, 64, LANES), v(10, 40, LANES),
                v(128, 2 * LANES),
                pltpu.SemaphoreType.DMA((2,)),
            ] + sems,
            compiler_params=pltpu.CompilerParams(
                collective_id=0, has_side_effects=True, vmem_limit_bytes=56262656
            ),
        )(right_side, phase)

    spec = P("gx", "gy", None)
    return jax.shard_map(local, mesh=mesh, in_specs=(spec, spec), out_specs=(spec, spec), check_vma=False)
```

```python
import functools

import numpy as np

import jax
import jax.numpy as jnp
from jax import lax
from jax.experimental import pallas as pl
from jax.experimental.pallas import tpu as pltpu
from jax.sharding import PartitionSpec as P

F32 = jnp.float32
MESH = pl.DeviceIdType.MESH
LANES = 128
BOTTOM = 8
RING = 10

_L, _D = np.float32(1.0), np.float32(0.1)
W_LL = float(np.float32(2) * _L * _L / (_L + _L))
W_MX = float(np.float32(2) * _L * _D / (_L + _D))
W_DD = float(np.float32(2) * _D * _D / (_D + _D))

REACH = 5
NEAR = [(-1, 0), (1, 0), (-1, -1), (1, -1), (-1, 1), (1, 1), (0, -1), (0, 1)]
FAR = [(dx, dy) for dx in (-2, 2) for dy in (-1, 0, 1)]
WIDE = NEAR + FAR
ALONG = [d * s for d in range(REACH, 0, -1) for s in (1, -1)]


def ring_order(n):
    side = 4
    return sorted(range(1, n), key=lambda d: -(min(d % side, side - d % side) + min(d // side, side - d // side)))


def rot(v, shift):
    return pltpu.roll(v, shift, 1)


def span(step, own, size, take):
    if step == 0:
        return own, size
    if isinstance(take, tuple):
        take = take[0] if step < 0 else take[1]
    if step > 0:
        return own + size - take, take
    return own, take


def kernel(
    nx, ny,
    rs_hbm, ph_hbm, out_p, out_r,
    rs_in, ph_in,
    ph, rs, wf, sf, df, rdf, pf, pb0, rf, tf, f1o,
    f1, b1, wm, sm, dm, rdm, pm, mb0, rm, em,
    lw, lb, gw, gb, ul, wl, sl, rdl, plow, e1, xo_s,
    in_sem,
    s_ph, r_ph, s_rs, r_rs, s_f1, r_f1, s_b1, r_b1, s_pb, r_pb, s_mb, r_mb,
    s_lw, r_lw, s_lb, r_lb, s_gw, r_gw, s_gb, r_gb, s_re, r_re,
):
    a = lax.axis_index("gx")
    b = lax.axis_index("gy")

    def exists(dx, dy):
        ok = None
        for pos, d, n in ((a, dx, nx), (b, dy, ny)):
            if d:
                one = (pos + d >= 0) if d < 0 else (pos + d < n)
                ok = one if ok is None else jnp.logical_and(ok, one)
        return ok

    started = []

    def copy(src, dst, ssem, rsem, i, dev):
        return pltpu.make_async_remote_copy(
            src_ref=src, dst_ref=dst, send_sem=ssem.at[i], recv_sem=rsem.at[i], device_id=dev, device_id_type=MESH
        )

    def send(steps, refs, ssem, rsem, base=0):
        for i, (dx, dy) in enumerate(steps):
            src, dst = refs(dx, dy)
            cp = functools.partial(copy, src, dst, ssem, rsem, base + i, (a + dx, b + dy))
            ok = exists(dx, dy)

            @pl.when(ok)
            def _():
                cp().start()

            started.append((ok, cp))

    def arrive(steps, refs, ssem, rsem, base=0):
        for i, (dx, dy) in enumerate(steps):
            src, dst = refs(dx, dy)

            @pl.when(exists(-dx, -dy))
            def _():
                copy(src, dst, ssem, rsem, base + i, (a - dx, b - dy)).wait_recv()

    ring = [dx for d in ring_order(nx) for dx in (d, d - nx) if abs(dx) <= RING]
    core = lax.rem(b, 2)

    def slot(dx):
        return (4 - dx) % nx

    def whole_rows(dx):
        return pl.ds(2 * abs(dx), 44 - 4 * abs(dx))

    def half_rows(dx):
        return pl.ds(2 * abs(dx) + core * (20 - 2 * abs(dx)), 24 - 2 * abs(dx))

    def send_w(dx):
        return copy(lw.at[:, half_rows(dx)], gw.at[slot(dx), :, half_rows(dx)], s_gw, r_gw, dx % nx - 1, (a + dx, b))

    def send_b(dx):
        return copy(lb.at[whole_rows(dx)], gb.at[slot(dx), whole_rows(dx)], s_gb, r_gb, dx % nx - 1, (a + dx, b))

    def relay(dx):
        d, n = 2 * abs(dx), 20 - 2 * abs(dx)
        src, dst = d + 4 + core * (16 - d), d + core * (24 - d)
        return copy(
            gw.at[slot(dx), :, pl.ds(src, n)], gw.at[slot(dx), :, pl.ds(dst, n)], s_re, r_re, dx % nx, (a, b + 1 - 2 * core)
        )

    def relay_comes(dx):
        d, n = 2 * abs(dx), 20 - 2 * abs(dx)
        dst = pl.ds(24 + core * (d - 24), n)
        return copy(
            gw.at[slot(dx), :, dst], gw.at[slot(dx), :, dst], s_re, r_re, dx % nx, (a, b + 1 - 2 * core)
        )

    def ring_send(made):
        for dx in ring:
            @pl.when(exists(dx, 0))
            def _():
                made(dx).start()

            started.append((exists(dx, 0), functools.partial(made, dx)))

    def ring_arrive(made):
        for dx in ring:
            @pl.when(exists(-dx, 0))
            def _():
                made(dx).wait_recv()

    def fine_refs(arr, lead, pairs, rows):
        def refs(dx, dy):
            x0, xn = span(dx, 3, 4, 2 if dy else pairs)
            y0, yn = span(dy, 8, 16, rows - 1 if dx else rows)
            pre = (slice(None),) * lead
            return (
                arr.at[pre + (pl.ds(x0, xn), slice(None), pl.ds(y0, yn))],
                arr.at[pre + (pl.ds(x0 - 4 * dx, xn), slice(None), pl.ds(y0 - 16 * dy, yn))],
            )

        return refs

    def mid_refs(arr, lead, own, size, far, rows, far_corner):
        def refs(dx, dy):
            x0, xn = span(dx, own, size, size if abs(dx) < 2 else far_corner[0] if dy else far)
            y0, yn = span(dy, 16, 8, rows[0] if dx == 0 else rows[1] if abs(dx) < 2 else far_corner[1])
            pre = (slice(None),) * lead
            return (
                arr.at[pre + (pl.ds(x0, xn), pl.ds(y0, yn))],
                arr.at[pre + (pl.ds(x0 - size * dx, xn), pl.ds(y0 - 8 * dy, yn))],
            )

        return refs

    def low_refs(arr, lead):
        def refs(dx, dy):
            pre = (slice(None),) * lead
            return arr.at[pre + (pl.ds(20, 4),)], arr.at[pre + (pl.ds(20 - 4 * dy, 4),)]

        return refs

    ph_refs = fine_refs(ph, 1, 3, 5)
    rs_refs = fine_refs(rs, 1, 2, 4)
    pb_refs = fine_refs(pb0, 0, 3, 5)
    f1_refs = mid_refs(f1, 1, 8, 4, (3, 2), ((7, 6), (6, 5)), (2, 2))
    b1_refs = mid_refs(b1, 0, 8, 4, 2, (6, 5), (1, 1))
    mb_refs = mid_refs(mb0, 0, 4, 2, 2, (7, 6), (1, 2))
    lw_refs = low_refs(lw, 1)
    lb_refs = low_refs(lb, 0)
    gy_steps = [(0, d) for d in ALONG]

    bar = pltpu.get_barrier_semaphore()
    count = jnp.int32(nx - 1)
    for dx, dy in [(dx, dy) for dx, dy in WIDE if dy] + [(0, d) for d in ALONG if abs(d) > 1]:
        ok = exists(dx, dy)

        @pl.when(ok)
        def _():
            pl.semaphore_signal(bar, inc=1, device_id=(a + dx, b + dy), device_id_type=MESH)

        count = count + ok.astype(jnp.int32)

    for d in ring_order(nx):
        pl.semaphore_signal(bar, inc=1, device_id=(lax.rem(a + d, nx), b), device_id_type=MESH)
    in_rs = pltpu.make_async_copy(rs_hbm, rs_in, in_sem.at[0])
    in_ph = pltpu.make_async_copy(ph_hbm, ph_in, in_sem.at[1])
    in_ph.start()
    in_rs.start()

    def iota(rows, dim):
        return lax.broadcasted_iota(jnp.int32, (rows, LANES), dim)

    def h1_of(rows):
        return iota(rows, 1) >= 64

    def lane_ok(rows):
        return lax.rem(iota(rows, 1), 64) < 48

    def odd_fine(rows, start, t):
        return lax.rem(iota(rows, 0) + (start + t), 2) == 1

    def odd_mid(rows, start):
        return lax.rem(iota(rows, 0) + start + lax.div(iota(rows, 1), 64), 2) == 1

    def odd_low(rows, start):
        return lax.rem(iota(rows, 0) + start + iota(rows, 1), 2) == 1

    def inverse(v):
        r = pl.reciprocal(v, approx=True)
        r = r * (2.0 - v * r)
        return r * (2.0 - v * r)

    def zero(ref):
        ref[...] = jnp.zeros(ref.shape, F32)

    @pl.when(a == 0)
    def _():
        zero(ph.at[:, 0:3]); zero(rs.at[:, 0:3]); zero(pb0.at[0:3]); zero(f1.at[:, 0:8]); zero(b1.at[0:8]); zero(mb0.at[0:4])

    @pl.when(a == 1)
    def _():
        zero(f1.at[:, 0:4]); zero(b1.at[0:4]); zero(mb0.at[0:2])

    @pl.when(a == nx - 1)
    def _():
        zero(ph.at[:, 7:10]); zero(rs.at[:, 7:10]); zero(pb0.at[7:10])
        zero(f1.at[:, 12:21]); zero(b1.at[12:20]); zero(mb0.at[6:10])

    @pl.when(a == nx - 2)
    def _():
        zero(f1.at[:, 16:21]); zero(b1.at[16:20]); zero(mb0.at[8:10])

    @pl.when(b == 0)
    def _():
        zero(ph.at[:, :, :, 0:8]); zero(rs.at[:, :, :, 0:8]); zero(pb0.at[:, :, 0:8])
        zero(f1.at[:, :, 0:16]); zero(b1.at[:, 0:16]); zero(mb0.at[:, 0:16])

    @pl.when(b == ny - 1)
    def _():
        zero(ph.at[:, :, :, 24:32]); zero(rs.at[:, :, :, 24:32]); zero(pb0.at[:, :, 24:32])
        zero(f1.at[:, :, 24:40]); zero(b1.at[:, 24:40]); zero(mb0.at[:, 24:40])

    for d in ALONG:
        @pl.when(jnp.logical_not(exists(0, d)))
        def _():
            zero(lw.at[:, pl.ds(20 + 4 * d, 4)])
            zero(lb.at[pl.ds(20 + 4 * d, 4)])

    for dx in list(range(1, nx)) + list(range(-1, -nx, -1)):
        @pl.when(exists(-dx, 0))
        def _():
            if abs(dx) > RING:
                zero(gw.at[slot(dx)])
                zero(gb.at[slot(dx)])
            else:
                for rows in (slice(0, 2 * abs(dx)), slice(44 - 2 * abs(dx), 48)):
                    zero(gw.at[slot(dx), :, rows])
                    zero(gb.at[slot(dx), rows])

    nz = rs_in.shape[2]
    kk = lax.broadcasted_iota(jnp.int32, (nz, 2 * LANES), 0)
    cc = lax.broadcasted_iota(jnp.int32, (nz, 2 * LANES), 1)
    q, hh, tt = lax.rem(cc, 64), lax.rem(lax.div(cc, 64), 2), lax.div(cc, 128)
    perm = jnp.where(jnp.logical_and(kk == 4 * q + 2 * hh + tt, q < 48), 1.0, 0.0).astype(F32)

    def reorder(v, matrix):
        m16 = matrix.astype(jnp.bfloat16)
        total = None
        for _ in range(3):
            part = v.astype(jnp.bfloat16)
            v = v - part.astype(F32)
            dot = jnp.dot(part, m16, preferred_element_type=F32)
            total = dot if total is None else total + dot
        return total

    def split_into(values, dst):
        for t in (0, 1):
            odd = odd_fine(16, 0, t)
            for m in range(4):
                lo = values[32 * m:32 * m + 16, t * LANES:(t + 1) * LANES]
                hi = values[32 * m + 16:32 * m + 32, t * LANES:(t + 1) * LANES]
                dst[0, 3 + m, t, 8:24, :] = jnp.where(odd, hi, lo)
                dst[1, 3 + m, t, 8:24, :] = jnp.where(odd, lo, hi)

    in_ph.wait()
    labels = jnp.where(ph_in[...] == 1, 1.0, 0.0).astype(F32).reshape(128, nz)
    split_into(jnp.dot(labels, perm, preferred_element_type=F32), ph)
    in_rs.wait()
    block = rs_in[...].reshape(128, nz)
    split_into(reorder(block, perm), rs)

    pl.semaphore_wait(bar, count)
    send(NEAR, ph_refs, s_ph, r_ph)
    send(NEAR, rs_refs, s_rs, r_rs)

    def pair_ok(first, m, total):
        g = first + m
        return jnp.logical_and(g >= 0, g < total)

    def inside(rows, start, total, ok):
        g = iota(rows, 0) + (start + jnp.where(ok, 0, -4096))
        return jnp.logical_and(jnp.logical_and(g >= 0, g < total), lane_ok(rows))

    def fine_sides(arr, c, m, t, r0, n, odd, h1):
        o = 1 - c
        xs = arr[o, m, t, pl.ds(r0, n), :]
        lo = arr[o, m - 1, t, pl.ds(r0, n), :]
        hi = arr[o, m + 1, t, pl.ds(r0, n), :]
        xo = jnp.where(odd, hi, lo) if c == 0 else jnp.where(odd, lo, hi)
        ym = arr[o, m, t, pl.ds(r0 - 1, n), :]
        yp = arr[o, m, t, pl.ds(r0 + 1, n), :]
        zs = arr[o, m, 1 - t, pl.ds(r0, n), :]
        if t == 0:
            zo = jnp.where(h1, rot(zs, 64), rot(zs, 65))
        else:
            zo = jnp.where(h1, rot(zs, 63), rot(zs, 64))
        return xs, xo, ym, yp, zs, zo

    R0, RN = 4, 24
    odd24 = [odd_fine(RN, R0, 0), odd_fine(RN, R0, 1)]
    h24 = h1_of(RN)

    arrive(NEAR, ph_refs, s_ph, r_ph)

    def levels(c, m, t):
        dense = ph[c, m, t, pl.ds(R0, RN), :] > 0.5
        return jnp.where(dense, W_DD, W_MX), jnp.where(dense, W_MX, W_LL)

    def own_faces(m, carry):
        fx = fy = fz = None
        for t in (0, 1):
            both = []
            for c in (0, 1):
                on, off = levels(c, m, t)
                side = fine_sides(ph, c, m, t, R0, RN, odd24[t], h24)
                both.append([jnp.where(side[f] > 0.5, on, off) for f in (1, 2, 5)])
            x = jnp.where(odd24[t], both[1][0], both[0][0])
            y = both[0][1] + both[1][1]
            fx = x if fx is None else fx + x
            fy = y if fy is None else fy + y
            if t == 0:
                fz = both[0][2] + both[1][2]
        tf[0, m, 0:RN, :] = fx
        tf[1, m, 0:RN, :] = fy
        tf[2, m, 0:RN, :] = fz
        return carry

    lax.fori_loop(3, 8, own_faces, 0, unroll=True)

    even, oddr = pl.ds(0, 16, stride=2), pl.ds(1, 16, stride=2)

    def mid_faces(i, carry):
        f1o[0, i, 0:16, :] = 0.25 * (tf[0, i + 3, even, :] + tf[0, i + 3, oddr, :])
        f1o[1, i, 0:16, :] = 0.25 * tf[1, i + 3, even, :]
        f1o[2, i, 0:16, :] = 0.25 * (tf[2, i + 3, even, :] + tf[2, i + 3, oddr, :])
        return carry

    lax.fori_loop(0, 5, mid_faces, 0, unroll=True)
    h8 = h1_of(8)
    for i in range(4):
        fx, fxn = f1o[0, i, 2:10, :], f1o[0, i + 1, 2:10, :]
        fy, fyn = f1o[1, i, 2:10, :], f1o[1, i, 3:11, :]
        fz = f1o[2, i, 2:10, :]
        fzn = jnp.where(h8, rot(fz, 63), rot(fz, 64))
        dg = ((((fx + fxn) + fy) + fyn) + fz) + fzn
        for f, w in enumerate((fx, fy, fz)):
            f1[f, 8 + i, 16:24, :] = jnp.where(lane_ok(8), w, rot(dg, 48 - 16 * f))
    send(NEAR, f1_refs, s_f1, r_f1)

    def zsum(v):
        return v + rot(v, 64)

    fx2 = [0.25 * zsum(f1o[0, 2 * i, pl.ds(2, 8, stride=2), :] + f1o[0, 2 * i, pl.ds(3, 8, stride=2), :]) for i in range(3)]
    fy2, fy2n, fz2, fz2n = [], [], [], []
    for i in range(2):
        fy2.append(0.25 * zsum(f1o[1, 2 * i, pl.ds(2, 8, stride=2), :] + f1o[1, 2 * i + 1, pl.ds(2, 8, stride=2), :]))
        fy2n.append(0.25 * zsum(f1o[1, 2 * i, pl.ds(4, 8, stride=2), :] + f1o[1, 2 * i + 1, pl.ds(4, 8, stride=2), :]))
        v = (f1o[2, 2 * i, pl.ds(2, 8, stride=2), :] + f1o[2, 2 * i, pl.ds(3, 8, stride=2), :]) + (
            f1o[2, 2 * i + 1, pl.ds(2, 8, stride=2), :] + f1o[2, 2 * i + 1, pl.ds(3, 8, stride=2), :]
        )
        v = 0.25 * jnp.where(h8, rot(v, 64), v)
        fz2.append(v)
        fz2n.append(rot(v, 127))
    odd8 = odd_low(8, 0)
    dg2 = [((((fx2[i] + fx2[i + 1]) + fy2[i]) + fy2n[i]) + fz2[i]) + fz2n[i] for i in range(2)]
    rd2 = [jnp.where(lane_ok(8), 1.0 / d, 0.0) for d in dg2]

    def red(v):
        return jnp.where(odd8, v[1], v[0])

    def black(v):
        return jnp.where(odd8, v[0], v[1])

    edge_low = jnp.where(a == 0, 0.0, 1.0)
    edge_high = jnp.where(a == nx - 1, 0.0, 1.0)
    xo2 = jnp.where(odd8, fx2[2] * edge_high, fx2[0] * edge_low)
    inv = jnp.where(h8, black(rd2), red(rd2))
    for f, (first, second) in enumerate(((fx2[1], xo2), (red(fy2), red(fy2n)), (red(fz2), red(fz2n)))):
        v = jnp.where(lane_ok(8), jnp.where(h8, second, first), rot(inv, 48 - 16 * f))
        lw[f, 20:24, :] = v[0:4]
    send(gy_steps, lw_refs, s_lw, r_lw)

    def fine_weights(m, carry):
        valid = inside(RN, 16 * b - 8 + R0, 16 * ny, pair_ok(4 * a - 3, m, 4 * nx))
        for t in (0, 1):
            for c in (0, 1):
                on, off = levels(c, m, t)
                side = fine_sides(ph, c, m, t, R0, RN, odd24[t], h24)
                many = ((((side[0] + side[1]) + side[2]) + side[3]) + side[4]) + side[5]
                dg = 6.0 * off + many * (on - off)
                rd = jnp.where(valid, inverse(dg), 0.0)
                won, woff = on * rd, off * rd
                for f in range(6):
                    wf[6 * c + f, m, t, pl.ds(R0, RN), :] = jnp.where(side[f] > 0.5, won, woff)
                df[c, m, t, pl.ds(R0, RN), :] = dg
                rdf[c, m, t, pl.ds(R0, RN), :] = rd
        return carry

    lax.fori_loop(1, 9, fine_weights, 0, unroll=True)

    def fine_nb(c, m, t, r0, n, odd, h1):
        v = fine_sides(pf, c, m, t, r0, n, odd, h1)
        total = wf[6 * c, m, t, pl.ds(r0, n), :] * v[0]
        for f in range(1, 6):
            total = total + wf[6 * c + f, m, t, pl.ds(r0, n), :] * v[f]
        return total

    def fine_half(c, m0, m1, r0, n):
        odd = [odd_fine(n, r0, 0), odd_fine(n, r0, 1)]
        h1 = h1_of(n)

        def body(m, carry):
            for t in (0, 1):
                nb = fine_nb(c, m, t, r0, n, odd[t], h1)
                pf[c, m, t, pl.ds(r0, n), :] = sf[c, m, t, pl.ds(r0, n), :] + nb
            return carry

        lax.fori_loop(m0, m1, body, 0, unroll=True)

    def fine_last(r0, n):
        odd = [odd_fine(n, r0, 0), odd_fine(n, r0, 1)]
        h1 = h1_of(n)

        def body(m, carry):
            for t in (0, 1):
                win = pl.ds(r0, n)
                nb = fine_nb(1, m, t, r0, n, odd[t], h1)
                fresh = sf[1, m, t, win, :] + nb
                pf[1, m, t, win, :] = fresh
                rf[1, m, t, win, :] = rs[1, m, t, win, :] - df[1, m, t, win, :] * (fresh - nb)
            return carry

        lax.fori_loop(2, 8, body, 0, unroll=True)

    def fine_red_residual():
        odd = [odd_fine(16, 8, 0), odd_fine(16, 8, 1)]
        h1 = h1_of(16)

        def body(m, carry):
            for t in (0, 1):
                win = pl.ds(8, 16)
                nb = fine_nb(0, m, t, 8, 16, odd[t], h1)
                rf[0, m, t, win, :] = rs[0, m, t, win, :] - df[0, m, t, win, :] * (pf[0, m, t, win, :] - nb)
            return carry

        lax.fori_loop(3, 7, body, 0, unroll=True)

    arrive(NEAR, rs_refs, s_rs, r_rs)

    def fine_source(m, carry):
        win = pl.ds(R0, RN)
        for t in (0, 1):
            first = rs[0, m, t, win, :] * rdf[0, m, t, win, :]
            sf[0, m, t, win, :] = first
            pf[0, m, t, win, :] = first
            sf[1, m, t, win, :] = rs[1, m, t, win, :] * rdf[1, m, t, win, :]
        return carry

    lax.fori_loop(1, 9, fine_source, 0, unroll=True)
    fine_half(1, 1, 9, 4, 24)
    fine_half(0, 2, 8, 6, 24)
    fine_last(7, 24)
    fine_red_residual()

    def restrict_fine(m, carry):
        v = (rf[0, m, 0, 8:24, :] + rf[1, m, 0, 8:24, :]) + (rf[0, m, 1, 8:24, :] + rf[1, m, 1, 8:24, :])
        rm[m, 0:16, :] = v
        b1[m + 5, 16:24, :] = 0.125 * (rm[m, pl.ds(0, 8, stride=2), :] + rm[m, pl.ds(1, 8, stride=2), :])
        return carry

    lax.fori_loop(3, 7, restrict_fine, 0, unroll=True)
    send(WIDE, b1_refs, s_b1, r_b1)

    def keep_black(m, carry):
        for t in (0, 1):
            pb0[m, t, 8:24, :] = pf[1, m, t, 8:24, :]
        return carry

    lax.fori_loop(3, 7, keep_black, 0, unroll=True)
    send(NEAR, pb_refs, s_pb, r_pb)
    send(FAR, f1_refs, s_f1, r_f1, len(NEAR))

    def mid_weights(m0, m1, r0, n, top):
        odd, h1 = odd_mid(n, r0), h1_of(n)
        win, nxt = pl.ds(r0, n), pl.ds(r0 + 1, n)
        q = lax.rem(iota(n, 1), 64)
        q16, q32 = q < 16, q < 32

        def body(m, carry):
            valid = inside(n, 8 * b - 16 + r0, 8 * ny, pair_ok(2 * a - 4, m, 2 * nx))
            e0, e1_ = 2 * m, 2 * m + 1
            fx0, fx1, fx2_ = f1[0, e0, win, :], f1[0, e1_, win, :], f1[0, jnp.minimum(e1_ + 1, top), win, :]
            ym = [f1[1, e, win, :] for e in (e0, e1_)]
            yp = [f1[1, e, nxt, :] for e in (e0, e1_)]
            fz = [f1[2, e, win, :] for e in (e0, e1_)]
            zs = [jnp.where(h1, v, rot(v, 64)) for v in fz]
            zo = [jnp.where(h1, rot(v, 63), v) for v in fz]
            dg = [
                jnp.where(q16, rot(f1[0, e, win, :], 80), jnp.where(q32, rot(f1[1, e, win, :], 96), rot(f1[2, e, win, :], 112)))
                for e in (e0, e1_)
            ]
            for c in (0, 1):
                def pick(v):
                    return jnp.where(odd, v[1 - c], v[c])

                xo = jnp.where(odd, fx2_, fx0) if c == 0 else jnp.where(odd, fx0, fx2_)
                d = pick(dg)
                rd = jnp.where(valid, 1.0 / d, 0.0)
                for f, w in enumerate((fx1, xo, pick(ym), pick(yp), pick(zs), pick(zo))):
                    wm[6 * c + f, m, win, :] = w * rd
                dm[c, m, win, :] = d
                rdm[c, m, win, :] = rd
            return carry

        lax.fori_loop(m0, m1, body, 0, unroll=True)

    def mid_source(m0, m1, r0, n, start):
        odd = odd_mid(n, r0)
        win = pl.ds(r0, n)

        def body(m, carry):
            lo, hi = b1[2 * m, win, :], b1[2 * m + 1, win, :]
            first = 4.0 * jnp.where(odd, hi, lo) * rdm[0, m, win, :]
            sm[0, m, win, :] = first
            if start:
                pm[0, m, win, :] = first
            sm[1, m, win, :] = 4.0 * jnp.where(odd, lo, hi) * rdm[1, m, win, :]
            return carry

        lax.fori_loop(m0, m1, body, 0, unroll=True)

    def mid_nb(c, m, r0, n, odd, h1):
        o = 1 - c
        win = pl.ds(r0, n)
        xs, lo, hi = pm[o, m, win, :], pm[o, m - 1, win, :], pm[o, m + 1, win, :]
        xo = jnp.where(odd, hi, lo) if c == 0 else jnp.where(odd, lo, hi)
        zo = jnp.where(h1, rot(xs, 63), rot(xs, 65))
        total = wm[6 * c, m, win, :] * xs
        total = total + wm[6 * c + 1, m, win, :] * xo
        total = total + wm[6 * c + 2, m, win, :] * pm[o, m, pl.ds(r0 - 1, n), :]
        total = total + wm[6 * c + 3, m, win, :] * pm[o, m, pl.ds(r0 + 1, n), :]
        total = total + wm[6 * c + 4, m, win, :] * rot(xs, 64)
        return total + wm[6 * c + 5, m, win, :] * zo

    def mid_half(c, m0, m1, r0, n):
        odd, h1 = odd_mid(n, r0), h1_of(n)

        def body(m, carry):
            win = pl.ds(r0, n)
            pm[c, m, win, :] = sm[c, m, win, :] + mid_nb(c, m, r0, n, odd, h1)
            return carry

        lax.fori_loop(m0, m1, body, 0, unroll=True)

    arrive(NEAR, f1_refs, s_f1, r_f1)
    mid_weights(2, 8, 12, 16, 15)
    arrive(gy_steps, lw_refs, s_lw, r_lw)
    ring_send(send_w)
    arrive(NEAR, b1_refs, s_b1, r_b1)
    mid_source(2, 8, 12, 16, True)
    mid_half(1, 2, 8, 13, 16)
    mid_half(0, 3, 7, 14, 16)
    mid_half(1, 3, 7, 15, 16)

    odd_own, h_own = odd_mid(8, 16), h1_of(8)
    own = pl.ds(16, 8)
    planes = []
    for m in (4, 5):
        lo, hi = b1[2 * m, own, :], b1[2 * m + 1, own, :]
        total = None
        for c in (0, 1):
            src = jnp.where(odd_own, hi, lo) if c == 0 else jnp.where(odd_own, lo, hi)
            nb = mid_nb(c, m, 16, 8, odd_own, h_own)
            res = src - dm[c, m, own, :] * (pm[c, m, own, :] - nb) * 0.25
            total = res if total is None else total + res
        rm[m, 0:8, :] = total
        rm[m, 8:16, :] = total
        planes.append(0.125 * zsum(rm[m, pl.ds(0, 8, stride=2), :] + rm[m, pl.ds(1, 8, stride=2), :]))
    lb[20:24, :] = jnp.where(h8, black(planes), red(planes))[0:4]
    send(gy_steps, lb_refs, s_lb, r_lb)
    for m in (4, 5):
        mb0[m, own, :] = pm[1, m, own, :]
    send(WIDE, mb_refs, s_mb, r_mb)

    arrive(FAR, f1_refs, s_f1, r_f1, len(NEAR))
    mid_weights(1, 9, 8, 24, 18)
    arrive(FAR, b1_refs, s_b1, r_b1, len(NEAR))
    mid_source(1, 9, 8, 24, False)

    arrive(gy_steps, lb_refs, s_lb, r_lb)
    ring_send(send_b)
    gw[4, :, 0:44] = lw[:, 0:44]
    gb[4, 0:44] = lb[0:44]

    LR = 48
    h48 = h1_of(LR)
    odd48 = odd_low(LR, 0)
    q48 = lax.rem(iota(LR, 1), 64)
    lwin = pl.ds(8, LR)

    def fold(lo, hi, half):
        if half == 0:
            return jnp.where(h48, rot(hi, 64), lo)
        return jnp.where(h48, hi, rot(lo, 64))

    ring_arrive(send_w)
    passed = [dx for dx in ring if abs(dx) < RING]
    for dx in passed:
        @pl.when(exists(-dx, 0))
        def _():
            relay(dx).start()

        started.append((exists(-dx, 0), functools.partial(relay, dx)))
    for dx in passed:
        @pl.when(exists(-dx, 0))
        def _():
            relay_comes(dx).wait_recv()

    def low_weights(s, carry):
        u = [fold(gw[s, f // 2], gw[s + 8, f // 2], f % 2) for f in range(6)]
        for c in (0, 1):
            third = jnp.where(q48 < 16, rot(u[c], 80), jnp.where(q48 < 32, rot(u[2 + c], 96), rot(u[4 + c], 112)))
            rdl[c, s, lwin, :] = jnp.where(q48 < 48, third, 0.0)
        rd = rdl[0, s, lwin, :]
        for f in range(6):
            ul[f, s + 1, lwin, :] = u[f]
            wl[f, s, lwin, :] = u[f] * rd
        return carry

    lax.fori_loop(0, 8, low_weights, 0, unroll=True)
    ul[1, 0, lwin, :] = rot(ul[1, 8, lwin, :], 64)
    ul[1, 9, lwin, :] = rot(ul[1, 1, lwin, :], 64)

    def low_black(s, carry):
        rd = rdl[1, s, lwin, :]
        wl[6, s, lwin, :] = ul[0, s + 1, lwin, :] * rd
        wl[7, s, lwin, :] = jnp.where(odd48, ul[1, s, lwin, :], ul[1, s + 2, lwin, :]) * rd
        wl[8, s, lwin, :] = ul[3, s + 1, pl.ds(7, LR), :] * rd
        wl[9, s, lwin, :] = ul[2, s + 1, pl.ds(9, LR), :] * rd
        wl[10, s, lwin, :] = rot(ul[5, s + 1, lwin, :], 1) * rd
        wl[11, s, lwin, :] = rot(ul[4, s + 1, lwin, :], 127) * rd
        return carry

    lax.fori_loop(0, 8, low_black, 0, unroll=True)

    ring_arrive(send_b)

    def low_source(s, carry):
        lo, hi = gb[s], gb[s + 8]
        first = 16.0 * fold(lo, hi, 0) * rdl[0, s, lwin, :]
        sl[0, s, lwin, :] = first
        plow[0, s + 1, lwin, :] = first
        sl[1, s, lwin, :] = 16.0 * fold(lo, hi, 1) * rdl[1, s, lwin, :]
        return carry

    lax.fori_loop(0, 8, low_source, 0, unroll=True)

    def low_ghosts(c, r0, n):
        win = pl.ds(r0, n)
        plow[c, 0, win, :] = rot(plow[c, 8, win, :], 64)
        plow[c, 9, win, :] = rot(plow[c, 1, win, :], 64)

    low_ghosts(0, 8, LR)
    for half in range(2, 2 * BOTTOM + 1):
        c = (half - 1) % 2
        reach = 4 + 2 * BOTTOM - half
        r0, n = 8 + 20 - reach, 8 * ((4 + 2 * reach + 7) // 8)
        odd = odd_low(n, r0)

        def low_body(s, carry, c=c, r0=r0, n=n, odd=odd):
            o = 1 - c
            win = pl.ds(r0, n)
            xs, lo, hi = plow[o, s + 1, win, :], plow[o, s, win, :], plow[o, s + 2, win, :]
            xo = jnp.where(odd, hi, lo) if c == 0 else jnp.where(odd, lo, hi)
            total = sl[c, s, win, :] + wl[6 * c, s, win, :] * xs
            total = total + wl[6 * c + 1, s, win, :] * xo
            total = total + wl[6 * c + 2, s, win, :] * plow[o, s + 1, pl.ds(r0 - 1, n), :]
            total = total + wl[6 * c + 3, s, win, :] * plow[o, s + 1, pl.ds(r0 + 1, n), :]
            total = total + wl[6 * c + 4, s, win, :] * rot(xs, 1)
            plow[c, s + 1, win, :] = total + wl[6 * c + 5, s, win, :] * rot(xs, 127)
            return carry

        side = (reach + 1) // 2
        if side <= 3:
            lax.fori_loop(4 - side, 5 + side, low_body, 0, unroll=True)
        else:
            lax.fori_loop(0, 8, low_body, 0, unroll=True)
            low_ghosts(c, r0, n)

    arrive(WIDE, mb_refs, s_mb, r_mb)
    odd16, h16 = odd_low(16, 0), h1_of(16)
    rows24 = pl.ds(8, 24)

    def mid_correct(s, carry):
        red_, black_ = plow[0, s + 3, pl.ds(24, 16), :], plow[1, s + 3, pl.ds(24, 16), :]
        for e in (0, 1):
            v = jnp.where(odd16, black_, red_) if e == 0 else jnp.where(odd16, red_, black_)
            v = jnp.where(h16, rot(v, 64), v)
            em[2 * s + e, pl.ds(0, 16, stride=2), :] = v
            em[2 * s + e, pl.ds(1, 16, stride=2), :] = v
            m = 2 * s + e
            add = em[m, 0:24, :] * jnp.where(pair_ok(2 * a - 4, m, 2 * nx), 1.0, 0.0)
            pm[1, m, rows24, :] = mb0[m, rows24, :] + add
        return carry

    lax.fori_loop(0, 5, mid_correct, 0, unroll=True)
    mid_half(0, 1, 9, 10, 24)
    mid_half(1, 1, 9, 11, 24)
    mid_half(0, 2, 8, 12, 16)
    mid_half(1, 2, 8, 13, 16)

    arrive(NEAR, pb_refs, s_pb, r_pb)
    odd_c = odd_mid(16, 13)

    for m in range(10):
        n, e = (m + 5) // 2, (m + 5) % 2
        red_, black_ = pm[0, n, pl.ds(13, 16), :], pm[1, n, pl.ds(13, 16), :]
        v = jnp.where(odd_c, black_, red_) if e == 0 else jnp.where(odd_c, red_, black_)
        e1[m, pl.ds(2, 16, stride=2), :] = v
        e1[m, pl.ds(3, 16, stride=2), :] = v
        for t in (0, 1):
            pf[1, m, t, pl.ds(3, 32), :] = pb0[m, t, pl.ds(3, 32), :] + e1[m, pl.ds(3, 32), :]

    fine_half(0, 1, 9, 4, 24)
    fine_half(1, 1, 9, 5, 24)
    fine_half(0, 2, 8, 6, 24)
    fine_last(7, 24)
    fine_red_residual()

    kk2 = lax.broadcasted_iota(jnp.int32, (2 * LANES, nz), 1)
    cc2 = lax.broadcasted_iota(jnp.int32, (2 * LANES, nz), 0)
    q2, hh2, tt2 = lax.rem(cc2, 64), lax.rem(lax.div(cc2, 64), 2), lax.div(cc2, 128)
    back = jnp.where(jnp.logical_and(kk2 == 4 * q2 + 2 * hh2 + tt2, q2 < 48), 1.0, 0.0).astype(F32)

    def join_from(src, out):
        for t in (0, 1):
            odd = odd_fine(16, 8, t)
            for m in range(4):
                r, k = src[0, 3 + m, t, 8:24, :], src[1, 3 + m, t, 8:24, :]
                xo_s[32 * m:32 * m + 16, t * LANES:(t + 1) * LANES] = jnp.where(odd, k, r)
                xo_s[32 * m + 16:32 * m + 32, t * LANES:(t + 1) * LANES] = jnp.where(odd, r, k)
        out[...] = reorder(xo_s[...], back).reshape(out.shape)

    join_from(pf, out_p)
    join_from(rf, out_r)
    for ok, cp in started:
        if ok is None:
            cp().wait_send()
        else:
            @pl.when(ok)
            def _():
                cp().wait_send()


def solution(mesh):
    nx, ny = mesh.shape["gx"], mesh.shape["gy"]

    def local(right_side, phase):
        shape = right_side.shape
        v = lambda *dims: pltpu.VMEM(dims, F32)
        sems = []
        for n in (len(NEAR), len(NEAR), len(WIDE), len(WIDE), len(NEAR), len(WIDE), len(ALONG), len(ALONG), nx - 1, nx - 1, nx):
            sems += [pltpu.SemaphoreType.DMA((n,)), pltpu.SemaphoreType.DMA((n,))]
        fine = (10, 2, 40, LANES)
        return pl.pallas_call(
            functools.partial(kernel, nx, ny),
            out_shape=[jax.ShapeDtypeStruct(shape, F32)] * 2,
            in_specs=[pl.BlockSpec(memory_space=pltpu.HBM)] * 2,
            out_specs=[pl.BlockSpec(memory_space=pltpu.VMEM)] * 2,
            scratch_shapes=[
                v(*shape), pltpu.VMEM(shape, jnp.int32),
                v(2, *fine), v(2, *fine), v(12, *fine), v(2, *fine), v(2, *fine), v(2, *fine), v(2, *fine), v(*fine),
                v(2, *fine), v(3, 10, 32, LANES), v(3, 5, 24, LANES),
                v(3, 21, 40, LANES), v(20, 40, LANES), v(12, 10, 40, LANES), v(2, 10, 40, LANES), v(2, 10, 40, LANES),
                v(2, 10, 40, LANES), v(2, 10, 40, LANES), v(10, 40, LANES), v(10, 16, LANES), v(10, 32, LANES),
                v(3, 48, LANES), v(48, LANES), v(16, 3, 48, LANES), v(16, 48, LANES), v(6, 10, 64, LANES),
                v(12, 8, 64, LANES), v(2, 8, 64, LANES), v(2, 8, 64, LANES), v(2, 10, 64, LANES), v(10, 40, LANES),
                v(128, 2 * LANES),
                pltpu.SemaphoreType.DMA((2,)),
            ] + sems,
            compiler_params=pltpu.CompilerParams(
                collective_id=0, has_side_effects=True, vmem_limit_bytes=56262656
            ),
        )(right_side, phase)

    spec = P("gx", "gy", None)
    return jax.shard_map(local, mesh=mesh, in_specs=(spec, spec), out_specs=(spec, spec), check_vma=False)
```

```python
import functools

import numpy as np

import jax
import jax.numpy as jnp
from jax import lax
from jax.experimental import pallas as pl
from jax.experimental.pallas import tpu as pltpu
from jax.sharding import PartitionSpec as P

F32 = jnp.float32
MESH = pl.DeviceIdType.MESH
LANES = 128
BOTTOM = 8
RING = 10

_L, _D = np.float32(1.0), np.float32(0.1)
W_LL = float(np.float32(2) * _L * _L / (_L + _L))
W_MX = float(np.float32(2) * _L * _D / (_L + _D))
W_DD = float(np.float32(2) * _D * _D / (_D + _D))

REACH = 5
NEAR = [(-1, 0), (1, 0), (-1, -1), (1, -1), (-1, 1), (1, 1), (0, -1), (0, 1)]
FAR = [(dx, dy) for dx in (-2, 2) for dy in (-1, 0, 1)]
WIDE = NEAR + FAR
ALONG = [d * s for d in range(REACH, 0, -1) for s in (1, -1)]


def ring_order(n):
    side = 4
    return sorted(range(1, n), key=lambda d: -(min(d % side, side - d % side) + min(d // side, side - d // side)))


def rot(v, shift):
    return pltpu.roll(v, shift, 1)


def span(step, own, size, take):
    if step == 0:
        return own, size
    if isinstance(take, tuple):
        take = take[0] if step < 0 else take[1]
    if step > 0:
        return own + size - take, take
    return own, take


def kernel(
    nx, ny,
    rs_hbm, ph_hbm, out_p, out_r,
    rs_in, ph_in,
    ph, rs, wf, sf, df, rdf, pf, pb0, rf, tf, f1o,
    f1, b1, wm, sm, dm, rdm, pm, mb0, rm, em,
    lw, lb, gw, gb, ul, wl, sl, rdl, plow, e1, xo_s,
    in_sem,
    s_ph, r_ph, s_rs, r_rs, s_f1, r_f1, s_b1, r_b1, s_pb, r_pb, s_mb, r_mb,
    s_lw, r_lw, s_lb, r_lb, s_gw, r_gw, s_gb, r_gb, s_re, r_re,
):
    a = lax.axis_index("gx")
    b = lax.axis_index("gy")

    def exists(dx, dy):
        ok = None
        for pos, d, n in ((a, dx, nx), (b, dy, ny)):
            if d:
                one = (pos + d >= 0) if d < 0 else (pos + d < n)
                ok = one if ok is None else jnp.logical_and(ok, one)
        return ok

    started = []

    def copy(src, dst, ssem, rsem, i, dev):
        return pltpu.make_async_remote_copy(
            src_ref=src, dst_ref=dst, send_sem=ssem.at[i], recv_sem=rsem.at[i], device_id=dev, device_id_type=MESH
        )

    def send(steps, refs, ssem, rsem, base=0):
        for i, (dx, dy) in enumerate(steps):
            src, dst = refs(dx, dy)
            cp = functools.partial(copy, src, dst, ssem, rsem, base + i, (a + dx, b + dy))
            ok = exists(dx, dy)

            @pl.when(ok)
            def _():
                cp().start()

            started.append((ok, cp))

    def arrive(steps, refs, ssem, rsem, base=0):
        for i, (dx, dy) in enumerate(steps):
            src, dst = refs(dx, dy)

            @pl.when(exists(-dx, -dy))
            def _():
                copy(src, dst, ssem, rsem, base + i, (a - dx, b - dy)).wait_recv()

    ring = [dx for d in ring_order(nx) for dx in (d, d - nx) if abs(dx) <= RING]
    core = lax.rem(b, 2)

    def slot(dx):
        return (4 - dx) % nx

    def whole_rows(dx):
        return pl.ds(2 * abs(dx), 44 - 4 * abs(dx))

    def half_rows(dx):
        return pl.ds(2 * abs(dx) + core * (20 - 2 * abs(dx)), 24 - 2 * abs(dx))

    def send_w(dx):
        return copy(lw.at[:, half_rows(dx)], gw.at[slot(dx), :, half_rows(dx)], s_gw, r_gw, dx % nx - 1, (a + dx, b))

    def send_b(dx):
        return copy(lb.at[whole_rows(dx)], gb.at[slot(dx), whole_rows(dx)], s_gb, r_gb, dx % nx - 1, (a + dx, b))

    def relay(dx):
        d, n = 2 * abs(dx), 20 - 2 * abs(dx)
        src, dst = d + 4 + core * (16 - d), d + core * (24 - d)
        return copy(
            gw.at[slot(dx), :, pl.ds(src, n)], gw.at[slot(dx), :, pl.ds(dst, n)], s_re, r_re, dx % nx, (a, b + 1 - 2 * core)
        )

    def relay_comes(dx):
        d, n = 2 * abs(dx), 20 - 2 * abs(dx)
        dst = pl.ds(24 + core * (d - 24), n)
        return copy(
            gw.at[slot(dx), :, dst], gw.at[slot(dx), :, dst], s_re, r_re, dx % nx, (a, b + 1 - 2 * core)
        )

    def ring_send(made):
        for dx in ring:
            @pl.when(exists(dx, 0))
            def _():
                made(dx).start()

            started.append((exists(dx, 0), functools.partial(made, dx)))

    def ring_arrive(made):
        for dx in ring:
            @pl.when(exists(-dx, 0))
            def _():
                made(dx).wait_recv()

    def fine_refs(arr, lead, pairs, rows):
        def refs(dx, dy):
            x0, xn = span(dx, 3, 4, 2 if dy else pairs)
            y0, yn = span(dy, 8, 16, rows - 1 if dx else rows)
            pre = (slice(None),) * lead
            return (
                arr.at[pre + (pl.ds(x0, xn), slice(None), pl.ds(y0, yn))],
                arr.at[pre + (pl.ds(x0 - 4 * dx, xn), slice(None), pl.ds(y0 - 16 * dy, yn))],
            )

        return refs

    def mid_refs(arr, lead, own, size, far, rows, far_corner):
        def refs(dx, dy):
            x0, xn = span(dx, own, size, size if abs(dx) < 2 else far_corner[0] if dy else far)
            y0, yn = span(dy, 16, 8, rows[0] if dx == 0 else rows[1] if abs(dx) < 2 else far_corner[1])
            pre = (slice(None),) * lead
            return (
                arr.at[pre + (pl.ds(x0, xn), pl.ds(y0, yn))],
                arr.at[pre + (pl.ds(x0 - size * dx, xn), pl.ds(y0 - 8 * dy, yn))],
            )

        return refs

    def low_refs(arr, lead):
        def refs(dx, dy):
            pre = (slice(None),) * lead
            return arr.at[pre + (pl.ds(20, 4),)], arr.at[pre + (pl.ds(20 - 4 * dy, 4),)]

        return refs

    ph_refs = fine_refs(ph, 1, 3, 5)
    rs_refs = fine_refs(rs, 1, 2, 4)
    pb_refs = fine_refs(pb0, 0, 3, 5)
    f1_refs = mid_refs(f1, 1, 8, 4, (3, 2), ((7, 6), (6, 5)), (2, 2))
    b1_refs = mid_refs(b1, 0, 8, 4, 2, (6, 5), (1, 1))
    mb_refs = mid_refs(mb0, 0, 4, 2, 2, (7, 6), (1, 2))
    lw_refs = low_refs(lw, 1)
    lb_refs = low_refs(lb, 0)
    gy_steps = [(0, d) for d in ALONG]

    bar = pltpu.get_barrier_semaphore()
    count = jnp.int32(nx - 1)
    for dx, dy in [(dx, dy) for dx, dy in WIDE if dy] + [(0, d) for d in ALONG if abs(d) > 1]:
        ok = exists(dx, dy)

        @pl.when(ok)
        def _():
            pl.semaphore_signal(bar, inc=1, device_id=(a + dx, b + dy), device_id_type=MESH)

        count = count + ok.astype(jnp.int32)

    for d in ring_order(nx):
        pl.semaphore_signal(bar, inc=1, device_id=(lax.rem(a + d, nx), b), device_id_type=MESH)
    in_rs = pltpu.make_async_copy(rs_hbm, rs_in, in_sem.at[0])
    in_ph = pltpu.make_async_copy(ph_hbm, ph_in, in_sem.at[1])
    in_ph.start()
    in_rs.start()

    def iota(rows, dim):
        return lax.broadcasted_iota(jnp.int32, (rows, LANES), dim)

    def h1_of(rows):
        return iota(rows, 1) >= 64

    def lane_ok(rows):
        return lax.rem(iota(rows, 1), 64) < 48

    def odd_fine(rows, start, t):
        return lax.rem(iota(rows, 0) + (start + t), 2) == 1

    def odd_mid(rows, start):
        return lax.rem(iota(rows, 0) + start + lax.div(iota(rows, 1), 64), 2) == 1

    def odd_low(rows, start):
        return lax.rem(iota(rows, 0) + start + iota(rows, 1), 2) == 1

    def inverse(v):
        r = pl.reciprocal(v, approx=True)
        r = r * (2.0 - v * r)
        return r * (2.0 - v * r)

    def zero(ref):
        ref[...] = jnp.zeros(ref.shape, F32)

    @pl.when(a == 0)
    def _():
        zero(ph.at[:, 0:3]); zero(rs.at[:, 0:3]); zero(pb0.at[0:3]); zero(f1.at[:, 0:8]); zero(b1.at[0:8]); zero(mb0.at[0:4])

    @pl.when(a == 1)
    def _():
        zero(f1.at[:, 0:4]); zero(b1.at[0:4]); zero(mb0.at[0:2])

    @pl.when(a == nx - 1)
    def _():
        zero(ph.at[:, 7:10]); zero(rs.at[:, 7:10]); zero(pb0.at[7:10])
        zero(f1.at[:, 12:21]); zero(b1.at[12:20]); zero(mb0.at[6:10])

    @pl.when(a == nx - 2)
    def _():
        zero(f1.at[:, 16:21]); zero(b1.at[16:20]); zero(mb0.at[8:10])

    @pl.when(b == 0)
    def _():
        zero(ph.at[:, :, :, 0:8]); zero(rs.at[:, :, :, 0:8]); zero(pb0.at[:, :, 0:8])
        zero(f1.at[:, :, 0:16]); zero(b1.at[:, 0:16]); zero(mb0.at[:, 0:16])

    @pl.when(b == ny - 1)
    def _():
        zero(ph.at[:, :, :, 24:32]); zero(rs.at[:, :, :, 24:32]); zero(pb0.at[:, :, 24:32])
        zero(f1.at[:, :, 24:40]); zero(b1.at[:, 24:40]); zero(mb0.at[:, 24:40])

    for d in ALONG:
        @pl.when(jnp.logical_not(exists(0, d)))
        def _():
            zero(lw.at[:, pl.ds(20 + 4 * d, 4)])
            zero(lb.at[pl.ds(20 + 4 * d, 4)])

    for dx in list(range(1, nx)) + list(range(-1, -nx, -1)):
        @pl.when(exists(-dx, 0))
        def _():
            if abs(dx) > RING:
                zero(gw.at[slot(dx)])
                zero(gb.at[slot(dx)])
            else:
                for rows in (slice(0, 2 * abs(dx)), slice(44 - 2 * abs(dx), 48)):
                    zero(gw.at[slot(dx), :, rows])
                    zero(gb.at[slot(dx), rows])

    nz = rs_in.shape[2]
    kk = lax.broadcasted_iota(jnp.int32, (nz, 2 * LANES), 0)
    cc = lax.broadcasted_iota(jnp.int32, (nz, 2 * LANES), 1)
    q, hh, tt = lax.rem(cc, 64), lax.rem(lax.div(cc, 64), 2), lax.div(cc, 128)
    perm = jnp.where(jnp.logical_and(kk == 4 * q + 2 * hh + tt, q < 48), 1.0, 0.0).astype(F32)

    def reorder(v, matrix):
        m16 = matrix.astype(jnp.bfloat16)
        total = None
        for _ in range(3):
            part = v.astype(jnp.bfloat16)
            v = v - part.astype(F32)
            dot = jnp.dot(part, m16, preferred_element_type=F32)
            total = dot if total is None else total + dot
        return total

    def split_into(values, dst):
        for t in (0, 1):
            odd = odd_fine(16, 0, t)
            for m in range(4):
                lo = values[32 * m:32 * m + 16, t * LANES:(t + 1) * LANES]
                hi = values[32 * m + 16:32 * m + 32, t * LANES:(t + 1) * LANES]
                dst[0, 3 + m, t, 8:24, :] = jnp.where(odd, hi, lo)
                dst[1, 3 + m, t, 8:24, :] = jnp.where(odd, lo, hi)

    in_ph.wait()
    labels = jnp.where(ph_in[...] == 1, 1.0, 0.0).astype(F32).reshape(128, nz)
    split_into(jnp.dot(labels, perm, preferred_element_type=F32), ph)
    in_rs.wait()
    block = rs_in[...].reshape(128, nz)
    split_into(reorder(block, perm), rs)

    pl.semaphore_wait(bar, count)
    send(NEAR, ph_refs, s_ph, r_ph)
    send(NEAR, rs_refs, s_rs, r_rs)

    def pair_ok(first, m, total):
        g = first + m
        return jnp.logical_and(g >= 0, g < total)

    def inside(rows, start, total, ok):
        g = iota(rows, 0) + (start + jnp.where(ok, 0, -4096))
        return jnp.logical_and(jnp.logical_and(g >= 0, g < total), lane_ok(rows))

    def fine_sides(arr, c, m, t, r0, n, odd, h1):
        o = 1 - c
        xs = arr[o, m, t, pl.ds(r0, n), :]
        lo = arr[o, m - 1, t, pl.ds(r0, n), :]
        hi = arr[o, m + 1, t, pl.ds(r0, n), :]
        xo = jnp.where(odd, hi, lo) if c == 0 else jnp.where(odd, lo, hi)
        ym = arr[o, m, t, pl.ds(r0 - 1, n), :]
        yp = arr[o, m, t, pl.ds(r0 + 1, n), :]
        zs = arr[o, m, 1 - t, pl.ds(r0, n), :]
        if t == 0:
            zo = jnp.where(h1, rot(zs, 64), rot(zs, 65))
        else:
            zo = jnp.where(h1, rot(zs, 63), rot(zs, 64))
        return xs, xo, ym, yp, zs, zo

    R0, RN = 4, 24
    odd24 = [odd_fine(RN, R0, 0), odd_fine(RN, R0, 1)]
    h24 = h1_of(RN)

    arrive(NEAR, ph_refs, s_ph, r_ph)

    def levels(c, m, t):
        dense = ph[c, m, t, pl.ds(R0, RN), :] > 0.5
        return jnp.where(dense, W_DD, W_MX), jnp.where(dense, W_MX, W_LL)

    def own_faces(m, carry):
        fx = fy = fz = None
        for t in (0, 1):
            both = []
            for c in (0, 1):
                on, off = levels(c, m, t)
                side = fine_sides(ph, c, m, t, R0, RN, odd24[t], h24)
                both.append([jnp.where(side[f] > 0.5, on, off) for f in (1, 2, 5)])
            x = jnp.where(odd24[t], both[1][0], both[0][0])
            y = both[0][1] + both[1][1]
            fx = x if fx is None else fx + x
            fy = y if fy is None else fy + y
            if t == 0:
                fz = both[0][2] + both[1][2]
        tf[0, m, 0:RN, :] = fx
        tf[1, m, 0:RN, :] = fy
        tf[2, m, 0:RN, :] = fz
        return carry

    lax.fori_loop(3, 8, own_faces, 0, unroll=True)

    even, oddr = pl.ds(0, 16, stride=2), pl.ds(1, 16, stride=2)

    def mid_faces(i, carry):
        f1o[0, i, 0:16, :] = 0.25 * (tf[0, i + 3, even, :] + tf[0, i + 3, oddr, :])
        f1o[1, i, 0:16, :] = 0.25 * tf[1, i + 3, even, :]
        f1o[2, i, 0:16, :] = 0.25 * (tf[2, i + 3, even, :] + tf[2, i + 3, oddr, :])
        return carry

    lax.fori_loop(0, 5, mid_faces, 0, unroll=True)
    h8 = h1_of(8)
    for i in range(4):
        fx, fxn = f1o[0, i, 2:10, :], f1o[0, i + 1, 2:10, :]
        fy, fyn = f1o[1, i, 2:10, :], f1o[1, i, 3:11, :]
        fz = f1o[2, i, 2:10, :]
        fzn = jnp.where(h8, rot(fz, 63), rot(fz, 64))
        dg = ((((fx + fxn) + fy) + fyn) + fz) + fzn
        for f, w in enumerate((fx, fy, fz)):
            f1[f, 8 + i, 16:24, :] = jnp.where(lane_ok(8), w, rot(dg, 48 - 16 * f))
    send(NEAR, f1_refs, s_f1, r_f1)

    def zsum(v):
        return v + rot(v, 64)

    fx2 = [0.25 * zsum(f1o[0, 2 * i, pl.ds(2, 8, stride=2), :] + f1o[0, 2 * i, pl.ds(3, 8, stride=2), :]) for i in range(3)]
    fy2, fy2n, fz2, fz2n = [], [], [], []
    for i in range(2):
        fy2.append(0.25 * zsum(f1o[1, 2 * i, pl.ds(2, 8, stride=2), :] + f1o[1, 2 * i + 1, pl.ds(2, 8, stride=2), :]))
        fy2n.append(0.25 * zsum(f1o[1, 2 * i, pl.ds(4, 8, stride=2), :] + f1o[1, 2 * i + 1, pl.ds(4, 8, stride=2), :]))
        v = (f1o[2, 2 * i, pl.ds(2, 8, stride=2), :] + f1o[2, 2 * i, pl.ds(3, 8, stride=2), :]) + (
            f1o[2, 2 * i + 1, pl.ds(2, 8, stride=2), :] + f1o[2, 2 * i + 1, pl.ds(3, 8, stride=2), :]
        )
        v = 0.25 * jnp.where(h8, rot(v, 64), v)
        fz2.append(v)
        fz2n.append(rot(v, 127))
    odd8 = odd_low(8, 0)
    dg2 = [((((fx2[i] + fx2[i + 1]) + fy2[i]) + fy2n[i]) + fz2[i]) + fz2n[i] for i in range(2)]
    rd2 = [jnp.where(lane_ok(8), 1.0 / d, 0.0) for d in dg2]

    def red(v):
        return jnp.where(odd8, v[1], v[0])

    def black(v):
        return jnp.where(odd8, v[0], v[1])

    edge_low = jnp.where(a == 0, 0.0, 1.0)
    edge_high = jnp.where(a == nx - 1, 0.0, 1.0)
    xo2 = jnp.where(odd8, fx2[2] * edge_high, fx2[0] * edge_low)
    inv = jnp.where(h8, black(rd2), red(rd2))
    for f, (first, second) in enumerate(((fx2[1], xo2), (red(fy2), red(fy2n)), (red(fz2), red(fz2n)))):
        v = jnp.where(lane_ok(8), jnp.where(h8, second, first), rot(inv, 48 - 16 * f))
        lw[f, 20:24, :] = v[0:4]
    send(gy_steps, lw_refs, s_lw, r_lw)

    def fine_weights(m, carry):
        valid = inside(RN, 16 * b - 8 + R0, 16 * ny, pair_ok(4 * a - 3, m, 4 * nx))
        for t in (0, 1):
            for c in (0, 1):
                on, off = levels(c, m, t)
                side = fine_sides(ph, c, m, t, R0, RN, odd24[t], h24)
                many = ((((side[0] + side[1]) + side[2]) + side[3]) + side[4]) + side[5]
                dg = 6.0 * off + many * (on - off)
                rd = jnp.where(valid, inverse(dg), 0.0)
                won, woff = on * rd, off * rd
                for f in range(6):
                    wf[6 * c + f, m, t, pl.ds(R0, RN), :] = jnp.where(side[f] > 0.5, won, woff)
                df[c, m, t, pl.ds(R0, RN), :] = dg
                rdf[c, m, t, pl.ds(R0, RN), :] = rd
        return carry

    lax.fori_loop(1, 9, fine_weights, 0, unroll=True)

    def fine_nb(c, m, t, r0, n, odd, h1):
        v = fine_sides(pf, c, m, t, r0, n, odd, h1)
        total = wf[6 * c, m, t, pl.ds(r0, n), :] * v[0]
        for f in range(1, 6):
            total = total + wf[6 * c + f, m, t, pl.ds(r0, n), :] * v[f]
        return total

    def fine_half(c, m0, m1, r0, n):
        odd = [odd_fine(n, r0, 0), odd_fine(n, r0, 1)]
        h1 = h1_of(n)

        def body(m, carry):
            for t in (0, 1):
                nb = fine_nb(c, m, t, r0, n, odd[t], h1)
                pf[c, m, t, pl.ds(r0, n), :] = sf[c, m, t, pl.ds(r0, n), :] + nb
            return carry

        lax.fori_loop(m0, m1, body, 0, unroll=True)

    def fine_last(r0, n):
        odd = [odd_fine(n, r0, 0), odd_fine(n, r0, 1)]
        h1 = h1_of(n)

        def body(m, carry):
            for t in (0, 1):
                win = pl.ds(r0, n)
                nb = fine_nb(1, m, t, r0, n, odd[t], h1)
                fresh = sf[1, m, t, win, :] + nb
                pf[1, m, t, win, :] = fresh
                rf[1, m, t, win, :] = rs[1, m, t, win, :] - df[1, m, t, win, :] * (fresh - nb)
            return carry

        lax.fori_loop(2, 8, body, 0, unroll=True)

    def fine_red_residual():
        odd = [odd_fine(16, 8, 0), odd_fine(16, 8, 1)]
        h1 = h1_of(16)

        def body(m, carry):
            for t in (0, 1):
                win = pl.ds(8, 16)
                nb = fine_nb(0, m, t, 8, 16, odd[t], h1)
                rf[0, m, t, win, :] = rs[0, m, t, win, :] - df[0, m, t, win, :] * (pf[0, m, t, win, :] - nb)
            return carry

        lax.fori_loop(3, 7, body, 0, unroll=True)

    arrive(NEAR, rs_refs, s_rs, r_rs)

    def fine_source(m, carry):
        win = pl.ds(R0, RN)
        for t in (0, 1):
            first = rs[0, m, t, win, :] * rdf[0, m, t, win, :]
            sf[0, m, t, win, :] = first
            pf[0, m, t, win, :] = first
            sf[1, m, t, win, :] = rs[1, m, t, win, :] * rdf[1, m, t, win, :]
        return carry

    lax.fori_loop(1, 9, fine_source, 0, unroll=True)
    fine_half(1, 1, 9, 4, 24)
    fine_half(0, 2, 8, 6, 24)
    fine_last(7, 24)
    fine_red_residual()

    def restrict_fine(m, carry):
        v = (rf[0, m, 0, 8:24, :] + rf[1, m, 0, 8:24, :]) + (rf[0, m, 1, 8:24, :] + rf[1, m, 1, 8:24, :])
        rm[m, 0:16, :] = v
        b1[m + 5, 16:24, :] = 0.125 * (rm[m, pl.ds(0, 8, stride=2), :] + rm[m, pl.ds(1, 8, stride=2), :])
        return carry

    lax.fori_loop(3, 7, restrict_fine, 0, unroll=True)
    send(WIDE, b1_refs, s_b1, r_b1)

    def keep_black(m, carry):
        for t in (0, 1):
            pb0[m, t, 8:24, :] = pf[1, m, t, 8:24, :]
        return carry

    lax.fori_loop(3, 7, keep_black, 0, unroll=True)
    send(NEAR, pb_refs, s_pb, r_pb)
    send(FAR, f1_refs, s_f1, r_f1, len(NEAR))

    def mid_weights(m0, m1, r0, n, top):
        odd, h1 = odd_mid(n, r0), h1_of(n)
        win, nxt = pl.ds(r0, n), pl.ds(r0 + 1, n)
        q = lax.rem(iota(n, 1), 64)
        q16, q32 = q < 16, q < 32

        def body(m, carry):
            valid = inside(n, 8 * b - 16 + r0, 8 * ny, pair_ok(2 * a - 4, m, 2 * nx))
            e0, e1_ = 2 * m, 2 * m + 1
            fx0, fx1, fx2_ = f1[0, e0, win, :], f1[0, e1_, win, :], f1[0, jnp.minimum(e1_ + 1, top), win, :]
            ym = [f1[1, e, win, :] for e in (e0, e1_)]
            yp = [f1[1, e, nxt, :] for e in (e0, e1_)]
            fz = [f1[2, e, win, :] for e in (e0, e1_)]
            zs = [jnp.where(h1, v, rot(v, 64)) for v in fz]
            zo = [jnp.where(h1, rot(v, 63), v) for v in fz]
            dg = [
                jnp.where(q16, rot(f1[0, e, win, :], 80), jnp.where(q32, rot(f1[1, e, win, :], 96), rot(f1[2, e, win, :], 112)))
                for e in (e0, e1_)
            ]
            for c in (0, 1):
                def pick(v):
                    return jnp.where(odd, v[1 - c], v[c])

                xo = jnp.where(odd, fx2_, fx0) if c == 0 else jnp.where(odd, fx0, fx2_)
                d = pick(dg)
                rd = jnp.where(valid, 1.0 / d, 0.0)
                for f, w in enumerate((fx1, xo, pick(ym), pick(yp), pick(zs), pick(zo))):
                    wm[6 * c + f, m, win, :] = w * rd
                dm[c, m, win, :] = d
                rdm[c, m, win, :] = rd
            return carry

        lax.fori_loop(m0, m1, body, 0, unroll=True)

    def mid_source(m0, m1, r0, n, start):
        odd = odd_mid(n, r0)
        win = pl.ds(r0, n)

        def body(m, carry):
            lo, hi = b1[2 * m, win, :], b1[2 * m + 1, win, :]
            first = 4.0 * jnp.where(odd, hi, lo) * rdm[0, m, win, :]
            sm[0, m, win, :] = first
            if start:
                pm[0, m, win, :] = first
            sm[1, m, win, :] = 4.0 * jnp.where(odd, lo, hi) * rdm[1, m, win, :]
            return carry

        lax.fori_loop(m0, m1, body, 0, unroll=True)

    def mid_nb(c, m, r0, n, odd, h1):
        o = 1 - c
        win = pl.ds(r0, n)
        xs, lo, hi = pm[o, m, win, :], pm[o, m - 1, win, :], pm[o, m + 1, win, :]
        xo = jnp.where(odd, hi, lo) if c == 0 else jnp.where(odd, lo, hi)
        zo = jnp.where(h1, rot(xs, 63), rot(xs, 65))
        total = wm[6 * c, m, win, :] * xs
        total = total + wm[6 * c + 1, m, win, :] * xo
        total = total + wm[6 * c + 2, m, win, :] * pm[o, m, pl.ds(r0 - 1, n), :]
        total = total + wm[6 * c + 3, m, win, :] * pm[o, m, pl.ds(r0 + 1, n), :]
        total = total + wm[6 * c + 4, m, win, :] * rot(xs, 64)
        return total + wm[6 * c + 5, m, win, :] * zo

    def mid_half(c, m0, m1, r0, n):
        odd, h1 = odd_mid(n, r0), h1_of(n)

        def body(m, carry):
            win = pl.ds(r0, n)
            pm[c, m, win, :] = sm[c, m, win, :] + mid_nb(c, m, r0, n, odd, h1)
            return carry

        lax.fori_loop(m0, m1, body, 0, unroll=True)

    arrive(NEAR, f1_refs, s_f1, r_f1)
    mid_weights(2, 8, 12, 16, 15)
    arrive(gy_steps, lw_refs, s_lw, r_lw)
    ring_send(send_w)
    arrive(NEAR, b1_refs, s_b1, r_b1)
    mid_source(2, 8, 12, 16, True)
    mid_half(1, 2, 8, 13, 16)
    mid_half(0, 3, 7, 14, 16)
    mid_half(1, 3, 7, 15, 16)

    odd_own, h_own = odd_mid(8, 16), h1_of(8)
    own = pl.ds(16, 8)
    planes = []
    for m in (4, 5):
        lo, hi = b1[2 * m, own, :], b1[2 * m + 1, own, :]
        total = None
        for c in (0, 1):
            src = jnp.where(odd_own, hi, lo) if c == 0 else jnp.where(odd_own, lo, hi)
            nb = mid_nb(c, m, 16, 8, odd_own, h_own)
            res = src - dm[c, m, own, :] * (pm[c, m, own, :] - nb) * 0.25
            total = res if total is None else total + res
        rm[m, 0:8, :] = total
        rm[m, 8:16, :] = total
        planes.append(0.125 * zsum(rm[m, pl.ds(0, 8, stride=2), :] + rm[m, pl.ds(1, 8, stride=2), :]))
    lb[20:24, :] = jnp.where(h8, black(planes), red(planes))[0:4]
    send(gy_steps, lb_refs, s_lb, r_lb)
    for m in (4, 5):
        mb0[m, own, :] = pm[1, m, own, :]
    send(WIDE, mb_refs, s_mb, r_mb)

    arrive(FAR, f1_refs, s_f1, r_f1, len(NEAR))
    mid_weights(1, 9, 8, 24, 18)
    arrive(FAR, b1_refs, s_b1, r_b1, len(NEAR))
    mid_source(1, 9, 8, 24, False)

    arrive(gy_steps, lb_refs, s_lb, r_lb)
    ring_send(send_b)
    gw[4, :, 0:44] = lw[:, 0:44]
    gb[4, 0:44] = lb[0:44]

    LR = 48
    h48 = h1_of(LR)
    odd48 = odd_low(LR, 0)
    q48 = lax.rem(iota(LR, 1), 64)
    lwin = pl.ds(8, LR)

    def fold(lo, hi, half):
        if half == 0:
            return jnp.where(h48, rot(hi, 64), lo)
        return jnp.where(h48, hi, rot(lo, 64))

    ring_arrive(send_w)
    passed = [dx for dx in ring if abs(dx) < RING]
    for dx in passed:
        @pl.when(exists(-dx, 0))
        def _():
            relay(dx).start()

        started.append((exists(-dx, 0), functools.partial(relay, dx)))
    for dx in passed:
        @pl.when(exists(-dx, 0))
        def _():
            relay_comes(dx).wait_recv()

    def low_weights(s, carry):
        u = [fold(gw[s, f // 2], gw[s + 8, f // 2], f % 2) for f in range(6)]
        for c in (0, 1):
            third = jnp.where(q48 < 16, rot(u[c], 80), jnp.where(q48 < 32, rot(u[2 + c], 96), rot(u[4 + c], 112)))
            rdl[c, s, lwin, :] = jnp.where(q48 < 48, third, 0.0)
        rd = rdl[0, s, lwin, :]
        for f in range(6):
            ul[f, s + 1, lwin, :] = u[f]
            wl[f, s, lwin, :] = u[f] * rd
        return carry

    lax.fori_loop(0, 8, low_weights, 0, unroll=True)
    ul[1, 0, lwin, :] = rot(ul[1, 8, lwin, :], 64)
    ul[1, 9, lwin, :] = rot(ul[1, 1, lwin, :], 64)

    def low_black(s, carry):
        rd = rdl[1, s, lwin, :]
        wl[6, s, lwin, :] = ul[0, s + 1, lwin, :] * rd
        wl[7, s, lwin, :] = jnp.where(odd48, ul[1, s, lwin, :], ul[1, s + 2, lwin, :]) * rd
        wl[8, s, lwin, :] = ul[3, s + 1, pl.ds(7, LR), :] * rd
        wl[9, s, lwin, :] = ul[2, s + 1, pl.ds(9, LR), :] * rd
        wl[10, s, lwin, :] = rot(ul[5, s + 1, lwin, :], 1) * rd
        wl[11, s, lwin, :] = rot(ul[4, s + 1, lwin, :], 127) * rd
        return carry

    lax.fori_loop(0, 8, low_black, 0, unroll=True)

    ring_arrive(send_b)

    def low_source(s, carry):
        lo, hi = gb[s], gb[s + 8]
        first = 16.0 * fold(lo, hi, 0) * rdl[0, s, lwin, :]
        sl[0, s, lwin, :] = first
        plow[0, s + 1, lwin, :] = first
        sl[1, s, lwin, :] = 16.0 * fold(lo, hi, 1) * rdl[1, s, lwin, :]
        return carry

    lax.fori_loop(0, 8, low_source, 0, unroll=True)

    def low_ghosts(c, r0, n):
        win = pl.ds(r0, n)
        plow[c, 0, win, :] = rot(plow[c, 8, win, :], 64)
        plow[c, 9, win, :] = rot(plow[c, 1, win, :], 64)

    low_ghosts(0, 8, LR)
    def low_half(c, first, step, times, reach):
        r0, n = 8 + 20 - reach, 8 * ((4 + 2 * reach + 7) // 8)
        odd = odd_low(n, r0)

        def low_body(i, carry):
            s = first + step * i
            o = 1 - c
            win = pl.ds(r0, n)
            xs, lo, hi = plow[o, s + 1, win, :], plow[o, s, win, :], plow[o, s + 2, win, :]
            xo = jnp.where(odd, hi, lo) if c == 0 else jnp.where(odd, lo, hi)
            total = sl[c, s, win, :] + wl[6 * c, s, win, :] * xs
            total = total + wl[6 * c + 1, s, win, :] * xo
            total = total + wl[6 * c + 2, s, win, :] * plow[o, s + 1, pl.ds(r0 - 1, n), :]
            total = total + wl[6 * c + 3, s, win, :] * plow[o, s + 1, pl.ds(r0 + 1, n), :]
            total = total + wl[6 * c + 4, s, win, :] * rot(xs, 1)
            plow[c, s + 1, win, :] = total + wl[6 * c + 5, s, win, :] * rot(xs, 127)
            return carry

        lax.fori_loop(0, times, low_body, 0, unroll=True)
        return r0, n

    for half in range(2, 2 * BOTTOM + 1):
        c = (half - 1) % 2
        reach = 4 + 2 * BOTTOM - half
        low_half(c, 4, 1, 1, reach)
        for far in (1, 2, 3):
            if reach >= 2 * far - 1:
                win = low_half(c, 4 - far, 2 * far, 2, reach - 2 * far + 1)
        if reach >= 7:
            low_half(c, 0, 1, 1, reach - 7)
            low_ghosts(c, *win)

    arrive(WIDE, mb_refs, s_mb, r_mb)
    odd16, h16 = odd_low(16, 0), h1_of(16)
    rows24 = pl.ds(8, 24)

    def mid_correct(s, carry):
        red_, black_ = plow[0, s + 3, pl.ds(24, 16), :], plow[1, s + 3, pl.ds(24, 16), :]
        for e in (0, 1):
            v = jnp.where(odd16, black_, red_) if e == 0 else jnp.where(odd16, red_, black_)
            v = jnp.where(h16, rot(v, 64), v)
            em[2 * s + e, pl.ds(0, 16, stride=2), :] = v
            em[2 * s + e, pl.ds(1, 16, stride=2), :] = v
            m = 2 * s + e
            add = em[m, 0:24, :] * jnp.where(pair_ok(2 * a - 4, m, 2 * nx), 1.0, 0.0)
            pm[1, m, rows24, :] = mb0[m, rows24, :] + add
        return carry

    lax.fori_loop(0, 5, mid_correct, 0, unroll=True)
    mid_half(0, 1, 9, 10, 24)
    mid_half(1, 1, 9, 11, 24)
    mid_half(0, 2, 8, 12, 16)
    mid_half(1, 2, 8, 13, 16)

    arrive(NEAR, pb_refs, s_pb, r_pb)
    odd_c = odd_mid(16, 13)

    for m in range(10):
        n, e = (m + 5) // 2, (m + 5) % 2
        red_, black_ = pm[0, n, pl.ds(13, 16), :], pm[1, n, pl.ds(13, 16), :]
        v = jnp.where(odd_c, black_, red_) if e == 0 else jnp.where(odd_c, red_, black_)
        e1[m, pl.ds(2, 16, stride=2), :] = v
        e1[m, pl.ds(3, 16, stride=2), :] = v
        for t in (0, 1):
            pf[1, m, t, pl.ds(3, 32), :] = pb0[m, t, pl.ds(3, 32), :] + e1[m, pl.ds(3, 32), :]

    fine_half(0, 1, 9, 4, 24)
    fine_half(1, 1, 9, 5, 24)
    fine_half(0, 2, 8, 6, 24)
    fine_last(7, 24)
    fine_red_residual()

    kk2 = lax.broadcasted_iota(jnp.int32, (2 * LANES, nz), 1)
    cc2 = lax.broadcasted_iota(jnp.int32, (2 * LANES, nz), 0)
    q2, hh2, tt2 = lax.rem(cc2, 64), lax.rem(lax.div(cc2, 64), 2), lax.div(cc2, 128)
    back = jnp.where(jnp.logical_and(kk2 == 4 * q2 + 2 * hh2 + tt2, q2 < 48), 1.0, 0.0).astype(F32)

    def join_from(src, out):
        for t in (0, 1):
            odd = odd_fine(16, 8, t)
            for m in range(4):
                r, k = src[0, 3 + m, t, 8:24, :], src[1, 3 + m, t, 8:24, :]
                xo_s[32 * m:32 * m + 16, t * LANES:(t + 1) * LANES] = jnp.where(odd, k, r)
                xo_s[32 * m + 16:32 * m + 32, t * LANES:(t + 1) * LANES] = jnp.where(odd, r, k)
        out[...] = reorder(xo_s[...], back).reshape(out.shape)

    join_from(pf, out_p)
    join_from(rf, out_r)
    for ok, cp in started:
        if ok is None:
            cp().wait_send()
        else:
            @pl.when(ok)
            def _():
                cp().wait_send()


def solution(mesh):
    nx, ny = mesh.shape["gx"], mesh.shape["gy"]

    def local(right_side, phase):
        shape = right_side.shape
        v = lambda *dims: pltpu.VMEM(dims, F32)
        sems = []
        for n in (len(NEAR), len(NEAR), len(WIDE), len(WIDE), len(NEAR), len(WIDE), len(ALONG), len(ALONG), nx - 1, nx - 1, nx):
            sems += [pltpu.SemaphoreType.DMA((n,)), pltpu.SemaphoreType.DMA((n,))]
        fine = (10, 2, 40, LANES)
        return pl.pallas_call(
            functools.partial(kernel, nx, ny),
            out_shape=[jax.ShapeDtypeStruct(shape, F32)] * 2,
            in_specs=[pl.BlockSpec(memory_space=pltpu.HBM)] * 2,
            out_specs=[pl.BlockSpec(memory_space=pltpu.VMEM)] * 2,
            scratch_shapes=[
                v(*shape), pltpu.VMEM(shape, jnp.int32),
                v(2, *fine), v(2, *fine), v(12, *fine), v(2, *fine), v(2, *fine), v(2, *fine), v(2, *fine), v(*fine),
                v(2, *fine), v(3, 10, 32, LANES), v(3, 5, 24, LANES),
                v(3, 21, 40, LANES), v(20, 40, LANES), v(12, 10, 40, LANES), v(2, 10, 40, LANES), v(2, 10, 40, LANES),
                v(2, 10, 40, LANES), v(2, 10, 40, LANES), v(10, 40, LANES), v(10, 16, LANES), v(10, 32, LANES),
                v(3, 48, LANES), v(48, LANES), v(16, 3, 48, LANES), v(16, 48, LANES), v(6, 10, 64, LANES),
                v(12, 8, 64, LANES), v(2, 8, 64, LANES), v(2, 8, 64, LANES), v(2, 10, 64, LANES), v(10, 40, LANES),
                v(128, 2 * LANES),
                pltpu.SemaphoreType.DMA((2,)),
            ] + sems,
            compiler_params=pltpu.CompilerParams(
                collective_id=0, has_side_effects=True, vmem_limit_bytes=56262656
            ),
        )(right_side, phase)

    spec = P("gx", "gy", None)
    return jax.shard_map(local, mesh=mesh, in_specs=(spec, spec), out_specs=(spec, spec), check_vma=False)
```

```python
import functools

import numpy as np

import jax
import jax.numpy as jnp
from jax import lax
from jax.experimental import pallas as pl
from jax.experimental.pallas import tpu as pltpu
from jax.sharding import PartitionSpec as P

F32 = jnp.float32
MESH = pl.DeviceIdType.MESH
LANES = 128
BOTTOM = 8
RING = 10

_L, _D = np.float32(1.0), np.float32(0.1)
W_LL = float(np.float32(2) * _L * _L / (_L + _L))
W_MX = float(np.float32(2) * _L * _D / (_L + _D))
W_DD = float(np.float32(2) * _D * _D / (_D + _D))

REACH = 5
NEAR = [(-1, 0), (1, 0), (-1, -1), (1, -1), (-1, 1), (1, 1), (0, -1), (0, 1)]
FAR = [(dx, dy) for dx in (-2, 2) for dy in (-1, 0, 1)]
WIDE = NEAR + FAR
ALONG = [d * s for d in range(REACH, 0, -1) for s in (1, -1)]


def ring_order(n):
    side = 4
    return sorted(range(1, n), key=lambda d: -(min(d % side, side - d % side) + min(d // side, side - d // side)))


def rot(v, shift):
    return pltpu.roll(v, shift, 1)


def span(step, own, size, take):
    if step == 0:
        return own, size
    if isinstance(take, tuple):
        take = take[0] if step < 0 else take[1]
    if step > 0:
        return own + size - take, take
    return own, take


def kernel(
    nx, ny,
    rs_hbm, ph_hbm, out_p, out_r,
    rs_in, ph_in,
    ph, rs, wf, sf, df, rdf, pf, pb0, rf, tf, f1o,
    f1, b1, wm, sm, dm, rdm, pm, mb0, rm, em,
    lw, lb, gw, gb, ul, wl, sl, rdl, plow, e1, xo_s,
    in_sem,
    s_ph, r_ph, s_rs, r_rs, s_f1, r_f1, s_b1, r_b1, s_pb, r_pb, s_mb, r_mb,
    s_lw, r_lw, s_lb, r_lb, s_gw, r_gw, s_gb, r_gb, s_re, r_re,
):
    a = lax.axis_index("gx")
    b = lax.axis_index("gy")

    def exists(dx, dy):
        ok = None
        for pos, d, n in ((a, dx, nx), (b, dy, ny)):
            if d:
                one = (pos + d >= 0) if d < 0 else (pos + d < n)
                ok = one if ok is None else jnp.logical_and(ok, one)
        return ok

    started = []

    def copy(src, dst, ssem, rsem, i, dev):
        return pltpu.make_async_remote_copy(
            src_ref=src, dst_ref=dst, send_sem=ssem.at[i], recv_sem=rsem.at[i], device_id=dev, device_id_type=MESH
        )

    def send(steps, refs, ssem, rsem, base=0):
        for i, (dx, dy) in enumerate(steps):
            src, dst = refs(dx, dy)
            cp = functools.partial(copy, src, dst, ssem, rsem, base + i, (a + dx, b + dy))
            ok = exists(dx, dy)

            @pl.when(ok)
            def _():
                cp().start()

            started.append((ok, cp))

    def arrive(steps, refs, ssem, rsem, base=0):
        for i, (dx, dy) in enumerate(steps):
            src, dst = refs(dx, dy)

            @pl.when(exists(-dx, -dy))
            def _():
                copy(src, dst, ssem, rsem, base + i, (a - dx, b - dy)).wait_recv()

    ring = [dx for d in ring_order(nx) for dx in (d, d - nx) if abs(dx) <= RING]
    core = lax.rem(b, 2)

    def slot(dx):
        return (4 - dx) % nx

    def whole_rows(dx):
        return pl.ds(2 * abs(dx), 44 - 4 * abs(dx))

    def half_rows(dx):
        return pl.ds(2 * abs(dx) + core * (20 - 2 * abs(dx)), 24 - 2 * abs(dx))

    def send_w(dx):
        return copy(lw.at[:, half_rows(dx)], gw.at[slot(dx), :, half_rows(dx)], s_gw, r_gw, dx % nx - 1, (a + dx, b))

    def send_b(dx):
        return copy(lb.at[whole_rows(dx)], gb.at[slot(dx), whole_rows(dx)], s_gb, r_gb, dx % nx - 1, (a + dx, b))

    def relay(dx):
        d, n = 2 * abs(dx), 20 - 2 * abs(dx)
        src, dst = d + 4 + core * (16 - d), d + core * (24 - d)
        return copy(
            gw.at[slot(dx), :, pl.ds(src, n)], gw.at[slot(dx), :, pl.ds(dst, n)], s_re, r_re, dx % nx, (a, b + 1 - 2 * core)
        )

    def relay_comes(dx):
        d, n = 2 * abs(dx), 20 - 2 * abs(dx)
        dst = pl.ds(24 + core * (d - 24), n)
        return copy(
            gw.at[slot(dx), :, dst], gw.at[slot(dx), :, dst], s_re, r_re, dx % nx, (a, b + 1 - 2 * core)
        )

    def ring_send(made):
        for dx in ring:
            @pl.when(exists(dx, 0))
            def _():
                made(dx).start()

            started.append((exists(dx, 0), functools.partial(made, dx)))

    def ring_arrive(made):
        for dx in ring:
            @pl.when(exists(-dx, 0))
            def _():
                made(dx).wait_recv()

    def fine_refs(arr, lead, pairs, rows):
        def refs(dx, dy):
            x0, xn = span(dx, 3, 4, 2 if dy else pairs)
            y0, yn = span(dy, 8, 16, rows - 1 if dx else rows)
            pre = (slice(None),) * lead
            return (
                arr.at[pre + (pl.ds(x0, xn), slice(None), pl.ds(y0, yn))],
                arr.at[pre + (pl.ds(x0 - 4 * dx, xn), slice(None), pl.ds(y0 - 16 * dy, yn))],
            )

        return refs

    def mid_refs(arr, lead, own, size, far, rows, far_corner):
        def refs(dx, dy):
            x0, xn = span(dx, own, size, size if abs(dx) < 2 else far_corner[0] if dy else far)
            y0, yn = span(dy, 16, 8, rows[0] if dx == 0 else rows[1] if abs(dx) < 2 else far_corner[1])
            pre = (slice(None),) * lead
            return (
                arr.at[pre + (pl.ds(x0, xn), pl.ds(y0, yn))],
                arr.at[pre + (pl.ds(x0 - size * dx, xn), pl.ds(y0 - 8 * dy, yn))],
            )

        return refs

    def low_refs(arr, lead):
        def refs(dx, dy):
            pre = (slice(None),) * lead
            return arr.at[pre + (pl.ds(20, 4),)], arr.at[pre + (pl.ds(20 - 4 * dy, 4),)]

        return refs

    ph_refs = fine_refs(ph, 1, 3, 5)
    rs_refs = fine_refs(rs, 1, 2, 4)
    pb_refs = fine_refs(pb0, 0, 3, 5)
    f1_refs = mid_refs(f1, 1, 8, 4, (3, 2), ((7, 6), (6, 5)), (2, 2))
    b1_refs = mid_refs(b1, 0, 8, 4, 2, (6, 5), (1, 1))
    mb_refs = mid_refs(mb0, 0, 4, 2, 2, (7, 6), (1, 2))
    lw_refs = low_refs(lw, 1)
    lb_refs = low_refs(lb, 0)
    gy_steps = [(0, d) for d in ALONG]

    bar = pltpu.get_barrier_semaphore()
    count = jnp.int32(nx - 1)
    for dx, dy in [(dx, dy) for dx, dy in WIDE if dy] + [(0, d) for d in ALONG if abs(d) > 1]:
        ok = exists(dx, dy)

        @pl.when(ok)
        def _():
            pl.semaphore_signal(bar, inc=1, device_id=(a + dx, b + dy), device_id_type=MESH)

        count = count + ok.astype(jnp.int32)

    for d in ring_order(nx):
        pl.semaphore_signal(bar, inc=1, device_id=(lax.rem(a + d, nx), b), device_id_type=MESH)
    in_rs = pltpu.make_async_copy(rs_hbm, rs_in, in_sem.at[0])
    in_ph = pltpu.make_async_copy(ph_hbm, ph_in, in_sem.at[1])
    in_ph.start()
    in_rs.start()

    def iota(rows, dim):
        return lax.broadcasted_iota(jnp.int32, (rows, LANES), dim)

    def h1_of(rows):
        return iota(rows, 1) >= 64

    def lane_ok(rows):
        return lax.rem(iota(rows, 1), 64) < 48

    def odd_fine(rows, start, t):
        return lax.rem(iota(rows, 0) + (start + t), 2) == 1

    def odd_mid(rows, start):
        return lax.rem(iota(rows, 0) + start + lax.div(iota(rows, 1), 64), 2) == 1

    def odd_low(rows, start):
        return lax.rem(iota(rows, 0) + start + iota(rows, 1), 2) == 1

    def inverse(v):
        r = pl.reciprocal(v, approx=True)
        r = r * (2.0 - v * r)
        return r * (2.0 - v * r)

    def zero(ref):
        ref[...] = jnp.zeros(ref.shape, F32)

    @pl.when(a == 0)
    def _():
        zero(ph.at[:, 0:3]); zero(rs.at[:, 0:3]); zero(pb0.at[0:3]); zero(f1.at[:, 0:8]); zero(b1.at[0:8]); zero(mb0.at[0:4])

    @pl.when(a == 1)
    def _():
        zero(f1.at[:, 0:4]); zero(b1.at[0:4]); zero(mb0.at[0:2])

    @pl.when(a == nx - 1)
    def _():
        zero(ph.at[:, 7:10]); zero(rs.at[:, 7:10]); zero(pb0.at[7:10])
        zero(f1.at[:, 12:21]); zero(b1.at[12:20]); zero(mb0.at[6:10])

    @pl.when(a == nx - 2)
    def _():
        zero(f1.at[:, 16:21]); zero(b1.at[16:20]); zero(mb0.at[8:10])

    @pl.when(b == 0)
    def _():
        zero(ph.at[:, :, :, 0:8]); zero(rs.at[:, :, :, 0:8]); zero(pb0.at[:, :, 0:8])
        zero(f1.at[:, :, 0:16]); zero(b1.at[:, 0:16]); zero(mb0.at[:, 0:16])

    @pl.when(b == ny - 1)
    def _():
        zero(ph.at[:, :, :, 24:32]); zero(rs.at[:, :, :, 24:32]); zero(pb0.at[:, :, 24:32])
        zero(f1.at[:, :, 24:40]); zero(b1.at[:, 24:40]); zero(mb0.at[:, 24:40])

    for d in ALONG:
        @pl.when(jnp.logical_not(exists(0, d)))
        def _():
            zero(lw.at[:, pl.ds(20 + 4 * d, 4)])
            zero(lb.at[pl.ds(20 + 4 * d, 4)])

    for dx in list(range(1, nx)) + list(range(-1, -nx, -1)):
        @pl.when(exists(-dx, 0))
        def _():
            if abs(dx) > RING:
                zero(gw.at[slot(dx)])
                zero(gb.at[slot(dx)])
            else:
                for rows in (slice(0, 2 * abs(dx)), slice(44 - 2 * abs(dx), 48)):
                    zero(gw.at[slot(dx), :, rows])
                    zero(gb.at[slot(dx), rows])

    nz = rs_in.shape[2]
    kk = lax.broadcasted_iota(jnp.int32, (nz, 2 * LANES), 0)
    cc = lax.broadcasted_iota(jnp.int32, (nz, 2 * LANES), 1)
    q, hh, tt = lax.rem(cc, 64), lax.rem(lax.div(cc, 64), 2), lax.div(cc, 128)
    perm = jnp.where(jnp.logical_and(kk == 4 * q + 2 * hh + tt, q < 48), 1.0, 0.0).astype(F32)

    def reorder(v, matrix):
        m16 = matrix.astype(jnp.bfloat16)
        total = None
        for _ in range(3):
            part = v.astype(jnp.bfloat16)
            v = v - part.astype(F32)
            dot = jnp.dot(part, m16, preferred_element_type=F32)
            total = dot if total is None else total + dot
        return total

    def split_into(values, dst):
        for t in (0, 1):
            odd = odd_fine(16, 0, t)
            for m in range(4):
                lo = values[32 * m:32 * m + 16, t * LANES:(t + 1) * LANES]
                hi = values[32 * m + 16:32 * m + 32, t * LANES:(t + 1) * LANES]
                dst[0, 3 + m, t, 8:24, :] = jnp.where(odd, hi, lo)
                dst[1, 3 + m, t, 8:24, :] = jnp.where(odd, lo, hi)

    in_ph.wait()
    labels = jnp.where(ph_in[...] == 1, 1.0, 0.0).astype(F32).reshape(128, nz)
    split_into(jnp.dot(labels, perm, preferred_element_type=F32), ph)
    in_rs.wait()
    block = rs_in[...].reshape(128, nz)
    split_into(reorder(block, perm), rs)

    pl.semaphore_wait(bar, count)
    send(NEAR, ph_refs, s_ph, r_ph)
    send(NEAR, rs_refs, s_rs, r_rs)

    def pair_ok(first, m, total):
        g = first + m
        return jnp.logical_and(g >= 0, g < total)

    def inside(rows, start, total, ok):
        g = iota(rows, 0) + (start + jnp.where(ok, 0, -4096))
        return jnp.logical_and(jnp.logical_and(g >= 0, g < total), lane_ok(rows))

    def fine_sides(arr, c, m, t, r0, n, odd, h1):
        o = 1 - c
        xs = arr[o, m, t, pl.ds(r0, n), :]
        lo = arr[o, m - 1, t, pl.ds(r0, n), :]
        hi = arr[o, m + 1, t, pl.ds(r0, n), :]
        xo = jnp.where(odd, hi, lo) if c == 0 else jnp.where(odd, lo, hi)
        ym = arr[o, m, t, pl.ds(r0 - 1, n), :]
        yp = arr[o, m, t, pl.ds(r0 + 1, n), :]
        zs = arr[o, m, 1 - t, pl.ds(r0, n), :]
        if t == 0:
            zo = jnp.where(h1, rot(zs, 64), rot(zs, 65))
        else:
            zo = jnp.where(h1, rot(zs, 63), rot(zs, 64))
        return xs, xo, ym, yp, zs, zo

    R0, RN = 4, 24
    odd24 = [odd_fine(RN, R0, 0), odd_fine(RN, R0, 1)]
    h24 = h1_of(RN)

    arrive(NEAR, ph_refs, s_ph, r_ph)

    def levels(c, m, t):
        dense = ph[c, m, t, pl.ds(R0, RN), :] > 0.5
        return jnp.where(dense, W_DD, W_MX), jnp.where(dense, W_MX, W_LL)

    def own_faces(m, carry):
        fx = fy = fz = None
        for t in (0, 1):
            both = []
            for c in (0, 1):
                on, off = levels(c, m, t)
                side = fine_sides(ph, c, m, t, R0, RN, odd24[t], h24)
                both.append([jnp.where(side[f] > 0.5, on, off) for f in (1, 2, 5)])
            x = jnp.where(odd24[t], both[1][0], both[0][0])
            y = both[0][1] + both[1][1]
            fx = x if fx is None else fx + x
            fy = y if fy is None else fy + y
            if t == 0:
                fz = both[0][2] + both[1][2]
        tf[0, m, 0:RN, :] = fx
        tf[1, m, 0:RN, :] = fy
        tf[2, m, 0:RN, :] = fz
        return carry

    lax.fori_loop(3, 8, own_faces, 0, unroll=True)

    even, oddr = pl.ds(0, 16, stride=2), pl.ds(1, 16, stride=2)

    def mid_faces(i, carry):
        f1o[0, i, 0:16, :] = 0.25 * (tf[0, i + 3, even, :] + tf[0, i + 3, oddr, :])
        f1o[1, i, 0:16, :] = 0.25 * tf[1, i + 3, even, :]
        f1o[2, i, 0:16, :] = 0.25 * (tf[2, i + 3, even, :] + tf[2, i + 3, oddr, :])
        return carry

    lax.fori_loop(0, 5, mid_faces, 0, unroll=True)
    h8 = h1_of(8)
    for i in range(4):
        fx, fxn = f1o[0, i, 2:10, :], f1o[0, i + 1, 2:10, :]
        fy, fyn = f1o[1, i, 2:10, :], f1o[1, i, 3:11, :]
        fz = f1o[2, i, 2:10, :]
        fzn = jnp.where(h8, rot(fz, 63), rot(fz, 64))
        dg = ((((fx + fxn) + fy) + fyn) + fz) + fzn
        for f, w in enumerate((fx, fy, fz)):
            f1[f, 8 + i, 16:24, :] = jnp.where(lane_ok(8), w, rot(dg, 48 - 16 * f))
    send(NEAR, f1_refs, s_f1, r_f1)

    def zsum(v):
        return v + rot(v, 64)

    fx2 = [0.25 * zsum(f1o[0, 2 * i, pl.ds(2, 8, stride=2), :] + f1o[0, 2 * i, pl.ds(3, 8, stride=2), :]) for i in range(3)]
    fy2, fy2n, fz2, fz2n = [], [], [], []
    for i in range(2):
        fy2.append(0.25 * zsum(f1o[1, 2 * i, pl.ds(2, 8, stride=2), :] + f1o[1, 2 * i + 1, pl.ds(2, 8, stride=2), :]))
        fy2n.append(0.25 * zsum(f1o[1, 2 * i, pl.ds(4, 8, stride=2), :] + f1o[1, 2 * i + 1, pl.ds(4, 8, stride=2), :]))
        v = (f1o[2, 2 * i, pl.ds(2, 8, stride=2), :] + f1o[2, 2 * i, pl.ds(3, 8, stride=2), :]) + (
            f1o[2, 2 * i + 1, pl.ds(2, 8, stride=2), :] + f1o[2, 2 * i + 1, pl.ds(3, 8, stride=2), :]
        )
        v = 0.25 * jnp.where(h8, rot(v, 64), v)
        fz2.append(v)
        fz2n.append(rot(v, 127))
    odd8 = odd_low(8, 0)
    dg2 = [((((fx2[i] + fx2[i + 1]) + fy2[i]) + fy2n[i]) + fz2[i]) + fz2n[i] for i in range(2)]
    rd2 = [jnp.where(lane_ok(8), 1.0 / d, 0.0) for d in dg2]

    def red(v):
        return jnp.where(odd8, v[1], v[0])

    def black(v):
        return jnp.where(odd8, v[0], v[1])

    edge_low = jnp.where(a == 0, 0.0, 1.0)
    edge_high = jnp.where(a == nx - 1, 0.0, 1.0)
    xo2 = jnp.where(odd8, fx2[2] * edge_high, fx2[0] * edge_low)
    inv = jnp.where(h8, black(rd2), red(rd2))
    for f, (first, second) in enumerate(((fx2[1], xo2), (red(fy2), red(fy2n)), (red(fz2), red(fz2n)))):
        v = jnp.where(lane_ok(8), jnp.where(h8, second, first), rot(inv, 48 - 16 * f))
        lw[f, 20:24, :] = v[0:4]
    send(gy_steps, lw_refs, s_lw, r_lw)

    def fine_weights(m, carry):
        valid = inside(RN, 16 * b - 8 + R0, 16 * ny, pair_ok(4 * a - 3, m, 4 * nx))
        for t in (0, 1):
            for c in (0, 1):
                on, off = levels(c, m, t)
                side = fine_sides(ph, c, m, t, R0, RN, odd24[t], h24)
                many = ((((side[0] + side[1]) + side[2]) + side[3]) + side[4]) + side[5]
                dg = 6.0 * off + many * (on - off)
                rd = jnp.where(valid, inverse(dg), 0.0)
                won, woff = on * rd, off * rd
                for f in range(6):
                    wf[6 * c + f, m, t, pl.ds(R0, RN), :] = jnp.where(side[f] > 0.5, won, woff)
                df[c, m, t, pl.ds(R0, RN), :] = dg
                rdf[c, m, t, pl.ds(R0, RN), :] = rd
        return carry

    lax.fori_loop(1, 9, fine_weights, 0, unroll=True)

    def fine_nb(c, m, t, r0, n, odd, h1):
        v = fine_sides(pf, c, m, t, r0, n, odd, h1)
        total = wf[6 * c, m, t, pl.ds(r0, n), :] * v[0]
        for f in range(1, 6):
            total = total + wf[6 * c + f, m, t, pl.ds(r0, n), :] * v[f]
        return total

    def fine_half(c, m0, m1, r0, n):
        odd = [odd_fine(n, r0, 0), odd_fine(n, r0, 1)]
        h1 = h1_of(n)

        def body(m, carry):
            for t in (0, 1):
                nb = fine_nb(c, m, t, r0, n, odd[t], h1)
                pf[c, m, t, pl.ds(r0, n), :] = sf[c, m, t, pl.ds(r0, n), :] + nb
            return carry

        lax.fori_loop(m0, m1, body, 0, unroll=True)

    def fine_last(r0, n):
        odd = [odd_fine(n, r0, 0), odd_fine(n, r0, 1)]
        h1 = h1_of(n)

        def body(m, carry):
            for t in (0, 1):
                win = pl.ds(r0, n)
                nb = fine_nb(1, m, t, r0, n, odd[t], h1)
                fresh = sf[1, m, t, win, :] + nb
                pf[1, m, t, win, :] = fresh
                rf[1, m, t, win, :] = rs[1, m, t, win, :] - df[1, m, t, win, :] * (fresh - nb)
            return carry

        lax.fori_loop(2, 8, body, 0, unroll=True)

    def fine_red_residual():
        odd = [odd_fine(16, 8, 0), odd_fine(16, 8, 1)]
        h1 = h1_of(16)

        def body(m, carry):
            for t in (0, 1):
                win = pl.ds(8, 16)
                nb = fine_nb(0, m, t, 8, 16, odd[t], h1)
                rf[0, m, t, win, :] = rs[0, m, t, win, :] - df[0, m, t, win, :] * (pf[0, m, t, win, :] - nb)
            return carry

        lax.fori_loop(3, 7, body, 0, unroll=True)

    arrive(NEAR, rs_refs, s_rs, r_rs)

    def fine_source(m, carry):
        win = pl.ds(R0, RN)
        for t in (0, 1):
            first = rs[0, m, t, win, :] * rdf[0, m, t, win, :]
            sf[0, m, t, win, :] = first
            pf[0, m, t, win, :] = first
            sf[1, m, t, win, :] = rs[1, m, t, win, :] * rdf[1, m, t, win, :]
        return carry

    lax.fori_loop(1, 9, fine_source, 0, unroll=True)
    fine_half(1, 1, 9, 4, 24)
    fine_half(0, 2, 8, 6, 24)
    fine_last(7, 24)
    fine_red_residual()

    def restrict_fine(m, carry):
        v = (rf[0, m, 0, 8:24, :] + rf[1, m, 0, 8:24, :]) + (rf[0, m, 1, 8:24, :] + rf[1, m, 1, 8:24, :])
        rm[m, 0:16, :] = v
        b1[m + 5, 16:24, :] = 0.125 * (rm[m, pl.ds(0, 8, stride=2), :] + rm[m, pl.ds(1, 8, stride=2), :])
        return carry

    lax.fori_loop(3, 7, restrict_fine, 0, unroll=True)
    send(WIDE, b1_refs, s_b1, r_b1)

    def keep_black(m, carry):
        for t in (0, 1):
            pb0[m, t, 8:24, :] = pf[1, m, t, 8:24, :]
        return carry

    lax.fori_loop(3, 7, keep_black, 0, unroll=True)
    send(NEAR, pb_refs, s_pb, r_pb)
    send(FAR, f1_refs, s_f1, r_f1, len(NEAR))

    def mid_weights(m0, m1, r0, n, top):
        odd, h1 = odd_mid(n, r0), h1_of(n)
        win, nxt = pl.ds(r0, n), pl.ds(r0 + 1, n)
        q = lax.rem(iota(n, 1), 64)
        q16, q32 = q < 16, q < 32

        def body(m, carry):
            valid = inside(n, 8 * b - 16 + r0, 8 * ny, pair_ok(2 * a - 4, m, 2 * nx))
            e0, e1_ = 2 * m, 2 * m + 1
            fx0, fx1, fx2_ = f1[0, e0, win, :], f1[0, e1_, win, :], f1[0, jnp.minimum(e1_ + 1, top), win, :]
            ym = [f1[1, e, win, :] for e in (e0, e1_)]
            yp = [f1[1, e, nxt, :] for e in (e0, e1_)]
            fz = [f1[2, e, win, :] for e in (e0, e1_)]
            zs = [jnp.where(h1, v, rot(v, 64)) for v in fz]
            zo = [jnp.where(h1, rot(v, 63), v) for v in fz]
            dg = [
                jnp.where(q16, rot(f1[0, e, win, :], 80), jnp.where(q32, rot(f1[1, e, win, :], 96), rot(f1[2, e, win, :], 112)))
                for e in (e0, e1_)
            ]
            for c in (0, 1):
                def pick(v):
                    return jnp.where(odd, v[1 - c], v[c])

                xo = jnp.where(odd, fx2_, fx0) if c == 0 else jnp.where(odd, fx0, fx2_)
                d = pick(dg)
                rd = jnp.where(valid, 1.0 / d, 0.0)
                for f, w in enumerate((fx1, xo, pick(ym), pick(yp), pick(zs), pick(zo))):
                    wm[6 * c + f, m, win, :] = w * rd
                dm[c, m, win, :] = d
                rdm[c, m, win, :] = rd
            return carry

        lax.fori_loop(m0, m1, body, 0, unroll=True)

    def mid_source(m0, m1, r0, n, start):
        odd = odd_mid(n, r0)
        win = pl.ds(r0, n)

        def body(m, carry):
            lo, hi = b1[2 * m, win, :], b1[2 * m + 1, win, :]
            first = 4.0 * jnp.where(odd, hi, lo) * rdm[0, m, win, :]
            sm[0, m, win, :] = first
            if start:
                pm[0, m, win, :] = first
            sm[1, m, win, :] = 4.0 * jnp.where(odd, lo, hi) * rdm[1, m, win, :]
            return carry

        lax.fori_loop(m0, m1, body, 0, unroll=True)

    def mid_nb(c, m, r0, n, odd, h1):
        o = 1 - c
        win = pl.ds(r0, n)
        xs, lo, hi = pm[o, m, win, :], pm[o, m - 1, win, :], pm[o, m + 1, win, :]
        xo = jnp.where(odd, hi, lo) if c == 0 else jnp.where(odd, lo, hi)
        zo = jnp.where(h1, rot(xs, 63), rot(xs, 65))
        total = wm[6 * c, m, win, :] * xs
        total = total + wm[6 * c + 1, m, win, :] * xo
        total = total + wm[6 * c + 2, m, win, :] * pm[o, m, pl.ds(r0 - 1, n), :]
        total = total + wm[6 * c + 3, m, win, :] * pm[o, m, pl.ds(r0 + 1, n), :]
        total = total + wm[6 * c + 4, m, win, :] * rot(xs, 64)
        return total + wm[6 * c + 5, m, win, :] * zo

    def mid_half(c, m0, m1, r0, n):
        odd, h1 = odd_mid(n, r0), h1_of(n)

        def body(m, carry):
            win = pl.ds(r0, n)
            pm[c, m, win, :] = sm[c, m, win, :] + mid_nb(c, m, r0, n, odd, h1)
            return carry

        lax.fori_loop(m0, m1, body, 0, unroll=True)

    arrive(gy_steps, lw_refs, s_lw, r_lw)
    ring_send(send_w)
    arrive(NEAR, f1_refs, s_f1, r_f1)
    mid_weights(2, 8, 12, 16, 15)
    arrive(NEAR, b1_refs, s_b1, r_b1)
    mid_source(2, 8, 12, 16, True)
    mid_half(1, 2, 8, 13, 16)
    mid_half(0, 3, 7, 14, 16)
    mid_half(1, 3, 7, 15, 16)

    odd_own, h_own = odd_mid(8, 16), h1_of(8)
    own = pl.ds(16, 8)
    planes = []
    for m in (4, 5):
        lo, hi = b1[2 * m, own, :], b1[2 * m + 1, own, :]
        total = None
        for c in (0, 1):
            src = jnp.where(odd_own, hi, lo) if c == 0 else jnp.where(odd_own, lo, hi)
            nb = mid_nb(c, m, 16, 8, odd_own, h_own)
            res = src - dm[c, m, own, :] * (pm[c, m, own, :] - nb) * 0.25
            total = res if total is None else total + res
        rm[m, 0:8, :] = total
        rm[m, 8:16, :] = total
        planes.append(0.125 * zsum(rm[m, pl.ds(0, 8, stride=2), :] + rm[m, pl.ds(1, 8, stride=2), :]))
    lb[20:24, :] = jnp.where(h8, black(planes), red(planes))[0:4]
    send(gy_steps, lb_refs, s_lb, r_lb)
    for m in (4, 5):
        mb0[m, own, :] = pm[1, m, own, :]
    send(WIDE, mb_refs, s_mb, r_mb)

    arrive(FAR, f1_refs, s_f1, r_f1, len(NEAR))
    mid_weights(1, 9, 8, 24, 18)
    arrive(FAR, b1_refs, s_b1, r_b1, len(NEAR))
    mid_source(1, 9, 8, 24, False)

    arrive(gy_steps, lb_refs, s_lb, r_lb)
    ring_send(send_b)
    gw[4, :, 0:44] = lw[:, 0:44]
    gb[4, 0:44] = lb[0:44]

    LR = 48
    h48 = h1_of(LR)
    odd48 = odd_low(LR, 0)
    q48 = lax.rem(iota(LR, 1), 64)
    lwin = pl.ds(8, LR)

    def fold(lo, hi, half):
        if half == 0:
            return jnp.where(h48, rot(hi, 64), lo)
        return jnp.where(h48, hi, rot(lo, 64))

    ring_arrive(send_w)
    passed = [dx for dx in ring if abs(dx) < RING]
    for dx in passed:
        @pl.when(exists(-dx, 0))
        def _():
            relay(dx).start()

        started.append((exists(-dx, 0), functools.partial(relay, dx)))
    for dx in passed:
        @pl.when(exists(-dx, 0))
        def _():
            relay_comes(dx).wait_recv()

    def low_weights(s, carry):
        u = [fold(gw[s, f // 2], gw[s + 8, f // 2], f % 2) for f in range(6)]
        for c in (0, 1):
            third = jnp.where(q48 < 16, rot(u[c], 80), jnp.where(q48 < 32, rot(u[2 + c], 96), rot(u[4 + c], 112)))
            rdl[c, s, lwin, :] = jnp.where(q48 < 48, third, 0.0)
        rd = rdl[0, s, lwin, :]
        for f in range(6):
            ul[f, s + 1, lwin, :] = u[f]
            wl[f, s, lwin, :] = u[f] * rd
        return carry

    lax.fori_loop(0, 8, low_weights, 0, unroll=True)
    ul[1, 0, lwin, :] = rot(ul[1, 8, lwin, :], 64)
    ul[1, 9, lwin, :] = rot(ul[1, 1, lwin, :], 64)

    def low_black(s, carry):
        rd = rdl[1, s, lwin, :]
        wl[6, s, lwin, :] = ul[0, s + 1, lwin, :] * rd
        wl[7, s, lwin, :] = jnp.where(odd48, ul[1, s, lwin, :], ul[1, s + 2, lwin, :]) * rd
        wl[8, s, lwin, :] = ul[3, s + 1, pl.ds(7, LR), :] * rd
        wl[9, s, lwin, :] = ul[2, s + 1, pl.ds(9, LR), :] * rd
        wl[10, s, lwin, :] = rot(ul[5, s + 1, lwin, :], 1) * rd
        wl[11, s, lwin, :] = rot(ul[4, s + 1, lwin, :], 127) * rd
        return carry

    lax.fori_loop(0, 8, low_black, 0, unroll=True)

    ring_arrive(send_b)

    def low_source(s, carry):
        lo, hi = gb[s], gb[s + 8]
        first = 16.0 * fold(lo, hi, 0) * rdl[0, s, lwin, :]
        sl[0, s, lwin, :] = first
        plow[0, s + 1, lwin, :] = first
        sl[1, s, lwin, :] = 16.0 * fold(lo, hi, 1) * rdl[1, s, lwin, :]
        return carry

    lax.fori_loop(0, 8, low_source, 0, unroll=True)

    def low_ghosts(c, r0, n):
        win = pl.ds(r0, n)
        plow[c, 0, win, :] = rot(plow[c, 8, win, :], 64)
        plow[c, 9, win, :] = rot(plow[c, 1, win, :], 64)

    low_ghosts(0, 8, LR)
    def low_half(c, first, step, times, reach):
        r0, n = 8 + 20 - reach, 8 * ((4 + 2 * reach + 7) // 8)
        odd = odd_low(n, r0)

        def low_body(i, carry):
            s = first + step * i
            o = 1 - c
            win = pl.ds(r0, n)
            xs, lo, hi = plow[o, s + 1, win, :], plow[o, s, win, :], plow[o, s + 2, win, :]
            xo = jnp.where(odd, hi, lo) if c == 0 else jnp.where(odd, lo, hi)
            total = sl[c, s, win, :] + wl[6 * c, s, win, :] * xs
            total = total + wl[6 * c + 1, s, win, :] * xo
            total = total + wl[6 * c + 2, s, win, :] * plow[o, s + 1, pl.ds(r0 - 1, n), :]
            total = total + wl[6 * c + 3, s, win, :] * plow[o, s + 1, pl.ds(r0 + 1, n), :]
            total = total + wl[6 * c + 4, s, win, :] * rot(xs, 1)
            plow[c, s + 1, win, :] = total + wl[6 * c + 5, s, win, :] * rot(xs, 127)
            return carry

        lax.fori_loop(0, times, low_body, 0, unroll=True)
        return r0, n

    for half in range(2, 2 * BOTTOM + 1):
        c = (half - 1) % 2
        reach = 4 + 2 * BOTTOM - half
        low_half(c, 4, 1, 1, reach)
        for far in (1, 2, 3):
            if reach >= 2 * far - 1:
                win = low_half(c, 4 - far, 2 * far, 2, reach - 2 * far + 1)
        if reach >= 7:
            low_half(c, 0, 1, 1, reach - 7)
            low_ghosts(c, *win)

    arrive(WIDE, mb_refs, s_mb, r_mb)
    odd16, h16 = odd_low(16, 0), h1_of(16)
    rows24 = pl.ds(8, 24)

    def mid_correct(s, carry):
        red_, black_ = plow[0, s + 3, pl.ds(24, 16), :], plow[1, s + 3, pl.ds(24, 16), :]
        for e in (0, 1):
            v = jnp.where(odd16, black_, red_) if e == 0 else jnp.where(odd16, red_, black_)
            v = jnp.where(h16, rot(v, 64), v)
            em[2 * s + e, pl.ds(0, 16, stride=2), :] = v
            em[2 * s + e, pl.ds(1, 16, stride=2), :] = v
            m = 2 * s + e
            add = em[m, 0:24, :] * jnp.where(pair_ok(2 * a - 4, m, 2 * nx), 1.0, 0.0)
            pm[1, m, rows24, :] = mb0[m, rows24, :] + add
        return carry

    lax.fori_loop(0, 5, mid_correct, 0, unroll=True)
    mid_half(0, 1, 9, 10, 24)
    mid_half(1, 1, 9, 11, 24)
    mid_half(0, 2, 8, 12, 16)
    mid_half(1, 2, 8, 13, 16)

    arrive(NEAR, pb_refs, s_pb, r_pb)
    odd_c = odd_mid(16, 13)

    for m in range(10):
        n, e = (m + 5) // 2, (m + 5) % 2
        red_, black_ = pm[0, n, pl.ds(13, 16), :], pm[1, n, pl.ds(13, 16), :]
        v = jnp.where(odd_c, black_, red_) if e == 0 else jnp.where(odd_c, red_, black_)
        e1[m, pl.ds(2, 16, stride=2), :] = v
        e1[m, pl.ds(3, 16, stride=2), :] = v
        for t in (0, 1):
            pf[1, m, t, pl.ds(3, 32), :] = pb0[m, t, pl.ds(3, 32), :] + e1[m, pl.ds(3, 32), :]

    fine_half(0, 1, 9, 4, 24)
    fine_half(1, 1, 9, 5, 24)
    fine_half(0, 2, 8, 6, 24)
    fine_last(7, 24)
    fine_red_residual()

    kk2 = lax.broadcasted_iota(jnp.int32, (2 * LANES, nz), 1)
    cc2 = lax.broadcasted_iota(jnp.int32, (2 * LANES, nz), 0)
    q2, hh2, tt2 = lax.rem(cc2, 64), lax.rem(lax.div(cc2, 64), 2), lax.div(cc2, 128)
    back = jnp.where(jnp.logical_and(kk2 == 4 * q2 + 2 * hh2 + tt2, q2 < 48), 1.0, 0.0).astype(F32)

    def join_from(src, out):
        for t in (0, 1):
            odd = odd_fine(16, 8, t)
            for m in range(4):
                r, k = src[0, 3 + m, t, 8:24, :], src[1, 3 + m, t, 8:24, :]
                xo_s[32 * m:32 * m + 16, t * LANES:(t + 1) * LANES] = jnp.where(odd, k, r)
                xo_s[32 * m + 16:32 * m + 32, t * LANES:(t + 1) * LANES] = jnp.where(odd, r, k)
        out[...] = reorder(xo_s[...], back).reshape(out.shape)

    join_from(pf, out_p)
    join_from(rf, out_r)
    for ok, cp in started:
        if ok is None:
            cp().wait_send()
        else:
            @pl.when(ok)
            def _():
                cp().wait_send()


def solution(mesh):
    nx, ny = mesh.shape["gx"], mesh.shape["gy"]

    def local(right_side, phase):
        shape = right_side.shape
        v = lambda *dims: pltpu.VMEM(dims, F32)
        sems = []
        for n in (len(NEAR), len(NEAR), len(WIDE), len(WIDE), len(NEAR), len(WIDE), len(ALONG), len(ALONG), nx - 1, nx - 1, nx):
            sems += [pltpu.SemaphoreType.DMA((n,)), pltpu.SemaphoreType.DMA((n,))]
        fine = (10, 2, 40, LANES)
        return pl.pallas_call(
            functools.partial(kernel, nx, ny),
            out_shape=[jax.ShapeDtypeStruct(shape, F32)] * 2,
            in_specs=[pl.BlockSpec(memory_space=pltpu.HBM)] * 2,
            out_specs=[pl.BlockSpec(memory_space=pltpu.VMEM)] * 2,
            scratch_shapes=[
                v(*shape), pltpu.VMEM(shape, jnp.int32),
                v(2, *fine), v(2, *fine), v(12, *fine), v(2, *fine), v(2, *fine), v(2, *fine), v(2, *fine), v(*fine),
                v(2, *fine), v(3, 10, 32, LANES), v(3, 5, 24, LANES),
                v(3, 21, 40, LANES), v(20, 40, LANES), v(12, 10, 40, LANES), v(2, 10, 40, LANES), v(2, 10, 40, LANES),
                v(2, 10, 40, LANES), v(2, 10, 40, LANES), v(10, 40, LANES), v(10, 16, LANES), v(10, 32, LANES),
                v(3, 48, LANES), v(48, LANES), v(16, 3, 48, LANES), v(16, 48, LANES), v(6, 10, 64, LANES),
                v(12, 8, 64, LANES), v(2, 8, 64, LANES), v(2, 8, 64, LANES), v(2, 10, 64, LANES), v(10, 40, LANES),
                v(128, 2 * LANES),
                pltpu.SemaphoreType.DMA((2,)),
            ] + sems,
            compiler_params=pltpu.CompilerParams(
                collective_id=0, has_side_effects=True, vmem_limit_bytes=56262656
            ),
        )(right_side, phase)

    spec = P("gx", "gy", None)
    return jax.shard_map(local, mesh=mesh, in_specs=(spec, spec), out_specs=(spec, spec), check_vma=False)
```
